32 devices in a mesh: dp: 8 (over z, x), seq: 4 (over y, core).
Axes of the slice: x: 2, y: 2, z: 4, core: 2. Of those that a mesh axis runs over, the one named last changes fastest.
Arguments:
- tokens: bfloat16 [32, 1024, 768], P('dp', 'seq'), may hold values from -6 to 6
- cotangent: bfloat16 [32, 1024, 768], P('dp', 'seq'), may hold values from -6 to 6
- lengths: int32 [32], P('dp'), may hold values from 1 to 1024, as said below
- qkv_weight: float32 [768, 2304], P('dp'), may hold values from -0.21875 to 0.21875
- qkv_first: float32 [768, 2304], P('dp'), may hold values from -0.00390625 to 0.00390625
- qkv_second: float32 [768, 2304], P('dp'), may hold values from 5.4253474e-07 to 2.170139e-06
- qkv_average: float32 [768, 2304], P('dp'), may hold values from -0.21875 to 0.21875
- proj_weight: float32 [768, 768], P('dp'), may hold values from -1.75 to 1.75
- proj_first: float32 [768, 768], P('dp'), may hold values from -0.00048828125 to 0.00048828125
- proj_second: float32 [768, 768], P('dp'), may hold values from 6.781684e-09 to 2.7126736e-08
- proj_average: float32 [768, 768], P('dp'), may hold values from -1.75 to 1.75
- inner_weight: float32 [768, 3072], P('dp'), may hold values from -0.21875 to 0.21875
- inner_first: float32 [768, 3072], P('dp'), may hold values from -0.0004272461 to 0.0004272461
- inner_second: float32 [768, 3072], P('dp'), may hold values from 5.086263e-09 to 2.0345052e-08
- inner_average: float32 [768, 3072], P('dp'), may hold values from -0.21875 to 0.21875
- outer_weight: float32 [3072, 768], P('dp'), may hold values from -0.109375 to 0.109375
- outer_first: float32 [3072, 768], P('dp'), may hold values from -0.0007324219 to 0.0007324219
- outer_second: float32 [3072, 768], P('dp'), may hold values from 1.2715658e-08 to 5.086263e-08
- outer_average: float32 [3072, 768], P('dp'), may hold values from -0.109375 to 0.109375
- gains: float32 [2, 768], P(None, 'dp'), may hold values from 0.3 to 2.4
- gain_first: float32 [2, 768], P(None, 'dp'), may hold values from -0.009765625 to 0.009765625
- gain_second: float32 [2, 768], P(None, 'dp'), may hold values from 2.2605614e-06 to 9.042245e-06
- gain_average: float32 [2, 768], P(None, 'dp'), may hold values from 0.1 to 1.9
- mixes: float32 [2, 12, 12], replicated, may hold values from -0.9 to 1.3
- mix_first: float32 [2, 12, 12], replicated, may hold values from -0.01953125 to 0.01953125
- mix_second: float32 [2, 12, 12], replicated, may hold values from 9.042245e-06 to 3.616898e-05
- mix_average: float32 [2, 12, 12], replicated, may hold values from -0.4 to 1.2
Outputs:
- output: bfloat16 [32, 1024, 768], P('dp', 'seq')
- grad_tokens: float32 [32, 1024, 768], P('dp', 'seq')
- grad_norm: float32 [], replicated
- next_qkv_first: float32 [768, 2304], P('dp')
- next_qkv_second: float32 [768, 2304], P('dp')
- next_qkv_weight: float32 [768, 2304], P('dp')
- next_qkv_average: float32 [768, 2304], P('dp')
- next_proj_first: float32 [768, 768], P('dp')
- next_proj_second: float32 [768, 768], P('dp')
- next_proj_weight: float32 [768, 768], P('dp')
- next_proj_average: float32 [768, 768], P('dp')
- next_inner_first: float32 [768, 3072], P('dp')
- next_inner_second: float32 [768, 3072], P('dp')
- next_inner_weight: float32 [768, 3072], P('dp')
- next_inner_average: float32 [768, 3072], P('dp')
- next_outer_first: float32 [3072, 768], P('dp')
- next_outer_second: float32 [3072, 768], P('dp')
- next_outer_weight: float32 [3072, 768], P('dp')
- next_outer_average: float32 [3072, 768], P('dp')
- next_gain_first: float32 [2, 768], P(None, 'dp')
- next_gain_second: float32 [2, 768], P(None, 'dp')
- next_gains: float32 [2, 768], P(None, 'dp')
- next_gain_average: float32 [2, 768], P(None, 'dp')
- next_mix_first: float32 [2, 12, 12], replicated
- next_mix_second: float32 [2, 12, 12], replicated
- next_mixes: float32 [2, 12, 12], replicated
- next_mix_average: float32 [2, 12, 12], replicated
- clipped_gain_grad: float32 [2, 768], P(None, 'dp')
The draws below stay inside these ranges and needn't reach their ends.
Inputs may be any that keep to these rules, and one draw needn't show every extreme that they name: `lengths`: in each aligned block of 4 sequences (one index of dp) at least one sequence has length 1024.
All inputs are finite; a program needn't handle non-finite values.
Results may differ from the reference program's by a relative error of at most 0.014.
The reference program's roundings to bfloat16 on the way count: a program that leaves them out, or rounds other values in their place, can miss the bound.
Values may be sent and summed in bfloat16 or wider, within the bound.
No kernel may reach another device: no remote copies, remote signals or barrier semaphores. Data moves between devices by JAX's collectives and lax.ppermute only.
A program may use at most 384 MiB of HBM per device.

```python
import math
import jax
import jax.numpy as jnp
from jax import lax

D = 768
HEADS = 12
HEAD_DIM = 64
FF = 3072
LEN = 1024
STEP = 10
GROUP_SEQS = 4
BATCH = 32


def draw_lengths(key, part):
    key = jax.random.fold_in(key, 11)
    key_level, key_cut, key_pick = jax.random.split(key, 3)
    level = jax.random.randint(key_level, (BATCH,), 0, 4)
    base = jnp.right_shift(jnp.full((BATCH,), LEN, jnp.int32), level.astype(jnp.int32))
    cut = jax.random.randint(key_cut, (BATCH,), 0, 1 << 20)
    ragged = base - jnp.remainder(cut, base // 2)
    pick = jax.random.randint(key_pick, (BATCH // GROUP_SEQS,), 0, GROUP_SEQS)
    chosen = (jnp.arange(GROUP_SEQS)[None, :] == pick[:, None]).reshape(BATCH)
    return jnp.where(chosen, LEN, ragged).astype(jnp.int32)


def draw_gains(key, part):
    key = jax.random.fold_in(key, 12)
    ramp = jnp.arange(D, dtype=jnp.float32) / D
    noise = jax.random.uniform(key, (2, D), jnp.float32, 0.8, 1.2)
    base = 0.5 + ramp
    return (base[None, :] * noise).astype(jnp.float32)


def draw_mixes(key, part):
    key = jax.random.fold_in(key, 13)
    key_diag, key_off = jax.random.split(key)
    eye = jnp.eye(HEADS, dtype=jnp.float32)
    diag = jax.random.uniform(key_diag, (2, HEADS, HEADS), jnp.float32, 0.7, 1.3)
    off = jnp.clip(0.3 * jax.random.normal(key_off, (2, HEADS, HEADS), jnp.float32), -0.9, 0.9)
    return (eye * diag + (1.0 - eye) * off).astype(jnp.float32)


def block_levels(rng, extent, cuts, smallest, high):
    def one(axis_at, parts):
        draws = jax.random.uniform(jax.random.fold_in(jax.random.fold_in(rng, 6), axis_at), (parts,), jnp.float32, smallest / len(cuts), high / len(cuts))
        return jnp.repeat(jnp.exp(draws), extent[axis_at] // parts).reshape((-1,) + (1,) * (len(extent) - axis_at - 1))

    gain = one(*cuts[0])
    for cut in cuts[1:]:
        gain = gain * one(*cut)
    return gain


def normal_values(key, shape, deviation, limit, cuts=(), kind=jnp.bfloat16):
    values = deviation * jax.random.normal(key, shape, jnp.float32)
    if cuts:
        values = values * block_levels(key, shape, cuts, -0.22, 0.18)
    return jnp.clip(values, -limit, limit).astype(kind)


def setup_inputs(seed: int = 0) -> dict:
    key_list = jax.random.split(jax.random.key(seed), 28)
    return {
        "tokens": normal_values(key_list[0], (BATCH, LEN, D), 1.0, 6.0, ((0, 8), (1, 4))),
        "cotangent": normal_values(key_list[1], (BATCH, LEN, D), 1.0, 6.0, ((0, 8), (1, 4))),
        "lengths": draw_lengths(jax.random.fold_in(key_list[27], 71), 0),
        "qkv_weight": normal_values(key_list[3], (D, 3 * D), D ** -0.5, 0.21875, ((0, 8),), jnp.float32),
        "qkv_first": normal_values(key_list[4], (D, 3 * D), ((0.32 / (D * D)) ** 0.5), 0.00390625, ((0, 8),), jnp.float32),
        "qkv_second": jnp.clip(jnp.exp(math.log(2.1701389414374717e-06) - 1.3862944 * jax.random.uniform(key_list[5], (D, 3 * D), jnp.float32) ** block_levels(key_list[5], (D, 3 * D), ((0, 8),), -0.2, 0.2)), 5.425347353593679e-07, 2.1701389414374717e-06),
        "qkv_average": normal_values(key_list[6], (D, 3 * D), D ** -0.5, 0.21875, ((0, 8),), jnp.float32),
        "proj_weight": normal_values(key_list[7], (D, D), (D * 16 // LEN) ** -0.5, 1.75, ((0, 8),), jnp.float32),
        "proj_first": normal_values(key_list[8], (D, D), ((0.004 / (D * D)) ** 0.5), 0.00048828125, ((0, 8),), jnp.float32),
        "proj_second": jnp.clip(jnp.exp(math.log(2.7126736412697028e-08) - 1.3862944 * jax.random.uniform(key_list[9], (D, D), jnp.float32) ** block_levels(key_list[9], (D, D), ((0, 8),), -0.2, 0.2)), 6.781684103174257e-09, 2.7126736412697028e-08),
        "proj_average": normal_values(key_list[10], (D, D), (D * 16 // LEN) ** -0.5, 1.75, ((0, 8),), jnp.float32),
        "inner_weight": normal_values(key_list[11], (D, FF), D ** -0.5, 0.21875, ((0, 8),), jnp.float32),
        "inner_first": normal_values(key_list[12], (D, FF), ((0.012 / (D * FF)) ** 0.5), 0.0004272461, ((0, 8),), jnp.float32),
        "inner_second": jnp.clip(jnp.exp(math.log(2.034505186543356e-08) - 1.3862944 * jax.random.uniform(key_list[13], (D, FF), jnp.float32) ** block_levels(key_list[13], (D, FF), ((0, 8),), -0.2, 0.2)), 5.08626296635839e-09, 2.034505186543356e-08),
        "inner_average": normal_values(key_list[14], (D, FF), D ** -0.5, 0.21875, ((0, 8),), jnp.float32),
        "outer_weight": normal_values(key_list[15], (FF, D), FF ** -0.5, 0.109375, ((0, 8),), jnp.float32),
        "outer_first": normal_values(key_list[16], (FF, D), ((0.03 / (D * FF)) ** 0.5), 0.0007324219, ((0, 8),), jnp.float32),
        "outer_second": jnp.clip(jnp.exp(math.log(5.086263143994074e-08) - 1.3862944 * jax.random.uniform(key_list[17], (FF, D), jnp.float32) ** block_levels(key_list[17], (FF, D), ((0, 8),), -0.2, 0.2)), 1.2715657859985185e-08, 5.086263143994074e-08),
        "outer_average": normal_values(key_list[18], (FF, D), FF ** -0.5, 0.109375, ((0, 8),), jnp.float32),
        "gains": draw_gains(jax.random.fold_in(key_list[27], 71), 0),
        "gain_first": normal_values(key_list[20], (2, D), (4 * (4 * D * D + 2 * D * FF) ** -0.5), 0.009765625, ((1, 8),), jnp.float32),
        "gain_second": jnp.clip(jnp.exp(math.log(9.042245437740348e-06) - 1.3862944 * jax.random.uniform(key_list[21], (2, D), jnp.float32) ** block_levels(key_list[21], (2, D), ((1, 8),), -0.2, 0.2)), 2.260561359435087e-06, 9.042245437740348e-06),
        "gain_average": jnp.clip(1.0 + 0.18 * jax.random.normal(key_list[22], (2, D), jnp.float32), 0.1, 1.9),
        "mixes": draw_mixes(jax.random.fold_in(key_list[27], 71), 0),
        "mix_first": normal_values(key_list[24], (2, HEADS, HEADS), (8 * (4 * D * D + 2 * D * FF) ** -0.5), 0.01953125, (), jnp.float32),
        "mix_second": jnp.clip(jnp.exp(jax.random.uniform(key_list[25], (2, HEADS, HEADS), jnp.float32, math.log(9.042245437740348e-06), math.log(3.616898175096139e-05))), 9.042245437740348e-06, 3.616898175096139e-05),
        "mix_average": jnp.clip(jax.random.uniform(key_list[26], (2, HEADS, HEADS), jnp.float32, -0.4, 1.2), -0.4, 1.2),
    }


NORM_EPS = 1e-06
BETA = 0.5
ADAM_EPS = 1e-08
DECAY = 0.01
EMA_KEEP = 0.8
CLIP = 1.0
TOP_PRECISION = lax.Precision.HIGHEST

@jax.custom_vjp
def low(v):
    return lax.optimization_barrier(v.astype(jnp.bfloat16)).astype(jnp.float32)

@jax.custom_vjp
def low_back(v):
    return v

def low_keep(v):
    return (low(v), None)

def low_pass(kept, grad):
    return (grad,)

def back_keep(v):
    return (v, None)

def back_low(kept, grad):
    return (low(grad),)
low.defvjp(low_keep, low_pass)
low_back.defvjp(back_keep, back_low)

def normalize(values):
    return values * lax.rsqrt(lax.optimization_barrier(jnp.mean(values * values, axis=-1, keepdims=True)) + NORM_EPS)

def matmul(left_operand, right_operand):
    return jnp.einsum('tpw,we->tpe', left_operand, right_operand, precision=TOP_PRECISION)

def attention(queries, keys_all, values_all, mixes, seq_lengths):
    block_rows = min(512, LEN)
    scaling = 1.0 / math.sqrt(HEAD_DIM)
    key_pos = jnp.arange(LEN, dtype=jnp.int32)

    def one_block(block_index):
        first_row = block_index * block_rows
        rows_q = lax.dynamic_slice_in_dim(queries, first_row, block_rows, 1)
        scores = low_back(low(jnp.einsum('sqhe,skhe->shqk', rows_q, keys_all, precision=TOP_PRECISION) * scaling))
        mixed = low_back(jnp.einsum('hj,shqk->sjqk', mixes[0], scores, precision=TOP_PRECISION))
        query_pos = first_row + jnp.arange(block_rows, dtype=jnp.int32)
        allowed = (key_pos[None, None, None, :] <= query_pos[None, None, :, None]) & (key_pos[None, None, None, :] < seq_lengths[:, None, None, None])
        mixed = jnp.where(allowed, mixed, -1e+30)
        shifted = jnp.exp(mixed - lax.optimization_barrier(jnp.max(mixed, axis=-1, keepdims=True)))
        probs = low(shifted / lax.optimization_barrier(jnp.sum(shifted, axis=-1, keepdims=True)))
        weights_low = low_back(low(jnp.einsum('ji,sjqk->siqk', mixes[1], probs, precision=TOP_PRECISION)))
        return jnp.einsum('siqk,skie->sqie', weights_low, values_all, precision=TOP_PRECISION)
    blocks = lax.map(jax.checkpoint(one_block), jnp.arange(LEN // block_rows, dtype=jnp.int32))
    return jnp.moveaxis(blocks, 0, 1).reshape(queries.shape[0], LEN, D)

def layer(block_in, seq_lengths, params):
    qkv_w, proj_w, inner_w, outer_w, gain_w, mix_w = params
    gains_low = low(gain_w)
    first_layer_input = low(normalize(block_in) * gains_low[0])
    qkv = low_back(low(matmul(first_layer_input, low(qkv_w))))
    shape_four = (block_in.shape[0], LEN, HEADS, HEAD_DIM)
    queries = qkv[..., :D].reshape(shape_four)
    keys_all = qkv[..., D:2 * D].reshape(shape_four)
    values_all = qkv[..., 2 * D:].reshape(shape_four)
    attention_output = low_back(low(attention(queries, keys_all, values_all, mix_w, seq_lengths)))
    residual_stream = block_in + low_back(matmul(attention_output, low(proj_w)))
    second_layer_input = low(normalize(residual_stream) * gains_low[1])
    hidden_state = low_back(matmul(second_layer_input, low(inner_w)))
    active = low(jax.nn.gelu(hidden_state, approximate=True))
    return residual_stream + matmul(active, low(outer_w))

def adamw(weight, first, second, average, grad, rate):
    first_new = BETA * first + (1.0 - BETA) * grad
    second_new = BETA * second + (1.0 - BETA) * grad * grad
    fix = 1.0 - BETA ** STEP
    weight_new = weight - rate * (first_new / fix / (jnp.sqrt(second_new / fix) + ADAM_EPS) + DECAY * weight)
    average_new = EMA_KEEP * average + (1.0 - EMA_KEEP) * weight_new
    return (first_new, second_new, weight_new, average_new)

def reference(tokens, cotangent, lengths, qkv_weight, qkv_first, qkv_second, qkv_average, proj_weight, proj_first, proj_second, proj_average, inner_weight, inner_first, inner_second, inner_average, outer_weight, outer_first, outer_second, outer_average, gains, gain_first, gain_second, gain_average, mixes, mix_first, mix_second, mix_average):
    per_step = math.gcd(BATCH, max(1, 4096 // LEN))
    step_count = BATCH // per_step
    group_layer = jax.checkpoint(layer)

    def forward(block_in, qkv_w, proj_w, inner_w, outer_w, gain_w, mix_w):
        params = (qkv_w, proj_w, inner_w, outer_w, gain_w, mix_w)

        def one_group(paired):
            return group_layer(paired[0], paired[1], params)
        grouped = (block_in.reshape(step_count, per_step, LEN, D), lengths.reshape(step_count, per_step))
        return lax.map(one_group, grouped).reshape(BATCH, LEN, D)
    result, pull_back = jax.vjp(forward, tokens.astype(jnp.float32), qkv_weight, proj_weight, inner_weight, outer_weight, gains, mixes)
    live = (jnp.arange(LEN, dtype=jnp.int32)[None, :] < lengths[:, None]).astype(jnp.float32)
    grads = pull_back(cotangent.astype(jnp.float32) * live[:, :, None])
    grad_tokens = grads[0]
    squares = jnp.sum(grads[1] * grads[1])
    for grad_part in grads[2:]:
        squares = squares + jnp.sum(grad_part * grad_part)
    grad_norm = jnp.sqrt(squares)
    factor = CLIP / jnp.maximum(grad_norm, CLIP)
    clipped_gains = grads[5] * factor
    qkv_new = adamw(qkv_weight, qkv_first, qkv_second, qkv_average, grads[1] * factor, 0.03)
    proj_new = adamw(proj_weight, proj_first, proj_second, proj_average, grads[2] * factor, 0.1)
    inner_new = adamw(inner_weight, inner_first, inner_second, inner_average, grads[3] * factor, 0.03)
    outer_new = adamw(outer_weight, outer_first, outer_second, outer_average, grads[4] * factor, 0.02)
    gain_new = adamw(gains, gain_first, gain_second, gain_average, clipped_gains, 0.3)
    mix_new = adamw(mixes, mix_first, mix_second, mix_average, grads[6] * factor, 0.3)
    return (result.astype(jnp.bfloat16), grad_tokens, grad_norm, qkv_new[0], qkv_new[1], qkv_new[2], qkv_new[3], proj_new[0], proj_new[1], proj_new[2], proj_new[3], inner_new[0], inner_new[1], inner_new[2], inner_new[3], outer_new[0], outer_new[1], outer_new[2], outer_new[3], gain_new[0], gain_new[1], gain_new[2], gain_new[3], mix_new[0], mix_new[1], mix_new[2], mix_new[3], clipped_gains)
```

```python
from functools import partial
import math

import jax
import jax.numpy as jnp
from jax import lax
from jax.experimental import pallas as pl
from jax.experimental.pallas import tpu as pltpu
from jax.sharding import PartitionSpec as P

STEP = 10

NORM_EPS = 1e-06
BETA = 0.5
ADAM_EPS = 1e-08
DECAY = 0.01
EMA_KEEP = 0.8
CLIP = 1.0

BF = jnp.bfloat16
F32 = jnp.float32
ROWS = 128
KEYS = 256
GROUP = 16
LANES = 128
SIDE = {1: 4, 2: 4, 3: 2, 4: 2}
NT = (((1,), (1,)), ((), ()))
NN = (((1,), (0,)), ((), ()))
TN = (((0,), (0,)), ((), ()))


def dot(left, right, dims=NN):
    return lax.dot_general(left, right, dims, preferred_element_type=F32)


def inverse_rms(values):
    return lax.rsqrt(jnp.mean(values * values, axis=-1, keepdims=True) + NORM_EPS)


def rms_backward(scale_inv, normed, grad_normed):
    return scale_inv * (
        grad_normed - normed * jnp.mean(normed * grad_normed, axis=-1, keepdims=True)
    )


def adamw(weight, first, second, average, grad, rate):
    first_new = BETA * first + (1.0 - BETA) * grad
    second_new = BETA * second + (1.0 - BETA) * grad * grad
    fix = 1.0 - BETA**STEP
    weight_new = weight - rate * (
        first_new / fix / (jnp.sqrt(second_new / fix) + ADAM_EPS) + DECAY * weight
    )
    average_new = EMA_KEEP * average + (1.0 - EMA_KEEP) * weight_new
    return (first_new, second_new, weight_new, average_new)


def swap(value, axis, mask):
    size = lax.axis_size(axis)
    return lax.ppermute(value, axis, [(i, i ^ mask) for i in range(size)])


def digits_of(size):
    found = []
    stride = 1
    while stride < size:
        radix = 2 if stride == 1 or size // stride < 4 else 4
        found.append((stride, radix))
        stride *= radix
    return found


def gather_shards(shard, axis):
    size = lax.axis_size(axis)
    have = shard[None]
    for stride, radix in reversed(digits_of(size)):
        parts = [have] + [swap(have, axis, k * stride) for k in range(1, radix)]
        have = jnp.stack(parts, 1).reshape((-1,) + shard.shape)
    order = jnp.bitwise_xor(jnp.arange(size, dtype=jnp.int32), lax.axis_index(axis))
    return have.at[order].get(mode="promise_in_bounds")


def reduce_shards(blocks, axis, small_first):
    size = lax.axis_size(axis)
    order = jnp.bitwise_xor(jnp.arange(size, dtype=jnp.int32), lax.axis_index(axis))
    blocks = blocks.at[order].get(mode="promise_in_bounds")
    digits = digits_of(size)
    left = list(reversed(digits))
    blocks = blocks.reshape(tuple(radix for _, radix in left) + blocks.shape[1:])
    for at, (stride, radix) in enumerate(digits if small_first else reversed(digits)):
        place = left.index((stride, radix))
        left.pop(place)
        if at:
            blocks = blocks.astype(BF)
        pieces = [lax.index_in_dim(blocks, k, place, keepdims=False) for k in range(radix)]
        total = pieces[0].astype(F32)
        for k in range(1, radix):
            total = total + swap(pieces[k], axis, k * stride).astype(F32)
        blocks = total
    return blocks


def sum_everywhere(value, axis):
    size = lax.axis_size(axis)
    mask = 1
    while mask < size:
        value = value + swap(value, axis, mask)
        mask *= 2
    return value


def after(value, *first):
    return lax.optimization_barrier((value,) + first)[0]


def spread(matrix):
    high = matrix.astype(BF)
    low = (matrix - lax.optimization_barrier(high).astype(F32)).astype(BF)
    eye = jnp.eye(GROUP, dtype=BF)
    both = jnp.stack([high, low])
    count = matrix.shape[0] * GROUP
    wide = both[:, :, None, :, None] * eye[None, None, :, None, :]
    return wide.reshape(2 * count, count)


def two_heads(rows, first, second):
    return jnp.concatenate([rows * first, rows * second], 0)


def mix(matrix, values):
    out = dot(matrix, values)
    half = matrix.shape[0] // 2
    return out[:half] + out[half:]


def head_masks(scaling):
    lane = lax.broadcasted_iota(jnp.int32, (1, LANES), 1)
    low = lane < LANES // 2
    return low, jnp.where(low, scaling, 0.0).astype(BF), jnp.where(low, 0.0, scaling).astype(BF)


def fill_sequence(meta, sources, qkv, sems):
    me = meta[1]
    width = qkv.shape[1] // 3
    copies = []
    for part in range(3):
        for d in range(4):
            source = sources[4 * part + d]
            start = pl.multiple_of(jnp.bitwise_xor(me, d) * KEYS, KEYS)
            copies.append(
                pltpu.make_async_copy(
                    source,
                    qkv.at[pl.ds(start, KEYS), part * width : (part + 1) * width],
                    sems.at[4 * part + d],
                )
            )
    for copy in copies:
        copy.start()
    for copy in copies:
        copy.wait()


def forward_kernel(meta, *refs):
    sources, (pre, post, attended, probs, weights, qkv, held, sems) = refs[:12], refs[12:]
    heads = probs.shape[0]
    width = attended.shape[1]
    pairs = heads // 2
    tall = heads * GROUP
    step = pl.program_id(0)
    pl.when(step == 0)(partial(fill_sequence, meta, sources, qkv, sems))
    length = meta[0]
    row0 = pl.multiple_of(step * KEYS + meta[2] * ROWS, ROWS)
    chunks = (jnp.minimum(row0 + ROWS, length) + KEYS - 1) // KEYS
    low, first_s, second_s = head_masks(1.0 / math.sqrt(width // heads))

    def score(kc, carry):
        k0 = pl.multiple_of(kc * KEYS, KEYS)
        for p in range(pairs):
            at = p * LANES
            queries = two_heads(qkv[pl.ds(row0, ROWS), at : at + LANES], first_s, second_s)
            keys = qkv[pl.ds(k0, KEYS), width + at : width + at + LANES]
            scores = dot(queries, keys, NT).astype(BF)
            weights[2 * p : 2 * p + 2, :, pl.ds(k0, KEYS)] = scores.reshape(2, ROWS, KEYS)
        return carry

    lax.fori_loop(0, chunks, score, 0)

    def group(n, batch, carry):
        side = SIDE[n]
        rows = [
            pl.ds(pl.multiple_of((batch * side + u) * GROUP, GROUP), GROUP) for u in range(side)
        ]
        col_at = lax.broadcasted_iota(jnp.int32, (GROUP, KEYS), 1)
        row_at = lax.broadcasted_iota(jnp.int32, (GROUP, KEYS), 0)
        peak = [None] * side
        total = [None] * side
        for kc in range(n):
            cols = slice(kc * KEYS, (kc + 1) * KEYS)
            for u in range(side):
                mixed = mix(pre[...], weights[:, rows[u], cols].reshape(tall, KEYS))
                key_pos = col_at + kc * KEYS
                query_pos = row0 + (batch * side + u) * GROUP + row_at
                allowed = (key_pos <= query_pos) & (key_pos < length)
                mixed = jnp.where(allowed[None], mixed.reshape(heads, GROUP, KEYS), -1e30)
                mixed = mixed.reshape(tall, KEYS)
                held[u, :, cols] = mixed
                part = jnp.maximum(mixed[:, :LANES], mixed[:, LANES:])
                peak[u] = part if kc == 0 else jnp.maximum(peak[u], part)
        top = [jnp.max(peak[u], axis=1, keepdims=True) for u in range(side)]
        for kc in range(n):
            cols = slice(kc * KEYS, (kc + 1) * KEYS)
            for u in range(side):
                shifted = jnp.exp(held[u, :, cols] - top[u])
                held[u, :, cols] = shifted
                part = shifted[:, :LANES] + shifted[:, LANES:]
                total[u] = part if kc == 0 else total[u] + part
        inverse = [1.0 / jnp.sum(total[u], axis=1, keepdims=True) for u in range(side)]
        for kc in range(n):
            cols = slice(kc * KEYS, (kc + 1) * KEYS)
            for u in range(side):
                low_probs = (held[u, :, cols] * inverse[u]).astype(BF)
                probs[:, rows[u], cols] = low_probs.reshape(heads, GROUP, KEYS)
                mixed = mix(post[...], low_probs).astype(BF)
                weights[:, rows[u], cols] = mixed.reshape(heads, GROUP, KEYS)
        return carry

    def rest(n):
        lax.fori_loop(0, ROWS // GROUP // SIDE[n], partial(group, n), 0)
        for p in range(pairs):
            at = p * LANES
            pair = weights[2 * p : 2 * p + 2, :, : n * KEYS].reshape(2 * ROWS, n * KEYS)
            out = dot(pair, qkv[: n * KEYS, 2 * width + at : 2 * width + at + LANES])
            attended[:, at : at + LANES] = jnp.where(low, out[:ROWS], out[ROWS:]).astype(BF)

    for n in range(1, probs.shape[2] // KEYS + 1):
        pl.when(chunks == n)(partial(rest, n))


def backward_kernel(meta, *refs):
    sources, refs = refs[:12], refs[12:]
    grad_rows, pre, post, probs, weights, grad_q, grad_kv, grad_pre, grad_post = refs[:9]
    qkv, scores, grads, held, sum_pre, sum_post, sems = refs[9:]
    heads = probs.shape[0]
    width = grad_rows.shape[1]
    pairs = heads // 2
    tall = heads * GROUP
    step = pl.program_id(0)
    me = meta[1]

    @pl.when(step == 0)
    def _():
        grad_kv[...] = jnp.zeros_like(grad_kv)
        sum_pre[...] = jnp.zeros_like(sum_pre)
        sum_post[...] = jnp.zeros_like(sum_post)
        fill_sequence(meta, sources, qkv, sems)

    length = meta[0]
    row0 = pl.multiple_of(step * KEYS + meta[2] * ROWS, ROWS)
    chunks = (jnp.minimum(row0 + ROWS, length) + KEYS - 1) // KEYS
    chunks = jnp.where(row0 < length, chunks, 0)
    scaling = 1.0 / math.sqrt(width // heads)
    low, first_s, second_s = head_masks(scaling)
    low, first_one, second_one = head_masks(1.0)

    @pl.when(chunks == 0)
    def _():
        grad_q[...] = jnp.zeros_like(grad_q)

    def score(kc, carry):
        k0 = pl.multiple_of(kc * KEYS, KEYS)
        for p in range(pairs):
            at = p * LANES
            queries = two_heads(qkv[pl.ds(row0, ROWS), at : at + LANES], first_s, second_s)
            grad = two_heads(grad_rows[:, at : at + LANES], first_one, second_one)
            keys = qkv[pl.ds(k0, KEYS), width + at : width + at + LANES]
            values = qkv[pl.ds(k0, KEYS), 2 * width + at : 2 * width + at + LANES]
            both = slice(2 * p, 2 * p + 2)
            cols = pl.ds(k0, KEYS)
            scores[both, :, cols] = dot(queries, keys, NT).astype(BF).reshape(2, ROWS, KEYS)
            grads[both, :, cols] = dot(grad, values, NT).astype(BF).reshape(2, ROWS, KEYS)
        return carry

    lax.fori_loop(0, chunks, score, 0)

    def group(n, batch, carry):
        side = SIDE[n]
        rows = [
            pl.ds(pl.multiple_of((batch * side + u) * GROUP, GROUP), GROUP) for u in range(side)
        ]
        span = slice(0, n * KEYS)
        total = [None] * side
        for kc in range(n):
            cols = slice(kc * KEYS, (kc + 1) * KEYS)
            for u in range(side):
                grad_probs = mix(post[...], grads[:, rows[u], cols].reshape(tall, KEYS))
                held[u, :, cols] = grad_probs
                term = probs[:, rows[u], cols].reshape(tall, KEYS).astype(F32) * grad_probs
                part = term[:, :LANES] + term[:, LANES:]
                total[u] = part if kc == 0 else total[u] + part
        added = None
        for u in range(side):
            left = probs[:, rows[u], span].reshape(tall, n * KEYS)
            term = dot(left, grads[:, rows[u], span].reshape(tall, n * KEYS), NT)
            added = term if u == 0 else added + term
        sum_post[...] += added
        delta = [jnp.sum(total[u], axis=1, keepdims=True) for u in range(side)]
        mixed = [[] for _ in range(side)]
        for kc in range(n):
            cols = slice(kc * KEYS, (kc + 1) * KEYS)
            for u in range(side):
                prob = probs[:, rows[u], cols].reshape(tall, KEYS).astype(F32)
                grad_mixed = (prob * (held[u, :, cols] - delta[u])).astype(BF)
                mixed[u].append(grad_mixed)
                back = mix(pre[...], grad_mixed).astype(BF)
                grads[:, rows[u], cols] = back.reshape(heads, GROUP, KEYS)
        added = None
        for u in range(side):
            left = scores[:, rows[u], span].reshape(tall, n * KEYS)
            term = dot(left, jnp.concatenate(mixed[u], 1), NT)
            added = term if u == 0 else added + term
        sum_pre[...] += added
        return carry

    def rest(n):
        lax.fori_loop(0, ROWS // GROUP // SIDE[n], partial(group, n), 0)
        for p in range(pairs):
            at = p * LANES
            mine = slice(at, at + LANES)
            both = slice(2 * p, 2 * p + 2)
            queries = two_heads(qkv[pl.ds(row0, ROWS), mine], first_s, second_s).T
            grad = two_heads(grad_rows[:, mine], first_one, second_one).T
            back = grads[both, :, : n * KEYS].reshape(2 * ROWS, n * KEYS)
            out = dot(back, qkv[: n * KEYS, width + at : width + at + LANES])
            grad_q[:, mine] = (jnp.where(low, out[:ROWS], out[ROWS:]) * scaling).astype(BF)
            for kc in range(n):
                cols = slice(kc * KEYS, (kc + 1) * KEYS)
                d = jnp.bitwise_xor(me, kc)
                to = 2 * jnp.bitwise_and(d, 1) + d // 2
                grad_kv[to, mine, :] += dot(queries, grads[both, :, cols].reshape(2 * ROWS, KEYS))
                grad_kv[to, width + at : width + at + LANES, :] += dot(
                    grad, weights[both, :, cols].reshape(2 * ROWS, KEYS)
                )

    for n in range(1, probs.shape[2] // KEYS + 1):
        pl.when(chunks == n)(partial(rest, n))

    @pl.when(step == pl.num_programs(0) - 1)
    def _():
        row = lax.broadcasted_iota(jnp.int32, (tall, tall), 0)
        col = lax.broadcasted_iota(jnp.int32, (tall, tall), 1)
        same = row % GROUP == col % GROUP
        pick = (
            lax.broadcasted_iota(jnp.int32, (tall, LANES), 0) // GROUP
            == lax.broadcasted_iota(jnp.int32, (tall, LANES), 1)
        ).astype(F32)
        for source, out in ((sum_pre, grad_pre), (sum_post, grad_post)):
            kept = jnp.where(same, source[...], 0.0)
            wide = lax.dot_general(
                kept, pick, NN, precision=lax.Precision.HIGHEST, preferred_element_type=F32
            )
            for head in range(heads):
                out[head : head + 1, :] = jnp.sum(
                    wide[head * GROUP : (head + 1) * GROUP], axis=0, keepdims=True
                )


ANY = pl.BlockSpec(memory_space=pl.ANY)


def is_live(step, meta):
    return step * KEYS + meta[2] * ROWS < meta[0]


def attend(meta, sources, pre, post, heads):
    width = sources[0].shape[1]
    tall = heads * GROUP
    steps = 4
    full_len = steps * KEYS
    matrix = pl.BlockSpec((2 * tall, tall), lambda i, m: (0, 0), pipeline_mode=pl.Buffered(1))
    wide = pl.BlockSpec(
        (None, heads, ROWS, full_len), lambda i, m: (jnp.where(is_live(i, m), i, steps), 0, 0, 0)
    )
    kept = jax.ShapeDtypeStruct((steps + 1, heads, ROWS, full_len), BF)
    return pl.pallas_call(
        forward_kernel,
        grid_spec=pltpu.PrefetchScalarGridSpec(
            num_scalar_prefetch=1,
            grid=(steps,),
            in_specs=[ANY] * 12 + [matrix, matrix],
            out_specs=[
                pl.BlockSpec((None, ROWS, width), lambda i, m: (jnp.bitwise_xor(i, m[1]), 0, 0)),
                wide,
                wide,
            ],
            scratch_shapes=[
                pltpu.VMEM((full_len, 3 * width), BF),
                pltpu.VMEM((4, tall, full_len), F32),
                pltpu.SemaphoreType.DMA((12,)),
            ],
        ),
        out_shape=[jax.ShapeDtypeStruct((steps, ROWS, width), BF), kept, kept],
        compiler_params=pltpu.CompilerParams(vmem_limit_bytes=56 * 2**20),
        cost_estimate=pl.CostEstimate(
            flops=26 * 10**9, bytes_accessed=30 * 10**6, transcendentals=0
        ),
        name="attend",
    )(meta, *sources, pre, post)


def attend_back(meta, sources, grad_rows, pre, post, probs, weights):
    width = sources[0].shape[1]
    steps = 4
    heads = probs.shape[1]
    tall = heads * GROUP
    full_len = steps * KEYS

    def newest(step, meta):
        last = 0
        for other in range(1, steps):
            last = jnp.where(is_live(other, meta), other, last)
        return jnp.minimum(step, last)

    matrix = pl.BlockSpec((2 * tall, tall), lambda i, m: (0, 0), pipeline_mode=pl.Buffered(1))
    wide = pl.BlockSpec((None, heads, ROWS, full_len), lambda i, m: (newest(i, m), 0, 0, 0))
    rows = pl.BlockSpec((None, ROWS, width), lambda i, m: (jnp.bitwise_xor(i, m[1]), 0, 0))
    small = pl.BlockSpec((heads, LANES), lambda i, m: (0, 0))
    return pl.pallas_call(
        backward_kernel,
        grid_spec=pltpu.PrefetchScalarGridSpec(
            num_scalar_prefetch=1,
            grid=(steps,),
            in_specs=[ANY] * 12 + [rows, matrix, matrix, wide, wide],
            out_specs=[
                rows,
                pl.BlockSpec(
                    (4, 2 * width, KEYS), lambda i, m: (0, 0, 0), pipeline_mode=pl.Buffered(1)
                ),
                small,
                small,
            ],
            scratch_shapes=[
                pltpu.VMEM((full_len, 3 * width), BF),
                pltpu.VMEM((heads, ROWS, full_len), BF),
                pltpu.VMEM((heads, ROWS, full_len), BF),
                pltpu.VMEM((4, tall, full_len), F32),
                pltpu.VMEM((tall, tall), F32),
                pltpu.VMEM((tall, tall), F32),
                pltpu.SemaphoreType.DMA((12,)),
            ],
        ),
        out_shape=[
            jax.ShapeDtypeStruct((steps, ROWS, width), BF),
            jax.ShapeDtypeStruct((4, 2 * width, KEYS), F32),
            jax.ShapeDtypeStruct((heads, LANES), F32),
            jax.ShapeDtypeStruct((heads, LANES), F32),
        ],
        compiler_params=pltpu.CompilerParams(vmem_limit_bytes=60 * 2**20),
        cost_estimate=pl.CostEstimate(
            flops=40 * 10**9, bytes_accessed=40 * 10**6, transcendentals=0
        ),
        name="attend_back",
    )(meta, *sources, grad_rows, pre, post, probs, weights)


def on_device(
    tokens,
    cotangent,
    lengths,
    qkv_weight,
    qkv_first,
    qkv_second,
    qkv_average,
    proj_weight,
    proj_first,
    proj_second,
    proj_average,
    inner_weight,
    inner_first,
    inner_second,
    inner_average,
    outer_weight,
    outer_first,
    outer_second,
    outer_average,
    gains,
    gain_first,
    gain_second,
    gain_average,
    mixes,
    mix_first,
    mix_second,
    mix_average,
):
    group_seqs, shard_len, width = tokens.shape
    owners = lax.axis_size("dp")
    heads = mixes.shape[1]
    own_rows = qkv_weight.shape[0]
    hidden = inner_weight.shape[1]
    half = width // 2
    slice_ff = hidden // owners // 2
    me = lax.axis_index("seq")
    pair = me // 2
    core = jnp.bitwise_and(me, 1)

    def by_core(mine, other, axis):
        return jnp.where(
            core == 0,
            jnp.concatenate([mine, other], axis),
            jnp.concatenate([other, mine], axis),
        )

    ahead = (lengths[None, :] > lengths[:, None]) | (
        (lengths[None, :] == lengths[:, None])
        & (jnp.arange(group_seqs)[None, :] < jnp.arange(group_seqs)[:, None])
    )
    rank = jnp.sum(ahead.astype(jnp.int32), axis=1)
    order = jnp.sum(
        jnp.where(
            rank[None, :] == jnp.arange(group_seqs)[:, None], jnp.arange(group_seqs)[None, :], 0
        ),
        axis=1,
    ).astype(jnp.int32)

    def sequence_of(slot, which):
        return order[which if slot == 0 else group_seqs - 1 - which]

    def arrange(value):
        return jnp.stack(
            [
                jnp.stack(
                    [
                        lax.dynamic_index_in_dim(
                            value, sequence_of(slot, jnp.bitwise_xor(pair, d)), 0, False
                        )
                        for d in range(2)
                    ]
                )
                for slot in range(2)
            ]
        )

    def restore(value):
        flat = value.reshape((4,) + value.shape[2:])
        which = jnp.where(rank < 2, rank, 3 - rank)
        place = 2 * (rank // 2) + jnp.bitwise_xor(which, pair)
        return flat.at[place].get(mode="promise_in_bounds")

    lengths_here = arrange(lengths)
    metas = [jnp.stack([lengths_here[slot, 0], me, core]).astype(jnp.int32) for slot in range(2)]

    gain_low = gather_shards(gains.astype(BF), "dp")
    gain_vals = jnp.moveaxis(gain_low, 0, 1).reshape(2, width).astype(F32)
    qkv_low = qkv_weight.astype(BF)
    gathered = []
    gate = None
    for part in range(3):
        mine = lax.dynamic_slice_in_dim(qkv_low, part * width + core * half, half, 1)
        if gate is not None:
            mine = after(mine, gate)
        whole = gather_shards(mine, "dp").reshape(owners * own_rows, half)
        gate = whole
        gathered.append(by_core(whole, swap(whole, "seq", 1), 1))

    proj_low = after(proj_weight.astype(BF), gate)
    inner_mine = inner_weight.astype(BF).reshape(own_rows, owners, 2, slice_ff)
    inner_mine = lax.dynamic_index_in_dim(inner_mine, core, 2, False)
    inner_mine = inner_mine.reshape(own_rows, owners * slice_ff)
    outer_mine = outer_weight.astype(BF).reshape(2, slice_ff, width)
    outer_mine = lax.dynamic_index_in_dim(outer_mine, core, 0, False)
    proj_all = lax.all_gather(proj_low, "dp", axis=0, tiled=True)
    inner_halves = [lax.all_gather(after(inner_mine, gate), "dp", axis=0, tiled=True)]
    outer_halves = [lax.all_gather(after(outer_mine, gate), "dp", axis=0, tiled=True)]
    inner_halves.append(swap(inner_halves[0], "seq", 1))
    outer_halves.append(swap(outer_halves[0], "seq", 1))

    input_rows = arrange(tokens).astype(F32)
    scale_one = inverse_rms(input_rows)
    normed_one = input_rows * scale_one
    first_in = (normed_one * gain_vals[0]).astype(BF)
    sources = [[None] * 12, [None] * 12]
    gate = None
    for slot in range(2):
        for part in range(3):
            far = dot(first_in[slot, 1], gathered[part]).astype(BF)
            if gate is not None:
                far = after(far, gate)
            near = dot(first_in[slot, 0], gathered[part]).astype(BF)
            far = swap(far, "seq", 2)
            sources[slot][4 * part : 4 * part + 4] = [
                near,
                swap(near, "seq", 1),
                far,
                swap(far, "seq", 1),
            ]
        gate = far

    pre_mix, post_mix = spread(mixes[0].T), spread(mixes[1].T)
    pre_back, post_back = spread(mixes[0]), spread(mixes[1])

    def to_homes(rows):
        got = [rows[0]] + [swap(rows[d], "seq", d) for d in range(1, 4)]
        return jnp.stack([by_core(got[2 * d], got[2 * d + 1], 0) for d in range(2)])

    def from_homes(rows):
        halves = rows.reshape(2, 2, ROWS, width)
        found = []
        for d in range(4):
            block = lax.dynamic_index_in_dim(
                halves[d // 2], jnp.bitwise_xor(core, d % 2), 0, False
            )
            found.append(swap(block, "seq", d) if d else block)
        return jnp.stack(found)

    attended, probs, weights = [], [], []
    meta = metas[0]
    for slot in range(2):
        out, prob, weight = attend(meta, sources[slot], pre_mix, post_mix, heads)
        if slot == 0:
            meta, out = lax.optimization_barrier((metas[1], out))
        attended.append(to_homes(out))
        probs.append(prob)
        weights.append(weight)
    attention_output = jnp.stack(attended)

    resid = input_rows + jnp.einsum(
        "sdrk,kc->sdrc", attention_output, proj_all, preferred_element_type=F32
    )
    scale_two = inverse_rms(resid)
    normed_two = resid * scale_two
    second_in = (normed_two * gain_vals[1]).astype(BF)
    positions = me * shard_len + jnp.arange(shard_len, dtype=jnp.int32)
    live = positions[None, None, :] < lengths_here[:, :, None]
    cot = arrange(cotangent)
    grad_out = jnp.where(live[..., None], cot, jnp.zeros_like(cot))
    output = resid
    grad_second = 0.0
    grad_inner, grad_outer = [], []
    for inner, outer in zip(inner_halves, outer_halves):
        hidden_state = jnp.einsum("sdrk,kf->sdrf", second_in, inner, preferred_element_type=F32)
        active, gelu_back = jax.vjp(partial(jax.nn.gelu, approximate=True), hidden_state)
        active = active.astype(BF)
        output = output + jnp.einsum(
            "sdrf,fk->sdrk", active, outer, preferred_element_type=F32
        )
        grad_outer.append(
            jnp.einsum("sdrf,sdrk->fk", active, grad_out, preferred_element_type=F32)
        )
        grad_active = jnp.einsum("sdrk,fk->sdrf", grad_out, outer, preferred_element_type=F32)
        grad_hidden = gelu_back(grad_active)[0].astype(BF)
        grad_inner.append(
            jnp.einsum("sdrk,sdrf->kf", second_in, grad_hidden, preferred_element_type=F32)
        )
        grad_second = grad_second + jnp.einsum(
            "sdrf,kf->sdrk", grad_hidden, inner, preferred_element_type=F32
        )
    output = output.astype(BF)
    gain_two = jnp.sum(grad_second * normed_two, axis=(0, 1, 2))
    grad_resid = grad_out.astype(F32) + rms_backward(
        scale_two, normed_two, grad_second * gain_vals[1]
    )
    resid_low = grad_resid.astype(BF)
    grad_attended = jnp.einsum(
        "sdrc,kc->sdrk", resid_low, proj_all, preferred_element_type=F32
    ).astype(BF)
    grad_proj = jnp.einsum(
        "sdrk,sdrc->kc", attention_output, resid_low, preferred_element_type=F32
    )

    def reduce_halves(mine, other, small_first):
        total = mine + swap(other.astype(BF), "seq", 1).astype(F32)
        total = reduce_shards(total.astype(BF), "dp", small_first)
        total = lax.optimization_barrier(total.astype(BF))
        total = total.astype(F32) + swap(total, "seq", 2).astype(F32)
        return total, swap(total, "seq", 1)

    grad_proj = grad_proj.reshape(owners, own_rows, 2, half)
    proj_mine, proj_other = reduce_halves(
        lax.dynamic_index_in_dim(grad_proj, core, 2, False),
        lax.dynamic_index_in_dim(grad_proj, 1 - core, 2, False),
        True,
    )
    red_proj = by_core(proj_mine, proj_other, 1)
    inner_sums = reduce_halves(
        *[g.reshape(owners, own_rows, owners * slice_ff) for g in grad_inner], True
    )
    red_inner = by_core(
        *[g.reshape(own_rows, owners, 1, slice_ff) for g in inner_sums], 2
    ).reshape(own_rows, hidden)
    outer_sums = reduce_halves(
        *[g.reshape(owners, slice_ff, width) for g in grad_outer], False
    )
    red_outer = by_core(*outer_sums, 0)

    grad_rows = [from_homes(grad_attended[slot]) for slot in range(2)]
    meta = metas[0]
    grad_mixes = 0.0
    grad_q, grad_kv = [], []
    for slot in range(2):
        back_q, back_kv, back_pre, back_post = attend_back(
            meta, sources[slot], grad_rows[slot], pre_back, post_back, probs[slot], weights[slot]
        )
        if slot == 0:
            meta, back_kv = lax.optimization_barrier((metas[1], back_kv))
        grad_mixes = grad_mixes + jnp.stack([back_pre[:, :heads], back_post[:, :heads]])
        summed = (back_kv[:2] + swap(back_kv[2:], "seq", 1)).astype(BF)
        grad_kv.append(jnp.stack([summed[0], swap(summed[1], "seq", 2)]))
        grad_q.append(to_homes(back_q))

    grad_first = []
    grad_qkv = 0.0
    weight_kv = jnp.concatenate(gathered[1:], axis=1)
    for slot in range(2):
        grad_first.append(
            jnp.einsum("drk,ck->drc", grad_q[slot], gathered[0], preferred_element_type=F32)
            + jnp.einsum("dkr,ck->drc", grad_kv[slot], weight_kv, preferred_element_type=F32)
        )
        grad_qkv = grad_qkv + jnp.concatenate(
            [
                jnp.einsum("drc,drk->ck", first_in[slot], grad_q[slot], preferred_element_type=F32),
                jnp.einsum(
                    "drc,dkr->ck", first_in[slot], grad_kv[slot], preferred_element_type=F32
                ),
            ],
            axis=1,
        )
    grad_first = jnp.stack(grad_first)
    gain_one = jnp.sum(grad_first * normed_one, axis=(0, 1, 2))
    grad_qkv = grad_qkv.reshape(owners, own_rows, 3, 2, half)
    mine = lax.dynamic_index_in_dim(grad_qkv, core, 3, False)
    other = lax.dynamic_index_in_dim(grad_qkv, 1 - core, 3, False)
    q_sums = reduce_halves(mine[:, :, :1], other[:, :, :1], False)
    kv_sums = reduce_halves(mine[:, :, 1:], other[:, :, 1:], True)
    red_qkv = jnp.concatenate(
        [
            by_core(*[g[..., None, :] for g in sums], 2)
            for sums in (q_sums, kv_sums)
        ],
        axis=1,
    ).reshape(own_rows, 3 * width)

    small = jnp.concatenate([gain_one, gain_two, grad_mixes.reshape(-1)])
    pad = -small.shape[0] % (8 * LANES)
    small = jnp.pad(small, (0, pad)).reshape(-1, LANES)
    small = sum_everywhere(sum_everywhere(small, "seq"), "dp").reshape(-1)
    own = lax.axis_index("dp")
    red_gains = lax.dynamic_slice_in_dim(
        small[: 2 * width].reshape(2, width), own * own_rows, own_rows, 1
    )
    gain_all = small[: 2 * width]
    red_mixes = small[2 * width : 2 * width + grad_mixes.size].reshape(mixes.shape)

    grad_rows_tokens = grad_resid + rms_backward(
        scale_one, normed_one, grad_first * gain_vals[0]
    )

    local_squares = (
        jnp.sum(red_qkv * red_qkv)
        + jnp.sum(red_proj * red_proj)
        + jnp.sum(red_inner * red_inner)
        + jnp.sum(red_outer * red_outer)
    )
    total_squares = sum_everywhere(jnp.broadcast_to(local_squares, (8, LANES)), "dp")[0, 0]
    grad_norm = jnp.sqrt(
        total_squares + jnp.sum(gain_all * gain_all) + jnp.sum(red_mixes * red_mixes)
    )
    factor = CLIP / jnp.maximum(grad_norm, CLIP)
    clipped_gains = red_gains * factor
    qkv_new = adamw(qkv_weight, qkv_first, qkv_second, qkv_average, red_qkv * factor, 0.03)
    proj_new = adamw(proj_weight, proj_first, proj_second, proj_average, red_proj * factor, 0.1)
    inner_new = adamw(
        inner_weight, inner_first, inner_second, inner_average, red_inner * factor, 0.03
    )
    outer_new = adamw(
        outer_weight, outer_first, outer_second, outer_average, red_outer * factor, 0.02
    )
    gain_new = adamw(gains, gain_first, gain_second, gain_average, clipped_gains, 0.3)
    mix_new = adamw(mixes, mix_first, mix_second, mix_average, red_mixes * factor, 0.3)
    return (
        restore(output),
        restore(grad_rows_tokens),
        grad_norm,
        *qkv_new,
        *proj_new,
        *inner_new,
        *outer_new,
        *gain_new,
        *mix_new,
        clipped_gains,
    )


def solution(mesh):
    rows = P("dp", "seq", None)
    matrix = P("dp", None)
    vector = P(None, "dp")
    in_specs = (rows, rows, P("dp")) + (matrix,) * 16 + (vector,) * 4 + (P(),) * 4
    out_specs = (rows, rows, P()) + (matrix,) * 16 + (vector,) * 4 + (P(),) * 4 + (vector,)
    return jax.shard_map(
        on_device, mesh=mesh, in_specs=in_specs, out_specs=out_specs, check_vma=False
    )
```

```python
from functools import partial
import math

import jax
import jax.numpy as jnp
from jax import lax
from jax.experimental import pallas as pl
from jax.experimental.pallas import tpu as pltpu
from jax.sharding import PartitionSpec as P

STEP = 10

NORM_EPS = 1e-06
BETA = 0.5
ADAM_EPS = 1e-08
DECAY = 0.01
EMA_KEEP = 0.8
CLIP = 1.0

BF = jnp.bfloat16
F32 = jnp.float32
ROWS = 128
KEYS = 256
GROUP = 16
LANES = 128
FLOPS = (60 * 10**9, 10**9)
SIDE = {1: 4, 2: 4, 3: 2, 4: 2}
NT = (((1,), (1,)), ((), ()))
NN = (((1,), (0,)), ((), ()))
TN = (((0,), (0,)), ((), ()))


def dot(left, right, dims=NN):
    return lax.dot_general(left, right, dims, preferred_element_type=F32)


def inverse_rms(values):
    return lax.rsqrt(jnp.mean(values * values, axis=-1, keepdims=True) + NORM_EPS)


def rms_backward(scale_inv, normed, grad_normed):
    return scale_inv * (
        grad_normed - normed * jnp.mean(normed * grad_normed, axis=-1, keepdims=True)
    )


def adamw(weight, first, second, average, grad, rate):
    first_new = BETA * first + (1.0 - BETA) * grad
    second_new = BETA * second + (1.0 - BETA) * grad * grad
    fix = 1.0 - BETA**STEP
    weight_new = weight - rate * (
        first_new / fix / (jnp.sqrt(second_new / fix) + ADAM_EPS) + DECAY * weight
    )
    average_new = EMA_KEEP * average + (1.0 - EMA_KEEP) * weight_new
    return (first_new, second_new, weight_new, average_new)


def swap(value, axis, mask):
    size = lax.axis_size(axis)
    return lax.ppermute(value, axis, [(i, i ^ mask) for i in range(size)])


def digits_of(size):
    found = []
    stride = 1
    while stride < size:
        radix = 2 if stride == 1 or size // stride < 4 else 4
        found.append((stride, radix))
        stride *= radix
    return found


def gather_steps(size):
    steps = []
    while size > 1:
        size //= 2
        steps.append(size)
    return steps


def own_order(shards, axis):
    size = shards.shape[0]
    order = jnp.bitwise_xor(jnp.arange(size, dtype=jnp.int32), lax.axis_index(axis))
    return shards.at[order].get(mode="promise_in_bounds")


def join_pieces(pieces, axis):
    place = {}
    for _, offs in pieces:
        for off in offs:
            place[off] = len(place)
    spots = jnp.array([place[off] for off in range(len(place))], jnp.int32)
    order = jnp.bitwise_xor(jnp.arange(len(place), dtype=jnp.int32), lax.axis_index(axis))
    whole = jnp.concatenate([piece for piece, _ in pieces])
    return whole.at[spots.at[order].get(mode="promise_in_bounds")].get(mode="promise_in_bounds")


def split_blocks(blocks, axis, digits, digit):
    stride, radix = digit
    place = digits.index(digit)
    mine = (lax.axis_index(axis) // stride) % radix
    parts = [
        lax.dynamic_index_in_dim(blocks, jnp.bitwise_xor(mine, k), place, False)
        for k in range(radix)
    ]
    return parts, [d for d in digits if d != digit]


def join_blocks(parts, axis, digit, *first):
    stride, radix = digit
    got = tuple(swap(parts[k], axis, k * stride) for k in range(1, radix))
    if first:
        got = after(got, *first)
    total = parts[0].astype(F32)
    for part in got:
        total = total + part.astype(F32)
    return total


def sum_everywhere(value, axis):
    size = lax.axis_size(axis)
    stride = 1
    while stride < size:
        radix = min(8, size // stride)
        parts = [value] + [swap(value, axis, k * stride) for k in range(1, radix)]
        while len(parts) > 1:
            parts = [parts[i] + parts[i + 1] for i in range(0, len(parts), 2)]
        value = parts[0]
        stride *= radix
    return value


def after(value, *first):
    return lax.optimization_barrier((value,) + first)[0]


def spread_kernel(mixes, pre, post, pre_back, post_back):
    heads = mixes.shape[1]
    tall = heads * GROUP
    wide = (lax.broadcasted_iota(jnp.int32, (tall, heads), 0) // GROUP) == (
        lax.broadcasted_iota(jnp.int32, (tall, heads), 1)
    )
    wide = wide.astype(F32)
    row = lax.broadcasted_iota(jnp.int32, (tall, tall), 0)
    col = lax.broadcasted_iota(jnp.int32, (tall, tall), 1)
    same = row % GROUP == col % GROUP

    def exact(left, right, dims):
        return lax.dot_general(
            left, right, dims, precision=lax.Precision.HIGHEST, preferred_element_type=F32
        )

    for which, (turned, straight) in enumerate(((pre, pre_back), (post, post_back))):
        matrix = mixes[which]
        for out, dims in ((straight, NN), (turned, NT)):
            tallest = exact(wide, matrix, dims)
            full = jnp.where(same, exact(tallest, wide, NT), 0.0)
            high = full.astype(BF)
            out[:tall, :] = high
            out[tall:, :] = (full - high.astype(F32)).astype(BF)


def spread(mixes):
    tall = mixes.shape[1] * GROUP
    return pl.pallas_call(
        spread_kernel,
        out_shape=[jax.ShapeDtypeStruct((2 * tall, tall), BF)] * 4,
        name="spread",
    )(mixes)


def two_heads(rows, first, second):
    return jnp.concatenate([rows * first, rows * second], 0)


def mix(matrix, values):
    out = dot(matrix, values)
    half = matrix.shape[0] // 2
    return out[:half] + out[half:]


def head_masks(scaling):
    lane = lax.broadcasted_iota(jnp.int32, (1, LANES), 1)
    low = lane < LANES // 2
    return low, jnp.where(low, scaling, 0.0).astype(BF), jnp.where(low, 0.0, scaling).astype(BF)


def fill_sequence(meta, sources, qkv, sems):
    copies = []
    for d, source in enumerate(sources):
        start = pl.multiple_of(jnp.bitwise_xor(meta[1], d) * KEYS, KEYS)
        copies.append(pltpu.make_async_copy(source, qkv.at[pl.ds(start, KEYS)], sems.at[d]))
    for copy in copies:
        copy.start()
    for copy in copies:
        copy.wait()


def forward_kernel(meta, *refs):
    sources, (pre, post, attended, probs, weights, qkv, held, sems) = refs[:4], refs[4:]
    heads = probs.shape[0]
    width = attended.shape[1]
    pairs = heads // 2
    tall = heads * GROUP
    step = pl.program_id(0)
    pl.when(step == 0)(partial(fill_sequence, meta, sources, qkv, sems))
    length = meta[0]
    row0 = pl.multiple_of(step * KEYS + meta[2] * ROWS, ROWS)
    chunks = (jnp.minimum(row0 + ROWS, length) + KEYS - 1) // KEYS
    low, first_s, second_s = head_masks(1.0 / math.sqrt(width // heads))

    def score(kc, carry):
        k0 = pl.multiple_of(kc * KEYS, KEYS)
        for p in range(pairs):
            at = p * LANES
            queries = two_heads(qkv[pl.ds(row0, ROWS), at : at + LANES], first_s, second_s)
            keys = qkv[pl.ds(k0, KEYS), width + at : width + at + LANES]
            scores = dot(queries, keys, NT).astype(BF)
            weights[2 * p : 2 * p + 2, :, pl.ds(k0, KEYS)] = scores.reshape(2, ROWS, KEYS)
        return carry

    lax.fori_loop(0, chunks, score, 0)

    def group(n, batch, carry):
        side = SIDE[n]
        rows = [
            pl.ds(pl.multiple_of((batch * side + u) * GROUP, GROUP), GROUP) for u in range(side)
        ]
        col_at = lax.broadcasted_iota(jnp.int32, (GROUP, KEYS), 1)
        row_at = lax.broadcasted_iota(jnp.int32, (GROUP, KEYS), 0)
        peak = [None] * side
        total = [None] * side
        for kc in range(n):
            cols = slice(kc * KEYS, (kc + 1) * KEYS)
            for u in range(side):
                mixed = mix(pre[...], weights[:, rows[u], cols].reshape(tall, KEYS))
                key_pos = col_at + kc * KEYS
                query_pos = row0 + (batch * side + u) * GROUP + row_at
                allowed = (key_pos <= query_pos) & (key_pos < length)
                mixed = jnp.where(allowed[None], mixed.reshape(heads, GROUP, KEYS), -1e30)
                mixed = mixed.reshape(tall, KEYS)
                held[u, :, cols] = mixed
                part = jnp.maximum(mixed[:, :LANES], mixed[:, LANES:])
                peak[u] = part if kc == 0 else jnp.maximum(peak[u], part)
        top = [jnp.max(peak[u], axis=1, keepdims=True) for u in range(side)]
        for kc in range(n):
            cols = slice(kc * KEYS, (kc + 1) * KEYS)
            for u in range(side):
                shifted = jnp.exp(held[u, :, cols] - top[u])
                held[u, :, cols] = shifted
                part = shifted[:, :LANES] + shifted[:, LANES:]
                total[u] = part if kc == 0 else total[u] + part
        inverse = [1.0 / jnp.sum(total[u], axis=1, keepdims=True) for u in range(side)]
        for kc in range(n):
            cols = slice(kc * KEYS, (kc + 1) * KEYS)
            for u in range(side):
                low_probs = (held[u, :, cols] * inverse[u]).astype(BF)
                probs[:, rows[u], cols] = low_probs.reshape(heads, GROUP, KEYS)
                mixed = mix(post[...], low_probs).astype(BF)
                weights[:, rows[u], cols] = mixed.reshape(heads, GROUP, KEYS)
        return carry

    def rest(n):
        lax.fori_loop(0, ROWS // GROUP // SIDE[n], partial(group, n), 0)
        for p in range(pairs):
            at = p * LANES
            pair = weights[2 * p : 2 * p + 2, :, : n * KEYS].reshape(2 * ROWS, n * KEYS)
            out = dot(pair, qkv[: n * KEYS, 2 * width + at : 2 * width + at + LANES])
            attended[:, at : at + LANES] = jnp.where(low, out[:ROWS], out[ROWS:]).astype(BF)

    for n in range(1, probs.shape[2] // KEYS + 1):
        pl.when(chunks == n)(partial(rest, n))


def backward_kernel(meta, *refs):
    sources, refs = refs[:4], refs[4:]
    grad_rows, pre, post, probs, weights, stay, away, grad_pre, grad_post = refs[:9]
    qkv, scores, grads, held, grad_qkv, sum_pre, sum_post, sems = refs[9:]
    heads = probs.shape[0]
    width = grad_rows.shape[1]
    pairs = heads // 2
    tall = heads * GROUP
    step = pl.program_id(0)
    me = meta[1]

    @pl.when(step == 0)
    def _():
        grad_qkv[...] = jnp.zeros_like(grad_qkv)
        sum_pre[...] = jnp.zeros_like(sum_pre)
        sum_post[...] = jnp.zeros_like(sum_post)
        fill_sequence(meta, sources, qkv, sems)

    length = meta[0]
    row0 = pl.multiple_of(step * KEYS + meta[2] * ROWS, ROWS)
    chunks = (jnp.minimum(row0 + ROWS, length) + KEYS - 1) // KEYS
    chunks = jnp.where(row0 < length, chunks, 0)
    scaling = 1.0 / math.sqrt(width // heads)
    low, first_s, second_s = head_masks(scaling)
    low, first_one, second_one = head_masks(1.0)
    lanes = pl.ds(pl.multiple_of(meta[2] * ROWS, ROWS), ROWS)

    def slot_of(home):
        d = jnp.bitwise_xor(me, home)
        return 2 * jnp.bitwise_and(d, 1) + d // 2


    def score(kc, carry):
        k0 = pl.multiple_of(kc * KEYS, KEYS)
        for p in range(pairs):
            at = p * LANES
            queries = two_heads(qkv[pl.ds(row0, ROWS), at : at + LANES], first_s, second_s)
            grad = two_heads(grad_rows[:, at : at + LANES], first_one, second_one)
            keys = qkv[pl.ds(k0, KEYS), width + at : width + at + LANES]
            values = qkv[pl.ds(k0, KEYS), 2 * width + at : 2 * width + at + LANES]
            both = slice(2 * p, 2 * p + 2)
            cols = pl.ds(k0, KEYS)
            scores[both, :, cols] = dot(queries, keys, NT).astype(BF).reshape(2, ROWS, KEYS)
            grads[both, :, cols] = dot(grad, values, NT).astype(BF).reshape(2, ROWS, KEYS)
        return carry

    lax.fori_loop(0, chunks, score, 0)

    def group(n, batch, carry):
        side = SIDE[n]
        rows = [
            pl.ds(pl.multiple_of((batch * side + u) * GROUP, GROUP), GROUP) for u in range(side)
        ]
        span = slice(0, n * KEYS)
        total = [None] * side
        for kc in range(n):
            cols = slice(kc * KEYS, (kc + 1) * KEYS)
            for u in range(side):
                grad_probs = mix(post[...], grads[:, rows[u], cols].reshape(tall, KEYS))
                held[u, :, cols] = grad_probs
                term = probs[:, rows[u], cols].reshape(tall, KEYS).astype(F32) * grad_probs
                part = term[:, :LANES] + term[:, LANES:]
                total[u] = part if kc == 0 else total[u] + part
        added = None
        for u in range(side):
            left = probs[:, rows[u], span].reshape(tall, n * KEYS)
            term = dot(left, grads[:, rows[u], span].reshape(tall, n * KEYS), NT)
            added = term if u == 0 else added + term
        sum_post[...] += added
        delta = [jnp.sum(total[u], axis=1, keepdims=True) for u in range(side)]
        mixed = [[] for _ in range(side)]
        for kc in range(n):
            cols = slice(kc * KEYS, (kc + 1) * KEYS)
            for u in range(side):
                prob = probs[:, rows[u], cols].reshape(tall, KEYS).astype(F32)
                grad_mixed = (prob * (held[u, :, cols] - delta[u])).astype(BF)
                mixed[u].append(grad_mixed)
                back = mix(pre[...], grad_mixed).astype(BF)
                grads[:, rows[u], cols] = back.reshape(heads, GROUP, KEYS)
        added = None
        for u in range(side):
            left = scores[:, rows[u], span].reshape(tall, n * KEYS)
            term = dot(left, jnp.concatenate(mixed[u], 1), NT)
            added = term if u == 0 else added + term
        sum_pre[...] += added
        return carry

    def rest(n):
        lax.fori_loop(0, ROWS // GROUP // SIDE[n], partial(group, n), 0)
        for p in range(pairs):
            at = p * LANES
            mine = slice(at, at + LANES)
            both = slice(2 * p, 2 * p + 2)
            queries = two_heads(qkv[pl.ds(row0, ROWS), mine], first_s, second_s).T
            grad = two_heads(grad_rows[:, mine], first_one, second_one).T
            back = grads[both, :, : n * KEYS].reshape(2 * ROWS, n * KEYS)
            out = dot(back, qkv[: n * KEYS, width + at : width + at + LANES])
            out = jnp.where(low, out[:ROWS], out[ROWS:]) * scaling
            grad_qkv[slot_of(step), mine, lanes] = out.T
            for kc in range(n):
                cols = slice(kc * KEYS, (kc + 1) * KEYS)
                to = slot_of(kc)
                grad_qkv[to, width + at : width + at + LANES, :] += dot(
                    queries, grads[both, :, cols].reshape(2 * ROWS, KEYS)
                )
                grad_qkv[to, 2 * width + at : 2 * width + at + LANES, :] += dot(
                    grad, weights[both, :, cols].reshape(2 * ROWS, KEYS)
                )

    for n in range(1, probs.shape[2] // KEYS + 1):
        pl.when(chunks == n)(partial(rest, n))

    @pl.when(step == pl.num_programs(0) - 1)
    def _():
        stay[...] = grad_qkv[:2]
        away[...] = grad_qkv[2:].astype(BF)
        row = lax.broadcasted_iota(jnp.int32, (tall, tall), 0)
        col = lax.broadcasted_iota(jnp.int32, (tall, tall), 1)
        same = row % GROUP == col % GROUP
        pick = (
            lax.broadcasted_iota(jnp.int32, (tall, LANES), 0) // GROUP
            == lax.broadcasted_iota(jnp.int32, (tall, LANES), 1)
        ).astype(F32)
        for source, out in ((sum_pre, grad_pre), (sum_post, grad_post)):
            kept = jnp.where(same, source[...], 0.0)
            wide = lax.dot_general(
                kept, pick, NN, precision=lax.Precision.HIGHEST, preferred_element_type=F32
            )
            for head in range(heads):
                out[head : head + 1, :] = jnp.sum(
                    wide[head * GROUP : (head + 1) * GROUP], axis=0, keepdims=True
                )


ANY = pl.BlockSpec(memory_space=pl.ANY)


def is_live(step, meta):
    return step * KEYS + meta[2] * ROWS < meta[0]


def attend(meta, sources, pre, post, heads, flops):
    width = sources[0].shape[1] // 3
    tall = heads * GROUP
    steps = 4
    full_len = steps * KEYS
    matrix = pl.BlockSpec((2 * tall, tall), lambda i, m: (0, 0), pipeline_mode=pl.Buffered(1))
    wide = pl.BlockSpec(
        (None, heads, ROWS, full_len), lambda i, m: (jnp.where(is_live(i, m), i, steps), 0, 0, 0)
    )
    kept = jax.ShapeDtypeStruct((steps + 1, heads, ROWS, full_len), BF)
    return pl.pallas_call(
        forward_kernel,
        grid_spec=pltpu.PrefetchScalarGridSpec(
            num_scalar_prefetch=1,
            grid=(steps,),
            in_specs=[ANY] * 4 + [matrix, matrix],
            out_specs=[
                pl.BlockSpec((None, ROWS, width), lambda i, m: (jnp.bitwise_xor(i, m[1]), 0, 0)),
                wide,
                wide,
            ],
            scratch_shapes=[
                pltpu.VMEM((full_len, 3 * width), BF),
                pltpu.VMEM((4, tall, full_len), F32),
                pltpu.SemaphoreType.DMA((4,)),
            ],
        ),
        out_shape=[jax.ShapeDtypeStruct((steps, ROWS, width), BF), kept, kept],
        compiler_params=pltpu.CompilerParams(vmem_limit_bytes=56 * 2**20),
        cost_estimate=pl.CostEstimate(
            flops=flops, bytes_accessed=2**20, transcendentals=0
        ),
        name="attend",
    )(meta, *sources, pre, post)


def attend_back(meta, sources, grad_rows, pre, post, probs, weights, flops):
    width = sources[0].shape[1] // 3
    steps = 4
    heads = probs.shape[1]
    tall = heads * GROUP
    full_len = steps * KEYS

    def newest(step, meta):
        last = 0
        for other in range(1, steps):
            last = jnp.where(is_live(other, meta), other, last)
        return jnp.minimum(step, last)

    matrix = pl.BlockSpec((2 * tall, tall), lambda i, m: (0, 0), pipeline_mode=pl.Buffered(1))
    wide = pl.BlockSpec((None, heads, ROWS, full_len), lambda i, m: (newest(i, m), 0, 0, 0))
    rows = pl.BlockSpec((None, ROWS, width), lambda i, m: (jnp.bitwise_xor(i, m[1]), 0, 0))
    small = pl.BlockSpec((heads, LANES), lambda i, m: (0, 0))
    pairs = pl.BlockSpec(
        (2, 3 * width, KEYS), lambda i, m: (0, 0, 0), pipeline_mode=pl.Buffered(1)
    )
    return pl.pallas_call(
        backward_kernel,
        grid_spec=pltpu.PrefetchScalarGridSpec(
            num_scalar_prefetch=1,
            grid=(steps,),
            in_specs=[ANY] * 4 + [rows, matrix, matrix, wide, wide],
            out_specs=[
                pairs,
                pairs,
                small,
                small,
            ],
            scratch_shapes=[
                pltpu.VMEM((full_len, 3 * width), BF),
                pltpu.VMEM((heads, ROWS, full_len), BF),
                pltpu.VMEM((heads, ROWS, full_len), BF),
                pltpu.VMEM((4, tall, full_len), F32),
                pltpu.VMEM((4, 3 * width, KEYS), F32),
                pltpu.VMEM((tall, tall), F32),
                pltpu.VMEM((tall, tall), F32),
                pltpu.SemaphoreType.DMA((4,)),
            ],
        ),
        out_shape=[
            jax.ShapeDtypeStruct((2, 3 * width, KEYS), F32),
            jax.ShapeDtypeStruct((2, 3 * width, KEYS), BF),
            jax.ShapeDtypeStruct((heads, LANES), F32),
            jax.ShapeDtypeStruct((heads, LANES), F32),
        ],
        compiler_params=pltpu.CompilerParams(vmem_limit_bytes=60 * 2**20),
        cost_estimate=pl.CostEstimate(
            flops=flops, bytes_accessed=2**20, transcendentals=0
        ),
        name="attend_back",
    )(meta, *sources, grad_rows, pre, post, probs, weights)


def gelu_both(value):
    scale = math.sqrt(2.0 / math.pi)
    square = value * value
    bent = jnp.tanh(scale * (value + 0.044715 * (square * value)))
    share = 0.5 * (1.0 + bent)
    slope = share + 0.5 * value * (1.0 - bent * bent) * (
        scale * (1.0 + 3.0 * 0.044715 * square)
    )
    return value * share, slope


def fill_weights(meta, sources, offs, inner, outer, proj, sems):
    hidden = inner.shape[1] // 2
    width = proj.shape[0]
    half = width // 2
    copies = []

    def copy(source, target):
        copies.append(pltpu.make_async_copy(source, target, sems.at[len(copies)]))

    count = len(sources) // 2
    for side in range(2):
        lanes = jnp.bitwise_xor(meta[1], side) * half
        to_proj = pl.ds(pl.multiple_of(lanes, LANES), half)
        to_inner = slice(side * hidden, (side + 1) * hidden)
        here = sources[count * side : count * side + count]
        if offs is None:
            copy(here[0], inner.at[:, to_inner])
            copy(here[1], proj.at[:, to_proj])
            copy(here[2], outer.at[to_inner])
            continue
        own_rows = here[0].shape[1]
        folds = hidden * own_rows // width // own_rows
        for source, owners in zip(here, offs):
            for at_source, off in enumerate(owners):
                block = source.at[at_source]
                owner = jnp.bitwise_xor(meta[0], off)
                rows = pl.ds(pl.multiple_of(owner * own_rows, own_rows), own_rows)
                copy(block.at[:, :hidden], inner.at[rows, to_inner])
                copy(block.at[:, hidden : hidden + half], proj.at[rows, to_proj])
                for fold in range(folds):
                    start = side * hidden + (owner * folds + fold) * own_rows
                    at = hidden + half + fold * width
                    copy(
                        block.at[:, at : at + width],
                        outer.at[pl.ds(pl.multiple_of(start, own_rows), own_rows)],
                    )
    for one in copies:
        one.start()
    for one in copies:
        one.wait()


TILE = 256
CHUNK = 512


def feed_kernel(offs, meta, gains, tokens, attended, grad_out, *refs):
    count = len(refs) - 17
    sources, refs = refs[:count], refs[count:]
    output, grad_resid, resid_low, grad_attended, gain_two, second_in = refs[:6]
    active, grad_hidden = refs[6:8], refs[8:10]
    inner, outer, proj, resid, out_sum, grad_sum, sems = refs[10:]
    rows = tokens.shape[0]
    step = pl.program_id(0)
    tiles = [slice(at, at + TILE) for at in range(0, rows, TILE)]

    @pl.when(step == 0)
    def _():
        fill_weights(meta, sources, offs, inner, outer, proj, sems)
        for tile in tiles:
            value = tokens[tile].astype(F32) + dot(attended[tile], proj[...])
            resid[tile] = value
            out_sum[tile] = value
            grad_sum[tile] = jnp.zeros_like(value)
            second_in[tile] = (value * inverse_rms(value) * gains[1:2]).astype(BF)

    cols = pl.ds(pl.multiple_of(step * CHUNK, CHUNK), CHUNK)
    for tile in tiles:
        up = inner[:, cols]
        down = outer[cols]
        value, slope = gelu_both(dot(second_in[tile], up))
        value = value.astype(BF)
        back = (dot(grad_out[tile], down, NT) * slope).astype(BF)
        for side in range(2):

            @pl.when((step * 2 >= pl.num_programs(0)) == (side == 1))
            def _():
                active[side][tile] = value
                grad_hidden[side][tile] = back

        out_sum[tile] += dot(value, down)
        grad_sum[tile] += dot(back, up, NT)

    @pl.when(step == pl.num_programs(0) - 1)
    def _():
        gain_sum = jnp.zeros((8, proj.shape[0]), F32)
        for tile in tiles:
            output[tile] = out_sum[tile].astype(BF)
            value = resid[tile]
            scale = inverse_rms(value)
            normed = value * scale
            grad = grad_sum[tile]
            gain_sum += jnp.sum((grad * normed).reshape(TILE // 8, 8, -1), axis=0)
            back = grad_out[tile].astype(F32) + rms_backward(scale, normed, grad * gains[1:2])
            grad_resid[tile] = back
            back = back.astype(BF)
            resid_low[tile] = back
            grad_attended[tile] = dot(back, proj[...], NT).astype(BF)
        gain_two[...] = gain_sum


def feed_forward(meta, gains, tokens, attended, grad_out, sources, offs, hidden):
    rows, width = tokens.shape
    copies = 6
    if offs is not None:
        owners = sum(len(o) for o in offs)
        copies = 2 * owners * (2 + hidden // 2 // width)
    chunks = hidden // CHUNK

    def whole(shape):
        return pl.BlockSpec(shape, lambda c, m: (0,) * len(shape), pipeline_mode=pl.Buffered(1))

    flat = whole((rows, width))
    first = pl.BlockSpec((rows, CHUNK), lambda c, m: (0, jnp.minimum(c, chunks // 2 - 1)))
    second = pl.BlockSpec((rows, CHUNK), lambda c, m: (0, jnp.maximum(c - chunks // 2, 0)))
    wide = jax.ShapeDtypeStruct((rows, hidden // 2), BF)
    return pl.pallas_call(
        partial(feed_kernel, offs),
        grid_spec=pltpu.PrefetchScalarGridSpec(
            num_scalar_prefetch=1,
            grid=(chunks,),
            in_specs=[whole((2, width)), flat, flat, flat] + [ANY] * len(sources),
            out_specs=[flat, flat, flat, flat, whole((8, width)), flat, first, second, first, second],
            scratch_shapes=[
                pltpu.VMEM((width, hidden), BF),
                pltpu.VMEM((hidden, width), BF),
                pltpu.VMEM((width, width), BF),
                pltpu.VMEM((rows, width), F32),
                pltpu.VMEM((rows, width), F32),
                pltpu.VMEM((rows, width), F32),
                pltpu.SemaphoreType.DMA((copies,)),
            ],
        ),
        out_shape=[
            jax.ShapeDtypeStruct((rows, width), BF),
            jax.ShapeDtypeStruct((rows, width), F32),
            jax.ShapeDtypeStruct((rows, width), BF),
            jax.ShapeDtypeStruct((rows, width), BF),
            jax.ShapeDtypeStruct((8, width), F32),
            jax.ShapeDtypeStruct((rows, width), BF),
            wide,
            wide,
            wide,
            wide,
        ],
        compiler_params=pltpu.CompilerParams(vmem_limit_bytes=56 * 2**20),
        cost_estimate=pl.CostEstimate(
            flops=22 * 10**9, bytes_accessed=40 * 10**6, transcendentals=0
        ),
        name="feed_forward",
    )(meta, gains, tokens, attended, grad_out, *sources)


def weight_kernel(meta, second_in, attended, resid_low, grad_out, active, back, first, last, turned):
    width = second_in.shape[1]
    hidden = active.shape[1]
    half = width // 2
    turned[...] = second_in[...].T
    lanes = pl.ds(pl.multiple_of(meta[0] * half, LANES), half)
    first[:, hidden:] = dot(attended[...], resid_low[:, lanes], TN).astype(first.dtype)
    for at in range(0, hidden, CHUNK):
        cols = slice(at, at + CHUNK)
        first[:, cols] = dot(turned[...], back[:, cols]).astype(first.dtype)
        last[cols] = dot(active[:, cols], grad_out[...], TN).astype(last.dtype)


def weight_sums(which, second_in, attended, resid_low, grad_out, active, back, kind):
    rows, width = second_in.shape
    hidden = active.shape[1]
    vmem = pl.BlockSpec(memory_space=pltpu.VMEM)
    return pl.pallas_call(
        weight_kernel,
        in_specs=[pl.BlockSpec(memory_space=pltpu.SMEM)] + [vmem] * 6,
        out_specs=[vmem, vmem],
        scratch_shapes=[pltpu.VMEM((width, rows), BF)],
        out_shape=[
            jax.ShapeDtypeStruct((width, hidden + width // 2), kind),
            jax.ShapeDtypeStruct((hidden, width), kind),
        ],
        compiler_params=pltpu.CompilerParams(vmem_limit_bytes=56 * 2**20),
        cost_estimate=pl.CostEstimate(
            flops=6 * 10**9, bytes_accessed=20 * 10**6, transcendentals=0
        ),
        name="weight_sums",
    )(which, second_in, attended, resid_low, grad_out, active, back)


def first_kernel(offs, meta, tokens, *refs):
    count = 2 * (1 if offs is None else len(offs))
    sources, refs = refs[:count], refs[count:]
    out, first_in, gains, refs = refs[0], refs[1], refs[2], refs[3:]
    weight, mixed, sems = refs
    side = weight.shape[1] // 2
    copies = []

    def copy(source, target):
        copies.append(pltpu.make_async_copy(source, target, sems.at[len(copies)]))

    for which in range(2):
        here = sources[which * (count // 2) : (which + 1) * (count // 2)]
        start = pl.multiple_of(jnp.bitwise_xor(meta[1], which) * side, side)
        if offs is None:
            copy(here[0].at[:, :side], weight.at[:, pl.ds(start, side)])
            if which == 0:
                copy(here[0].at[:, side:], mixed)
            continue
        own_rows = here[0].shape[1]
        for source, owners in zip(here, offs):
            for at, off in enumerate(owners):
                owner = jnp.bitwise_xor(meta[0], off)
                rows = pl.ds(pl.multiple_of(owner * own_rows, own_rows), own_rows)
                copy(source.at[at, :, :side], weight.at[rows, pl.ds(start, side)])
                if which == 0:
                    copy(source.at[at, :, side:], mixed.at[rows])
    for one in copies:
        one.start()
    for one in copies:
        one.wait()
    gain = mixed[...].astype(F32).T[:8]
    gains[...] = gain
    for at in range(0, tokens.shape[0], KEYS):
        value = tokens[at : at + KEYS].astype(F32)
        low = (value * inverse_rms(value) * gain[:1]).astype(BF)
        first_in[at : at + KEYS] = low
        for col in range(0, 2 * side, width_of(side)):
            cols = slice(col, col + width_of(side))
            out[at : at + KEYS, cols] = dot(low, weight[:, cols]).astype(BF)


def width_of(side):
    return 2 * side // 3


def first_product(meta, tokens, pieces, offs, with_weight):
    rows, width = tokens.shape
    vmem = pl.BlockSpec(memory_space=pltpu.VMEM)
    out_shape = [
        jax.ShapeDtypeStruct((rows, 3 * width), BF),
        jax.ShapeDtypeStruct((rows, width), BF),
        jax.ShapeDtypeStruct((8, width), F32),
    ]
    scratch = [
        pltpu.VMEM((width, LANES), BF),
        pltpu.SemaphoreType.DMA((3 if offs is None else 3 * sum(len(o) for o in offs),)),
    ]
    if with_weight:
        out_shape.append(jax.ShapeDtypeStruct((width, 3 * width), BF))
    else:
        scratch = [pltpu.VMEM((width, 3 * width), BF)] + scratch
    return pl.pallas_call(
        partial(first_kernel, offs),
        in_specs=[pl.BlockSpec(memory_space=pltpu.SMEM), vmem] + [ANY] * len(pieces),
        out_specs=[vmem] * len(out_shape),
        out_shape=out_shape,
        scratch_shapes=scratch,
        compiler_params=pltpu.CompilerParams(vmem_limit_bytes=40 * 2**20),
        cost_estimate=pl.CostEstimate(
            flops=4 * 10**9, bytes_accessed=5 * 2**20, transcendentals=0
        ),
        name="first_product",
    )(meta, tokens, *pieces)


def first_grads_kernel(meta, first_in, *refs):
    cols, (out,) = refs[:-1], refs[-1:]
    side = out.shape[1]
    take = pl.ds(pl.multiple_of(meta[0] * side, side), side)
    total = None
    for block, grads in enumerate(cols):
        rows = first_in[block * KEYS : (block + 1) * KEYS].T
        term = dot(rows, grads[take], NT)
        total = term if block == 0 else total + term
        if block + 1 < len(cols):
            continue
        out[...] = total.astype(out.dtype)


def first_grads(which, first_in, cols, kind):
    width = first_in.shape[1]
    side = cols[0].shape[0] // 2
    vmem = pl.BlockSpec(memory_space=pltpu.VMEM)
    return pl.pallas_call(
        first_grads_kernel,
        in_specs=[pl.BlockSpec(memory_space=pltpu.SMEM)] + [vmem] * (1 + len(cols)),
        out_specs=vmem,
        out_shape=jax.ShapeDtypeStruct((width, side), kind),
        compiler_params=pltpu.CompilerParams(vmem_limit_bytes=50 * 2**20),
        cost_estimate=pl.CostEstimate(
            flops=3 * 10**9, bytes_accessed=5 * 2**20, transcendentals=0
        ),
        name="first_grads",
    )(which, first_in, *cols)


def token_grads_kernel(meta, gains, near, far, weight, tokens, grad_resid, *refs):
    out, gain_out = refs[-2:]
    step = pl.program_id(0)

    @pl.when(step == 0)
    def _():
        gain_out[...] = jnp.zeros_like(gain_out)

    for which, grads in enumerate((near, far)):

        @pl.when(step == which)
        def _():
            back = dot(weight[...], grads[...]).T
            value = tokens[...].astype(F32)
            scale = inverse_rms(value)
            normed = value * scale
            gain_out[...] += jnp.sum((back * normed).reshape(KEYS // 8, 8, -1), axis=0)
            out[...] = grad_resid[...] + rms_backward(scale, normed, back * gains[:1])


def token_grads(slot, seqs, gains, near, far, weight, tokens, grad_resid, before):
    _, rows, width = tokens.shape

    def whole(shape):
        return pl.BlockSpec(shape, lambda i, m: (0,) * len(shape), pipeline_mode=pl.Buffered(1))

    place = pl.BlockSpec((None, rows, width), lambda i, m: (m[i], 0, 0))
    extra = [] if before is None else [before]
    return pl.pallas_call(
        token_grads_kernel,
        grid_spec=pltpu.PrefetchScalarGridSpec(
            num_scalar_prefetch=1,
            grid=(2,),
            in_specs=[
                whole(gains.shape),
                whole(near.shape),
                whole(far.shape),
                whole(weight.shape),
                place,
                pl.BlockSpec((None, rows, width), lambda i, m: (2 * slot + i, 0, 0)),
            ]
            + [ANY] * len(extra),
            out_specs=[place, whole((8, width))],
        ),
        out_shape=[
            jax.ShapeDtypeStruct(tokens.shape, F32),
            jax.ShapeDtypeStruct((8, width), F32),
        ],
        input_output_aliases={7: 0} if extra else {},
        compiler_params=pltpu.CompilerParams(vmem_limit_bytes=50 * 2**20),
        cost_estimate=pl.CostEstimate(
            flops=4 * 10**9, bytes_accessed=5 * 2**20, transcendentals=0
        ),
        name="token_grads",
    )(seqs, gains, near, far, weight, tokens, grad_resid, *extra)


def on_device(
    tokens,
    cotangent,
    lengths,
    qkv_weight,
    qkv_first,
    qkv_second,
    qkv_average,
    proj_weight,
    proj_first,
    proj_second,
    proj_average,
    inner_weight,
    inner_first,
    inner_second,
    inner_average,
    outer_weight,
    outer_first,
    outer_second,
    outer_average,
    gains,
    gain_first,
    gain_second,
    gain_average,
    mixes,
    mix_first,
    mix_second,
    mix_average,
):
    group_seqs, shard_len, width = tokens.shape
    owners = lax.axis_size("dp")
    heads = mixes.shape[1]
    own_rows = qkv_weight.shape[0]
    hidden = inner_weight.shape[1]
    half = width // 2
    slice_ff = hidden // owners // 2
    me = lax.axis_index("seq")
    pair = me // 2
    core = jnp.bitwise_and(me, 1)

    def by_core(mine, other, axis):
        return jnp.where(
            core == 0,
            jnp.concatenate([mine, other], axis),
            jnp.concatenate([other, mine], axis),
        )

    ahead = (lengths[None, :] > lengths[:, None]) | (
        (lengths[None, :] == lengths[:, None])
        & (jnp.arange(group_seqs)[None, :] < jnp.arange(group_seqs)[:, None])
    )
    rank = jnp.sum(ahead.astype(jnp.int32), axis=1)
    order = jnp.sum(
        jnp.where(
            rank[None, :] == jnp.arange(group_seqs)[:, None], jnp.arange(group_seqs)[None, :], 0
        ),
        axis=1,
    ).astype(jnp.int32)

    def sequence_of(slot, which):
        return order[which if slot == 0 else group_seqs - 1 - which]

    def arrange(value):
        return jnp.stack(
            [
                jnp.stack(
                    [
                        lax.dynamic_index_in_dim(
                            value, sequence_of(slot, jnp.bitwise_xor(pair, d)), 0, False
                        )
                        for d in range(2)
                    ]
                )
                for slot in range(2)
            ]
        )

    def restore(value):
        flat = value.reshape((4,) + value.shape[2:])
        which = jnp.where(rank < 2, rank, 3 - rank)
        place = 2 * (rank // 2) + jnp.bitwise_xor(which, pair)
        return flat.at[place].get(mode="promise_in_bounds")

    lengths_here = arrange(lengths)
    metas = [jnp.stack([lengths_here[slot, 0], me, core]).astype(jnp.int32) for slot in range(2)]

    low_rows = arrange(tokens)
    pre_mix, post_mix, pre_back, post_back = spread(mixes)
    positions = me * shard_len + jnp.arange(shard_len, dtype=jnp.int32)
    live = positions[None, None, :] < lengths_here[:, :, None]
    cot = arrange(cotangent)
    grad_out = jnp.where(live[..., None], cot, jnp.zeros_like(cot))
    side = qkv_weight.shape[1] // 2
    mine = lax.dynamic_slice_in_dim(qkv_weight.astype(BF), core * side, side, 1)
    mine = jnp.concatenate([mine, jnp.pad(gains.astype(BF).T, ((0, 0), (0, LANES - 2)))], 1)
    offs = None
    if owners == 8:
        shard = mine[None]
        got = swap(shard, "dp", 4)
        got, early = lax.optimization_barrier((got, (low_rows, pre_mix, grad_out)))
        pieces = [jnp.concatenate([shard, got])]
        far_z, far_x = swap(pieces[0], "dp", 2), swap(pieces[0], "dp", 1)
        beside = [swap(pieces[0], "seq", 1)]
        pieces += [far_z, far_x]
        pieces.append(swap(far_z, "dp", 1))
        beside += [swap(p, "seq", 1) for p in pieces[1:]]
        offs = ((0, 4), (2, 6), (1, 5), (3, 7))
        pieces += beside
        late = pieces[3]
    else:
        mine = lax.all_gather(mine, "dp", axis=0, tiled=True)
        pieces = [mine, swap(mine, "seq", 1)]
        early = late = mine

    folds = slice_ff // own_rows
    inner_mine = inner_weight.astype(BF).reshape(own_rows, owners, 2, slice_ff)
    inner_mine = lax.dynamic_index_in_dim(inner_mine, core, 2, False)
    outer_mine = outer_weight.astype(BF).reshape(2, folds, own_rows, width)
    outer_mine = lax.dynamic_index_in_dim(outer_mine, core, 0, False)
    rest = jnp.concatenate(
        [
            inner_mine.reshape(own_rows, owners * slice_ff),
            lax.dynamic_slice_in_dim(proj_weight.astype(BF), core * half, half, 1),
        ]
        + [outer_mine[f] for f in range(folds)],
        axis=1,
    )[None]
    if offs is not None:
        got = swap(after(rest, early), "dp", 4)
        got, late = lax.optimization_barrier((got, late))
    place = jnp.stack([lax.axis_index("dp"), core]).astype(jnp.int32)
    out, *_ = first_product(place, low_rows[0, 1], pieces, offs, False)
    far = [out]
    if offs is not None:
        got = after(got, far[0])
        rest_pieces = [jnp.concatenate([rest, got])]
        far_z, far_x = swap(rest_pieces[0], "dp", 2), swap(rest_pieces[0], "dp", 1)
    here = swap(far[0], "seq", 2)
    out, first_in, gain_vals, weight_qkv = first_product(
        after(place, far[0]), low_rows.reshape(-1, width), pieces, offs, True
    )
    out = out.reshape(4, shard_len, 3 * width)
    near = [out[0], out[2]]
    far.append(out[3])
    beside = swap(near[0], "seq", 1)
    if offs is None:
        here, beside = lax.optimization_barrier((here, beside, far[1], near[1]))[:2]
    else:
        here, beside, far_z, far_x = lax.optimization_barrier(
            (here, beside, far_z, far_x, far[1], near[1])
        )[:4]
        rest_pieces += [far_z, far_x]
        far_x = swap(far_z, "dp", 1)
    sources = [[near[0], beside, here, swap(here, "seq", 1)]]
    next_far = swap(after(far[1], here), "seq", 2)
    beside = swap(after(near[1], here), "seq", 1)
    def by_half(rows):
        return jnp.where(core == 0, rows, rows[:, ::-1])

    rows, probs, weights = [None, None], [None, None], [None, None]
    meta = after(metas[0], sources[0], rest)
    if offs is not None:
        beside_rest = [swap(p, "seq", 1) for p in rest_pieces]
    rows[0], probs[0], weights[0] = attend(meta, sources[0], pre_mix, post_mix, heads, FLOPS[0])
    next_far, beside = lax.optimization_barrier((next_far, beside, rows[0]))[:2]
    if offs is not None:
        rest_pieces.append(after(far_x, rows[0]))
        beside_rest.append(swap(rest_pieces[3], "seq", 1))
    sources.append([near[1], beside, next_far, swap(next_far, "seq", 1)])
    far_rows = swap(rows[0][2:], "seq", 2)
    rows[1], probs[1], weights[1] = attend(
        metas[1], sources[1], pre_mix, post_mix, heads, FLOPS[1]
    )
    far_rows = after(far_rows, rows[1])
    cut = owners * slice_ff + half
    if offs is not None:
        beside_rest = after(beside_rest, rows[1])
        feed_weights = rest_pieces + list(beside_rest)
    else:
        rest = lax.all_gather(rest[0], "dp")
        feed_weights = []
        for part in (rest, swap(rest, "seq", 1)):
            flat = part.reshape(owners * own_rows, -1)
            down = jnp.moveaxis(part[:, :, cut:].reshape(owners, own_rows, folds, width), 2, 1)
            feed_weights += [
                flat[:, : cut - half],
                flat[:, cut - half : cut],
                down.reshape(owners * slice_ff, width),
            ]
    far_rows = jnp.stack([far_rows, swap(rows[1][2:], "seq", 2)])
    near_rows = jnp.stack([rows[0][1], rows[1][1]])
    got = swap(jnp.stack([near_rows, far_rows[:, 1]]), "seq", 1)
    attention_output = jnp.stack(
        [
            by_half(
                jnp.stack(
                    [
                        jnp.stack([rows[slot][0], got[0, slot]]),
                        jnp.stack([far_rows[slot, 0], got[1, slot]]),
                    ]
                )
            ).reshape(2, 2 * ROWS, width)
            for slot in range(2)
        ]
    )

    flat = (-1, width)
    attention_output = attention_output.reshape(flat)
    flat_out = grad_out.reshape(flat)
    output, grad_resid, resid_low, grad_attended, gain_two, second_in, *wide = feed_forward(
        place,
        gain_vals[:2],
        low_rows.reshape(flat),
        attention_output,
        flat_out,
        feed_weights,
        offs,
        hidden,
    )
    grad_attended = grad_attended.reshape(grad_out.shape)
    grad_resid = grad_resid.reshape(4, shard_len, width)

    def sums_of(side, which, kind):
        return weight_sums(
            which[None],
            second_in,
            attention_output,
            resid_low,
            flat_out,
            wide[side],
            wide[2 + side],
            kind,
        )

    output = restore(output.reshape(grad_out.shape))
    gain_two = jnp.sum(gain_two, axis=0)

    sent = sums_of(1, 1 - core, BF)
    arrived = swap(sent[0], "seq", 1), swap(sent[1], "seq", 1)
    meta = after(core, sent)
    mine = sums_of(0, meta, F32)
    arrived = after(arrived, mine, output)
    twos = [(2**k, 2) for k in range(owners.bit_length() - 1)]
    orders = [twos, twos[1:] + twos[:1]]
    chains = []
    for at in range(2):
        total = (mine[at] + arrived[at].astype(F32)).astype(BF)
        total = total.reshape((2,) * len(twos) + (-1, total.shape[1]))
        chains.append(split_blocks(total, "dp", twos[::-1], orders[at][0]))

    def step_on(at, place, parts, *first):
        total = join_blocks(parts[0], "dp", orders[at][place], *first)
        if place + 1 == len(twos):
            return total
        return split_blocks(total.astype(BF), "dp", parts[1], orders[at][place + 1])

    def to_far(slot):
        found = by_half(grad_attended[slot].reshape(2, 2, ROWS, width)).reshape(4, ROWS, width)
        return found, swap(found[2:], "seq", 2)

    def from_near(found, far):
        got = swap(jnp.stack([found[1], far[1]]), "seq", 1)
        return jnp.stack([found[0], got[0], far[0], got[1]])

    def attend_slot(slot, meta, rows):
        return attend_back(
            meta, sources[slot], rows, pre_back, post_back, probs[slot], weights[slot], FLOPS[slot]
        )

    found, far = to_far(0)
    far = after(far, mine)
    next_found, next_far = to_far(1)
    meta = after(metas[0], chains)
    stay, away, back_pre, back_post = attend_slot(0, meta, from_near(found, far))
    grad_mixes = jnp.stack([back_pre[:, :heads], back_post[:, :heads]])
    chains = [step_on(at, 0, chains[at], stay) for at in range(2)]
    away, next_far = lax.optimization_barrier((away, next_far, chains))[:2]
    next_rows = from_near(next_found, next_far)
    summed = (stay + swap(away, "seq", 1).astype(F32)).astype(BF)
    far = swap(summed[1], "seq", 2)
    meta = after(metas[1], summed, chains)
    stay, away, back_pre, back_post = attend_slot(1, meta, next_rows)
    grad_mixes = grad_mixes + jnp.stack([back_pre[:, :heads], back_post[:, :heads]])
    chains = [step_on(at, 1, chains[at], stay) for at in range(2)]
    away, far = lax.optimization_barrier((away, far, chains))[:2]
    grad_cols = [(summed[0], far)]
    summed = (stay + swap(away, "seq", 1).astype(F32)).astype(BF)
    chains = [(after(parts, summed), left) for parts, left in chains]
    far = swap(summed[1], "seq", 2)

    seqs = [jnp.stack([sequence_of(s, pair), sequence_of(s, 1 - pair)]) for s in range(2)]

    def to_tokens(slot, before):
        return token_grads(
            slot,
            seqs[slot].astype(jnp.int32),
            gain_vals,
            *grad_cols[slot],
            weight_qkv,
            tokens,
            grad_resid,
            before,
        )

    begun = to_tokens(0, None)
    for turn in range(2, len(twos)):
        chains = [step_on(at, turn, chains[at], begun) for at in range(2)]
    first_part, second_part = chains
    others = first_part.astype(BF), second_part.astype(BF)
    far, begun, others = lax.optimization_barrier((far, begun, others))
    grad_cols.append((summed[0], far))
    cols = grad_cols[0] + grad_cols[1]
    sent = first_grads((1 - core)[None], first_in, cols, BF)
    others = after(others, sent)
    qkv_mine = first_grads(after(core, sent)[None], first_in, cols, F32)

    def over_pairs(total):
        total = lax.optimization_barrier(jax.tree.map(lambda v: v.astype(BF), total))
        return jax.tree.map(lambda v: v.astype(F32) + swap(v, "seq", 2).astype(F32), total)

    arrived = after(swap(sent, "seq", 1), qkv_mine)
    qkv_total = (qkv_mine + arrived.astype(F32)).astype(BF)
    grad_rows_tokens, gain_more = to_tokens(1, begun[0])
    gain_one = jnp.sum(begun[1] + gain_more, axis=0)
    qkv_total = qkv_total.reshape((2,) * len(twos) + (own_rows, side))
    third = side // LANES // 3 * LANES
    chains = [qkv_total[..., third:], qkv_total[..., :third]]
    chains = [split_blocks(chains[at], "dp", twos[::-1], orders[at][0]) for at in range(2)]
    others = over_pairs(others)
    small = jnp.concatenate([gain_one, gain_two, grad_mixes.reshape(-1)])
    count = small.shape[0]
    small = jnp.pad(small, (0, -(count + 1) % (8 * LANES) + 1)).reshape(-1, LANES)
    chains = [step_on(at, 0, chains[at]) for at in range(2)]

    first_halves = (others[0], swap(others[0], "seq", 1))
    last_halves = (others[1], swap(others[1], "seq", 1))
    red_proj = by_core(*[g[:, cut - half :] for g in first_halves], 1)
    red_inner = by_core(
        *[g[:, : cut - half].reshape(own_rows, owners, 1, slice_ff) for g in first_halves], 2
    ).reshape(own_rows, hidden)
    red_outer = by_core(*last_halves, 0)
    squares = (
        jnp.sum(red_proj * red_proj)
        + jnp.sum(red_inner * red_inner)
        + jnp.sum(red_outer * red_outer)
    )
    small = small + swap(small, "seq", 1)
    small = small + swap(small, "seq", 2)
    pins = [(), (small,)]
    for turn in range(1, len(twos)):
        pin = pins[turn - 1] if turn <= len(pins) else ()
        chains = [step_on(at, turn, chains[at], *pin) for at in range(2)]
    qkv_total = jnp.concatenate(chains[::-1], axis=-1)
    qkv_total = over_pairs(qkv_total)
    red_qkv = by_core(qkv_total, swap(qkv_total, "seq", 1), 1)

    squares = squares + jnp.sum(red_qkv * red_qkv)
    place = lax.broadcasted_iota(jnp.int32, small.shape, 0) * LANES
    place = place + lax.broadcasted_iota(jnp.int32, small.shape, 1)
    small = sum_everywhere(jnp.where(place == count, squares, small), "dp").reshape(-1)
    gain_all = small[: 2 * width].reshape(2, width)
    red_gains = lax.dynamic_slice_in_dim(gain_all, lax.axis_index("dp") * own_rows, own_rows, 1)
    red_mixes = small[2 * width : count].reshape(mixes.shape)
    grad_norm = jnp.sqrt(
        small[count] + jnp.sum(gain_all * gain_all) + jnp.sum(red_mixes * red_mixes)
    )
    factor = CLIP / jnp.maximum(grad_norm, CLIP)
    clipped_gains = red_gains * factor
    qkv_new = adamw(qkv_weight, qkv_first, qkv_second, qkv_average, red_qkv * factor, 0.03)
    proj_new = adamw(proj_weight, proj_first, proj_second, proj_average, red_proj * factor, 0.1)
    inner_new = adamw(
        inner_weight, inner_first, inner_second, inner_average, red_inner * factor, 0.03
    )
    outer_new = adamw(
        outer_weight, outer_first, outer_second, outer_average, red_outer * factor, 0.02
    )
    gain_new = adamw(gains, gain_first, gain_second, gain_average, clipped_gains, 0.3)
    mix_new = adamw(mixes, mix_first, mix_second, mix_average, red_mixes * factor, 0.3)
    return (
        output,
        grad_rows_tokens,
        grad_norm,
        *qkv_new,
        *proj_new,
        *inner_new,
        *outer_new,
        *gain_new,
        *mix_new,
        clipped_gains,
    )


def solution(mesh):
    rows = P("dp", "seq", None)
    matrix = P("dp", None)
    vector = P(None, "dp")
    in_specs = (rows, rows, P("dp")) + (matrix,) * 16 + (vector,) * 4 + (P(),) * 4
    out_specs = (rows, rows, P()) + (matrix,) * 16 + (vector,) * 4 + (P(),) * 4 + (vector,)
    return jax.shard_map(
        on_device, mesh=mesh, in_specs=in_specs, out_specs=out_specs, check_vma=False
    )
```

```python
from functools import partial
import math

import jax
import jax.numpy as jnp
from jax import lax
from jax.experimental import pallas as pl
from jax.experimental.pallas import tpu as pltpu
from jax.sharding import PartitionSpec as P

STEP = 10

NORM_EPS = 1e-06
BETA = 0.5
ADAM_EPS = 1e-08
DECAY = 0.01
EMA_KEEP = 0.8
CLIP = 1.0

BF = jnp.bfloat16
F32 = jnp.float32
ROWS = 128
KEYS = 256
GROUP = 16
LANES = 128
FLOPS = (60 * 10**9, 1)
SIDE = {1: 8, 2: 8, 3: 8, 4: 8}
SIDE_BACK = {1: 4, 2: 4, 3: 2, 4: 2}
NT = (((1,), (1,)), ((), ()))
NN = (((1,), (0,)), ((), ()))
TN = (((0,), (0,)), ((), ()))


def dot(left, right, dims=NN):
    return lax.dot_general(left, right, dims, preferred_element_type=F32)


def inverse_rms(values):
    return lax.rsqrt(jnp.mean(values * values, axis=-1, keepdims=True) + NORM_EPS)


def rms_backward(scale_inv, normed, grad_normed):
    return scale_inv * (
        grad_normed - normed * jnp.mean(normed * grad_normed, axis=-1, keepdims=True)
    )


def adamw(weight, first, second, average, grad, rate):
    first_new = BETA * first + (1.0 - BETA) * grad
    second_new = BETA * second + (1.0 - BETA) * grad * grad
    fix = 1.0 - BETA**STEP
    weight_new = weight - rate * (
        first_new / fix / (jnp.sqrt(second_new / fix) + ADAM_EPS) + DECAY * weight
    )
    average_new = EMA_KEEP * average + (1.0 - EMA_KEEP) * weight_new
    return (first_new, second_new, weight_new, average_new)


def swap(value, axis, mask):
    size = lax.axis_size(axis)
    return lax.ppermute(value, axis, [(i, i ^ mask) for i in range(size)])


def digits_of(size):
    found = []
    stride = 1
    while stride < size:
        radix = 2 if stride == 1 or size // stride < 4 else 4
        found.append((stride, radix))
        stride *= radix
    return found


def gather_steps(size):
    steps = []
    while size > 1:
        size //= 2
        steps.append(size)
    return steps


def own_order(shards, axis):
    size = shards.shape[0]
    order = jnp.bitwise_xor(jnp.arange(size, dtype=jnp.int32), lax.axis_index(axis))
    return shards.at[order].get(mode="promise_in_bounds")


def join_pieces(pieces, axis):
    place = {}
    for _, offs in pieces:
        for off in offs:
            place[off] = len(place)
    spots = jnp.array([place[off] for off in range(len(place))], jnp.int32)
    order = jnp.bitwise_xor(jnp.arange(len(place), dtype=jnp.int32), lax.axis_index(axis))
    whole = jnp.concatenate([piece for piece, _ in pieces])
    return whole.at[spots.at[order].get(mode="promise_in_bounds")].get(mode="promise_in_bounds")


def split_blocks(blocks, axis, digits, digit):
    stride, radix = digit
    place = digits.index(digit)
    mine = (lax.axis_index(axis) // stride) % radix
    parts = [
        lax.dynamic_index_in_dim(blocks, jnp.bitwise_xor(mine, k), place, False)
        for k in range(radix)
    ]
    return parts, [d for d in digits if d != digit]


def join_blocks(parts, axis, digit, *first):
    stride, radix = digit
    got = tuple(swap(parts[k], axis, k * stride) for k in range(1, radix))
    if first:
        got = after(got, *first)
    total = parts[0].astype(F32)
    for part in got:
        total = total + part.astype(F32)
    return total


def sum_everywhere(value, axis):
    size = lax.axis_size(axis)
    stride = 1
    while stride < size:
        radix = min(8, size // stride)
        parts = [value] + [swap(value, axis, k * stride) for k in range(1, radix)]
        while len(parts) > 1:
            parts = [parts[i] + parts[i + 1] for i in range(0, len(parts), 2)]
        value = parts[0]
        stride *= radix
    return value


def after(value, *first):
    return lax.optimization_barrier((value,) + first)[0]


def spread_kernel(mixes, pre, post, pre_back, post_back):
    heads = mixes.shape[1]
    tall = heads * GROUP
    wide = (lax.broadcasted_iota(jnp.int32, (tall, heads), 0) // GROUP) == (
        lax.broadcasted_iota(jnp.int32, (tall, heads), 1)
    )
    wide = wide.astype(F32)
    row = lax.broadcasted_iota(jnp.int32, (tall, tall), 0)
    col = lax.broadcasted_iota(jnp.int32, (tall, tall), 1)
    same = row % GROUP == col % GROUP

    def exact(left, right, dims):
        return lax.dot_general(
            left, right, dims, precision=lax.Precision.HIGHEST, preferred_element_type=F32
        )

    for which, (turned, straight) in enumerate(((pre, pre_back), (post, post_back))):
        matrix = mixes[which]
        for out, dims in ((straight, NN), (turned, NT)):
            tallest = exact(wide, matrix, dims)
            full = jnp.where(same, exact(tallest, wide, NT), 0.0)
            high = full.astype(BF)
            out[:tall, :] = high
            out[tall:, :] = (full - high.astype(F32)).astype(BF)


def spread(mixes):
    tall = mixes.shape[1] * GROUP
    return pl.pallas_call(
        spread_kernel,
        out_shape=[jax.ShapeDtypeStruct((2 * tall, tall), BF)] * 4,
        name="spread",
    )(mixes)


def two_heads(rows, first, second):
    return jnp.concatenate([rows * first, rows * second], 0)


def mix(matrix, values):
    out = dot(matrix, values)
    half = matrix.shape[0] // 2
    return out[:half] + out[half:]


def head_masks(scaling):
    lane = lax.broadcasted_iota(jnp.int32, (1, LANES), 1)
    low = lane < LANES // 2
    return low, jnp.where(low, scaling, 0.0).astype(BF), jnp.where(low, 0.0, scaling).astype(BF)


def fill_sequence(meta, sources, qkv, sems):
    copies = []
    for d, source in enumerate(sources):
        start = pl.multiple_of(jnp.bitwise_xor(meta[1], d) * KEYS, KEYS)
        copies.append(pltpu.make_async_copy(source, qkv.at[pl.ds(start, KEYS)], sems.at[d]))
    for copy in copies:
        copy.start()
    for copy in copies:
        copy.wait()


def forward_kernel(meta, *refs):
    sources, (pre, post, attended, probs, weights, qkv, held, sems) = refs[:4], refs[4:]
    heads = probs.shape[0]
    width = attended.shape[1]
    pairs = heads // 2
    tall = heads * GROUP
    step = pl.program_id(0)
    pl.when(step == 0)(partial(fill_sequence, meta, sources, qkv, sems))
    length = meta[0]
    row0 = pl.multiple_of(step * KEYS + meta[2] * ROWS, ROWS)
    chunks = (jnp.minimum(row0 + ROWS, length) + KEYS - 1) // KEYS
    low, first_s, second_s = head_masks(1.0 / math.sqrt(width // heads))

    def score(kc, carry):
        k0 = pl.multiple_of(kc * KEYS, KEYS)
        for p in range(pairs):
            at = p * LANES
            queries = two_heads(qkv[pl.ds(row0, ROWS), at : at + LANES], first_s, second_s)
            keys = qkv[pl.ds(k0, KEYS), width + at : width + at + LANES]
            scores = dot(queries, keys, NT).astype(BF)
            weights[2 * p : 2 * p + 2, :, pl.ds(k0, KEYS)] = scores.reshape(2, ROWS, KEYS)
        return carry

    lax.fori_loop(0, chunks, score, 0)

    def group(n, batch, carry):
        side = SIDE[n]
        rows = [
            pl.ds(pl.multiple_of((batch * side + u) * GROUP, GROUP), GROUP) for u in range(side)
        ]
        col_at = lax.broadcasted_iota(jnp.int32, (GROUP, KEYS), 1)
        row_at = lax.broadcasted_iota(jnp.int32, (GROUP, KEYS), 0)
        peak = [None] * side
        total = [None] * side
        for kc in range(n):
            cols = slice(kc * KEYS, (kc + 1) * KEYS)
            for u in range(side):
                mixed = mix(pre[...], weights[:, rows[u], cols].reshape(tall, KEYS))
                key_pos = col_at + kc * KEYS
                query_pos = row0 + (batch * side + u) * GROUP + row_at
                allowed = (key_pos <= query_pos) & (key_pos < length)
                mixed = jnp.where(allowed[None], mixed.reshape(heads, GROUP, KEYS), -1e30)
                mixed = mixed.reshape(tall, KEYS)
                held[u, :, cols] = mixed
                part = jnp.maximum(mixed[:, :LANES], mixed[:, LANES:])
                peak[u] = part if kc == 0 else jnp.maximum(peak[u], part)
        top = [jnp.max(peak[u], axis=1, keepdims=True) for u in range(side)]
        for kc in range(n):
            cols = slice(kc * KEYS, (kc + 1) * KEYS)
            for u in range(side):
                shifted = jnp.exp(held[u, :, cols] - top[u])
                held[u, :, cols] = shifted
                part = shifted[:, :LANES] + shifted[:, LANES:]
                total[u] = part if kc == 0 else total[u] + part
        inverse = [1.0 / jnp.sum(total[u], axis=1, keepdims=True) for u in range(side)]
        for kc in range(n):
            cols = slice(kc * KEYS, (kc + 1) * KEYS)
            for u in range(side):
                low_probs = (held[u, :, cols] * inverse[u]).astype(BF)
                probs[:, rows[u], cols] = low_probs.reshape(heads, GROUP, KEYS)
                mixed = mix(post[...], low_probs).astype(BF)
                weights[:, rows[u], cols] = mixed.reshape(heads, GROUP, KEYS)
        return carry

    def rest(n):
        lax.fori_loop(0, ROWS // GROUP // SIDE[n], partial(group, n), 0)
        for p in range(pairs):
            at = p * LANES
            pair = weights[2 * p : 2 * p + 2, :, : n * KEYS].reshape(2 * ROWS, n * KEYS)
            out = dot(pair, qkv[: n * KEYS, 2 * width + at : 2 * width + at + LANES])
            attended[:, at : at + LANES] = jnp.where(low, out[:ROWS], out[ROWS:]).astype(BF)

    for n in range(1, probs.shape[2] // KEYS + 1):
        pl.when(chunks == n)(partial(rest, n))


def backward_kernel(meta, *refs):
    sources, refs = refs[:4], refs[4:]
    grad_rows, pre, post, probs, weights, stay, away, grad_pre, grad_post = refs[:9]
    qkv, scores, grads, held, grad_qkv, sum_pre, sum_post, sems = refs[9:]
    heads = probs.shape[0]
    width = grad_rows.shape[1]
    pairs = heads // 2
    tall = heads * GROUP
    step = pl.program_id(0)
    me = meta[1]

    @pl.when(step == 0)
    def _():
        grad_qkv[...] = jnp.zeros_like(grad_qkv)
        sum_pre[...] = jnp.zeros_like(sum_pre)
        sum_post[...] = jnp.zeros_like(sum_post)
        fill_sequence(meta, sources, qkv, sems)

    length = meta[0]
    row0 = pl.multiple_of(step * KEYS + meta[2] * ROWS, ROWS)
    chunks = (jnp.minimum(row0 + ROWS, length) + KEYS - 1) // KEYS
    chunks = jnp.where(row0 < length, chunks, 0)
    scaling = 1.0 / math.sqrt(width // heads)
    low, first_s, second_s = head_masks(scaling)
    low, first_one, second_one = head_masks(1.0)
    lanes = pl.ds(pl.multiple_of(meta[2] * ROWS, ROWS), ROWS)

    def slot_of(home):
        d = jnp.bitwise_xor(me, home)
        return 2 * jnp.bitwise_and(d, 1) + d // 2


    def score(kc, carry):
        k0 = pl.multiple_of(kc * KEYS, KEYS)
        for p in range(pairs):
            at = p * LANES
            queries = two_heads(qkv[pl.ds(row0, ROWS), at : at + LANES], first_s, second_s)
            grad = two_heads(grad_rows[:, at : at + LANES], first_one, second_one)
            keys = qkv[pl.ds(k0, KEYS), width + at : width + at + LANES]
            values = qkv[pl.ds(k0, KEYS), 2 * width + at : 2 * width + at + LANES]
            both = slice(2 * p, 2 * p + 2)
            cols = pl.ds(k0, KEYS)
            scores[both, :, cols] = dot(queries, keys, NT).astype(BF).reshape(2, ROWS, KEYS)
            grads[both, :, cols] = dot(grad, values, NT).astype(BF).reshape(2, ROWS, KEYS)
        return carry

    lax.fori_loop(0, chunks, score, 0)

    def group(n, batch, carry):
        side = SIDE_BACK[n]
        rows = [
            pl.ds(pl.multiple_of((batch * side + u) * GROUP, GROUP), GROUP) for u in range(side)
        ]
        span = slice(0, n * KEYS)
        total = [None] * side
        for kc in range(n):
            cols = slice(kc * KEYS, (kc + 1) * KEYS)
            for u in range(side):
                grad_probs = mix(post[...], grads[:, rows[u], cols].reshape(tall, KEYS))
                held[u, :, cols] = grad_probs
                term = probs[:, rows[u], cols].reshape(tall, KEYS).astype(F32) * grad_probs
                part = term[:, :LANES] + term[:, LANES:]
                total[u] = part if kc == 0 else total[u] + part
        added = None
        for u in range(side):
            left = probs[:, rows[u], span].reshape(tall, n * KEYS)
            term = dot(left, grads[:, rows[u], span].reshape(tall, n * KEYS), NT)
            added = term if u == 0 else added + term
        sum_post[...] += added
        delta = [jnp.sum(total[u], axis=1, keepdims=True) for u in range(side)]
        mixed = [[] for _ in range(side)]
        for kc in range(n):
            cols = slice(kc * KEYS, (kc + 1) * KEYS)
            for u in range(side):
                prob = probs[:, rows[u], cols].reshape(tall, KEYS).astype(F32)
                grad_mixed = (prob * (held[u, :, cols] - delta[u])).astype(BF)
                mixed[u].append(grad_mixed)
                back = mix(pre[...], grad_mixed).astype(BF)
                grads[:, rows[u], cols] = back.reshape(heads, GROUP, KEYS)
        added = None
        for u in range(side):
            left = scores[:, rows[u], span].reshape(tall, n * KEYS)
            term = dot(left, jnp.concatenate(mixed[u], 1), NT)
            added = term if u == 0 else added + term
        sum_pre[...] += added
        return carry

    def rest(n):
        lax.fori_loop(0, ROWS // GROUP // SIDE_BACK[n], partial(group, n), 0)
        for p in range(pairs):
            at = p * LANES
            mine = slice(at, at + LANES)
            both = slice(2 * p, 2 * p + 2)
            queries = two_heads(qkv[pl.ds(row0, ROWS), mine], first_s, second_s).T
            grad = two_heads(grad_rows[:, mine], first_one, second_one).T
            back = grads[both, :, : n * KEYS].reshape(2 * ROWS, n * KEYS)
            out = dot(back, qkv[: n * KEYS, width + at : width + at + LANES])
            out = jnp.where(low, out[:ROWS], out[ROWS:]) * scaling
            grad_qkv[slot_of(step), mine, lanes] = out.T
            for kc in range(n):
                cols = slice(kc * KEYS, (kc + 1) * KEYS)
                to = slot_of(kc)
                grad_qkv[to, width + at : width + at + LANES, :] += dot(
                    queries, grads[both, :, cols].reshape(2 * ROWS, KEYS)
                )
                grad_qkv[to, 2 * width + at : 2 * width + at + LANES, :] += dot(
                    grad, weights[both, :, cols].reshape(2 * ROWS, KEYS)
                )

    for n in range(1, probs.shape[2] // KEYS + 1):
        pl.when(chunks == n)(partial(rest, n))

    @pl.when(step == pl.num_programs(0) - 1)
    def _():
        stay[...] = grad_qkv[:2]
        away[...] = grad_qkv[2:].astype(BF)
        row = lax.broadcasted_iota(jnp.int32, (tall, tall), 0)
        col = lax.broadcasted_iota(jnp.int32, (tall, tall), 1)
        same = row % GROUP == col % GROUP
        pick = (
            lax.broadcasted_iota(jnp.int32, (tall, LANES), 0) // GROUP
            == lax.broadcasted_iota(jnp.int32, (tall, LANES), 1)
        ).astype(F32)
        for source, out in ((sum_pre, grad_pre), (sum_post, grad_post)):
            kept = jnp.where(same, source[...], 0.0)
            wide = lax.dot_general(
                kept, pick, NN, precision=lax.Precision.HIGHEST, preferred_element_type=F32
            )
            for head in range(heads):
                out[head : head + 1, :] = jnp.sum(
                    wide[head * GROUP : (head + 1) * GROUP], axis=0, keepdims=True
                )


ANY = pl.BlockSpec(memory_space=pl.ANY)


def is_live(step, meta):
    return step * KEYS + meta[2] * ROWS < meta[0]


def attend(meta, sources, pre, post, heads, flops):
    width = sources[0].shape[1] // 3
    tall = heads * GROUP
    steps = 4
    full_len = steps * KEYS
    matrix = pl.BlockSpec((2 * tall, tall), lambda i, m: (0, 0), pipeline_mode=pl.Buffered(1))
    wide = pl.BlockSpec(
        (None, heads, ROWS, full_len), lambda i, m: (jnp.where(is_live(i, m), i, steps), 0, 0, 0)
    )
    kept = jax.ShapeDtypeStruct((steps + 1, heads, ROWS, full_len), BF)
    return pl.pallas_call(
        forward_kernel,
        grid_spec=pltpu.PrefetchScalarGridSpec(
            num_scalar_prefetch=1,
            grid=(steps,),
            in_specs=[ANY] * 4 + [matrix, matrix],
            out_specs=[
                pl.BlockSpec((None, ROWS, width), lambda i, m: (jnp.bitwise_xor(i, m[1]), 0, 0)),
                wide,
                wide,
            ],
            scratch_shapes=[
                pltpu.VMEM((full_len, 3 * width), BF),
                pltpu.VMEM((8, tall, full_len), F32),
                pltpu.SemaphoreType.DMA((4,)),
            ],
        ),
        out_shape=[jax.ShapeDtypeStruct((steps, ROWS, width), BF), kept, kept],
        compiler_params=pltpu.CompilerParams(vmem_limit_bytes=56 * 2**20),
        cost_estimate=pl.CostEstimate(
            flops=flops, bytes_accessed=1, transcendentals=0
        ),
        name="attend",
    )(meta, *sources, pre, post)


def attend_back(meta, sources, grad_rows, pre, post, probs, weights, flops):
    width = sources[0].shape[1] // 3
    steps = 4
    heads = probs.shape[1]
    tall = heads * GROUP
    full_len = steps * KEYS

    def newest(step, meta):
        last = 0
        for other in range(1, steps):
            last = jnp.where(is_live(other, meta), other, last)
        return jnp.minimum(step, last)

    matrix = pl.BlockSpec((2 * tall, tall), lambda i, m: (0, 0), pipeline_mode=pl.Buffered(1))
    wide = pl.BlockSpec((None, heads, ROWS, full_len), lambda i, m: (newest(i, m), 0, 0, 0))
    rows = pl.BlockSpec((None, ROWS, width), lambda i, m: (jnp.bitwise_xor(i, m[1]), 0, 0))
    small = pl.BlockSpec((heads, LANES), lambda i, m: (0, 0))
    pairs = pl.BlockSpec(
        (2, 3 * width, KEYS), lambda i, m: (0, 0, 0), pipeline_mode=pl.Buffered(1)
    )
    return pl.pallas_call(
        backward_kernel,
        grid_spec=pltpu.PrefetchScalarGridSpec(
            num_scalar_prefetch=1,
            grid=(steps,),
            in_specs=[ANY] * 4 + [rows, matrix, matrix, wide, wide],
            out_specs=[
                pairs,
                pairs,
                small,
                small,
            ],
            scratch_shapes=[
                pltpu.VMEM((full_len, 3 * width), BF),
                pltpu.VMEM((heads, ROWS, full_len), BF),
                pltpu.VMEM((heads, ROWS, full_len), BF),
                pltpu.VMEM((4, tall, full_len), F32),
                pltpu.VMEM((4, 3 * width, KEYS), F32),
                pltpu.VMEM((tall, tall), F32),
                pltpu.VMEM((tall, tall), F32),
                pltpu.SemaphoreType.DMA((4,)),
            ],
        ),
        out_shape=[
            jax.ShapeDtypeStruct((2, 3 * width, KEYS), F32),
            jax.ShapeDtypeStruct((2, 3 * width, KEYS), BF),
            jax.ShapeDtypeStruct((heads, LANES), F32),
            jax.ShapeDtypeStruct((heads, LANES), F32),
        ],
        compiler_params=pltpu.CompilerParams(vmem_limit_bytes=60 * 2**20),
        cost_estimate=pl.CostEstimate(
            flops=flops, bytes_accessed=1, transcendentals=0
        ),
        name="attend_back",
    )(meta, *sources, grad_rows, pre, post, probs, weights)


def gelu_both(value):
    scale = math.sqrt(2.0 / math.pi)
    square = value * value
    bent = jnp.tanh(scale * (value + 0.044715 * (square * value)))
    share = 0.5 * (1.0 + bent)
    slope = share + 0.5 * value * (1.0 - bent * bent) * (
        scale * (1.0 + 3.0 * 0.044715 * square)
    )
    return value * share, slope


def fill_weights(meta, sources, offs, inner, outer, proj, sems):
    hidden = inner.shape[1] // 2
    width = proj.shape[0]
    half = width // 2
    late, early = [], []

    def copy(source, target, kind=None):
        sem = sems.at[len(late) + len(early)]
        (late if kind is None else early).append(pltpu.make_async_copy(source, target, sem))

    count = len(sources) // 2
    for side in range(2):
        lanes = jnp.bitwise_xor(meta[1], side) * half
        to_proj = pl.ds(pl.multiple_of(lanes, LANES), half)
        to_inner = slice(side * hidden, (side + 1) * hidden)
        here = sources[count * side : count * side + count]
        if offs is None:
            copy(here[0], inner.at[:, to_inner])
            copy(here[1], proj.at[:, to_proj], 1)
            copy(here[2], outer.at[to_inner])
            continue
        own_rows = here[0].shape[1]
        folds = hidden * own_rows // width // own_rows
        for source, owners in zip(here, offs):
            for at_source, off in enumerate(owners):
                block = source.at[at_source]
                owner = jnp.bitwise_xor(meta[0], off)
                rows = pl.ds(pl.multiple_of(owner * own_rows, own_rows), own_rows)
                copy(block.at[:, :hidden], inner.at[rows, to_inner])
                copy(block.at[:, hidden : hidden + half], proj.at[rows, to_proj], 1)
                for fold in range(folds):
                    start = side * hidden + (owner * folds + fold) * own_rows
                    at = hidden + half + fold * width
                    copy(
                        block.at[:, at : at + width],
                        outer.at[pl.ds(pl.multiple_of(start, own_rows), own_rows)],
                    )
    for one in early + late:
        one.start()
    return early, late


TILE = 256
CHUNK = 512


def feed_kernel(offs, meta, gains, tokens, attended, grad_out, *refs):
    count = len(refs) - 17
    sources, refs = refs[:count], refs[count:]
    output, grad_resid, resid_low, grad_attended, gain_two, second_in = refs[:6]
    active, grad_hidden = refs[6:8], refs[8:10]
    inner, outer, proj, resid, out_sum, grad_sum, sems = refs[10:]
    rows = tokens.shape[0]
    step = pl.program_id(0)
    tiles = [slice(at, at + TILE) for at in range(0, rows, TILE)]

    @pl.when(step == 0)
    def _():
        early, late = fill_weights(meta, sources, offs, inner, outer, proj, sems)
        for one in early:
            one.wait()
        for tile in tiles:
            seq = meta[2 + tile.start // TILE]
            value = tokens[pl.ds(pl.multiple_of(seq * TILE, TILE), TILE)].astype(F32)
            value = value + dot(attended[tile], proj[...])
            resid[tile] = value
            out_sum[tile] = value
            grad_sum[tile] = jnp.zeros_like(value)
            second_in[tile] = (value * inverse_rms(value) * gains[1:2]).astype(BF)
        for one in late:
            one.wait()

    cols = pl.ds(pl.multiple_of(step * CHUNK, CHUNK), CHUNK)
    for tile in tiles:
        up = inner[:, cols]
        down = outer[cols]
        value, slope = gelu_both(dot(second_in[tile], up))
        value = value.astype(BF)
        back = (dot(grad_out[tile], down, NT) * slope).astype(BF)
        for side in range(2):

            @pl.when((step * 2 >= pl.num_programs(0)) == (side == 1))
            def _():
                active[side][tile] = value
                grad_hidden[side][tile] = back

        out_sum[tile] += dot(value, down)
        grad_sum[tile] += dot(back, up, NT)

    @pl.when(step == pl.num_programs(0) - 1)
    def _():
        gain_sum = jnp.zeros((8, proj.shape[0]), F32)
        for tile in tiles:
            seq = meta[2 + tile.start // TILE]
            output[pl.ds(pl.multiple_of(seq * TILE, TILE), TILE)] = out_sum[tile].astype(BF)
            value = resid[tile]
            scale = inverse_rms(value)
            normed = value * scale
            grad = grad_sum[tile]
            gain_sum += jnp.sum((grad * normed).reshape(TILE // 8, 8, -1), axis=0)
            back = grad_out[tile].astype(F32) + rms_backward(scale, normed, grad * gains[1:2])
            grad_resid[tile] = back
            back = back.astype(BF)
            resid_low[tile] = back
            grad_attended[tile] = dot(back, proj[...], NT).astype(BF)
        gain_two[...] = gain_sum


def feed_forward(meta, gains, tokens, attended, grad_out, sources, offs, hidden):
    rows, width = tokens.shape
    copies = 6
    if offs is not None:
        owners = sum(len(o) for o in offs)
        copies = 2 * owners * (2 + hidden // 2 // width)
    chunks = hidden // CHUNK

    def whole(shape):
        return pl.BlockSpec(shape, lambda c, m: (0,) * len(shape), pipeline_mode=pl.Buffered(1))

    flat = whole((rows, width))
    first = pl.BlockSpec((rows, CHUNK), lambda c, m: (0, jnp.minimum(c, chunks // 2 - 1)))
    second = pl.BlockSpec((rows, CHUNK), lambda c, m: (0, jnp.maximum(c - chunks // 2, 0)))
    wide = jax.ShapeDtypeStruct((rows, hidden // 2), BF)
    return pl.pallas_call(
        partial(feed_kernel, offs),
        grid_spec=pltpu.PrefetchScalarGridSpec(
            num_scalar_prefetch=1,
            grid=(chunks,),
            in_specs=[whole((2, width)), flat, flat, flat] + [ANY] * len(sources),
            out_specs=[flat, flat, flat, flat, whole((8, width)), flat, first, second, first, second],
            scratch_shapes=[
                pltpu.VMEM((width, hidden), BF),
                pltpu.VMEM((hidden, width), BF),
                pltpu.VMEM((width, width), BF),
                pltpu.VMEM((rows, width), F32),
                pltpu.VMEM((rows, width), F32),
                pltpu.VMEM((rows, width), F32),
                pltpu.SemaphoreType.DMA((copies,)),
            ],
        ),
        out_shape=[
            jax.ShapeDtypeStruct((rows, width), BF),
            jax.ShapeDtypeStruct((rows, width), F32),
            jax.ShapeDtypeStruct((rows, width), BF),
            jax.ShapeDtypeStruct((rows, width), BF),
            jax.ShapeDtypeStruct((8, width), F32),
            jax.ShapeDtypeStruct((rows, width), BF),
            wide,
            wide,
            wide,
            wide,
        ],
        compiler_params=pltpu.CompilerParams(vmem_limit_bytes=56 * 2**20),
        cost_estimate=pl.CostEstimate(
            flops=22 * 10**9, bytes_accessed=40 * 10**6, transcendentals=0
        ),
        name="feed_forward",
    )(meta, gains, tokens, attended, grad_out, *sources)


def weight_kernel(meta, second_in, attended, resid_low, grad_out, active, back, first, last, turned):
    width = second_in.shape[1]
    half = width // 2
    step = pl.program_id(0)

    @pl.when(step == 0)
    def _():
        turned[...] = second_in[...].T
        lanes = pl.ds(pl.multiple_of(meta[0] * half, LANES), half)
        hidden = first.shape[1] - half
        first[:, hidden:] = dot(attended[...], resid_low[:, lanes], TN).astype(first.dtype)

    cols = pl.ds(pl.multiple_of(step * CHUNK, CHUNK), CHUNK)
    first[:, cols] = dot(turned[...], back[...]).astype(first.dtype)
    last[...] = dot(active[...], grad_out[...], TN).astype(last.dtype)


def weight_sums(which, second_in, attended, resid_low, grad_out, active, back, kind):
    rows, width = second_in.shape
    hidden = active.shape[1]

    def whole(shape):
        return pl.BlockSpec(shape, lambda c, m: (0, 0), pipeline_mode=pl.Buffered(1))

    flat = whole((rows, width))
    chunk = pl.BlockSpec((rows, CHUNK), lambda c, m: (0, c))
    return pl.pallas_call(
        weight_kernel,
        grid_spec=pltpu.PrefetchScalarGridSpec(
            num_scalar_prefetch=1,
            grid=(hidden // CHUNK,),
            in_specs=[flat] * 4 + [chunk, chunk],
            out_specs=[
                whole((width, hidden + width // 2)),
                pl.BlockSpec((CHUNK, width), lambda c, m: (c, 0)),
            ],
            scratch_shapes=[pltpu.VMEM((width, rows), BF)],
        ),
        out_shape=[
            jax.ShapeDtypeStruct((width, hidden + width // 2), kind),
            jax.ShapeDtypeStruct((hidden, width), kind),
        ],
        compiler_params=pltpu.CompilerParams(vmem_limit_bytes=56 * 2**20),
        cost_estimate=pl.CostEstimate(flops=1, bytes_accessed=1, transcendentals=0),
        name="weight_sums",
    )(which, second_in, attended, resid_low, grad_out, active, back)


def squares_kernel(*refs):
    pairs, out = refs[:-1], refs[-1]
    total = jnp.zeros((8, LANES), F32)
    for at in range(0, len(pairs), 2):
        both = []
        for ref in pairs[at : at + 2]:
            rows, cols = ref.shape
            part = jnp.zeros((8, LANES), F32)
            value = ref[...]
            value = value * value
            value = jnp.sum(value.reshape(rows // 8, 8, cols), axis=0)
            for lane in range(0, cols, LANES):
                part = part + value[:, lane : lane + LANES]
            both.append(part)
        total = total + (both[0] + both[1])
    out[...] = total


def assemble_kernel(piece, meta, mine, other, last_mine, last_other, inner, proj, outer, out):
    squares_kernel(mine, other, last_mine, last_other, out)
    first = meta[0] == 0
    width = proj.shape[1]
    cut = inner.shape[1] // 2
    for which, (left, right) in enumerate(((mine, other), (other, mine))):

        @pl.when(first == (which == 0))
        def _():
            proj[:, : width // 2] = left[:, cut:]
            proj[:, width // 2 :] = right[:, cut:]
            for at in range(0, cut, piece):
                cols = slice(at, at + piece)
                inner[:, 2 * at : 2 * at + 2 * piece] = jnp.concatenate(
                    [left[:, cols], right[:, cols]], axis=1
                )

    for which, (left, right) in enumerate(((last_mine, last_other), (last_other, last_mine))):

        @pl.when(first == (which == 0))
        def _():
            rows = left.shape[0]
            outer[:rows] = left[...]
            outer[rows:] = right[...]


def assemble(core, piece, halves, last_halves):
    rows, wide = halves[0].shape
    last_rows, width = last_halves[0].shape
    vmem = pl.BlockSpec(memory_space=pltpu.VMEM)
    *found, squares = pl.pallas_call(
        partial(assemble_kernel, piece),
        in_specs=[pl.BlockSpec(memory_space=pltpu.SMEM)] + [vmem] * 4,
        out_specs=[vmem] * 4,
        out_shape=[
            jax.ShapeDtypeStruct((rows, 2 * wide - width), F32),
            jax.ShapeDtypeStruct((rows, width), F32),
            jax.ShapeDtypeStruct((2 * last_rows, width), F32),
            jax.ShapeDtypeStruct((8, LANES), F32),
        ],
        cost_estimate=pl.CostEstimate(flops=1, bytes_accessed=1, transcendentals=0),
        compiler_params=pltpu.CompilerParams(vmem_limit_bytes=40 * 2**20),
        name="assemble",
    )(core[None], *halves, *last_halves)
    return *found, jnp.sum(squares)


def squares_of(pairs):
    if any(v.shape[0] % 8 for pair in pairs for v in pair):
        found = [jnp.sum(a * a) + jnp.sum(b * b) for a, b in pairs]
        return sum(found[1:], found[0])
    vmem = pl.BlockSpec(memory_space=pltpu.VMEM)
    flat = [v for pair in pairs for v in pair]
    out = pl.pallas_call(
        squares_kernel,
        in_specs=[vmem] * len(flat),
        out_specs=vmem,
        out_shape=jax.ShapeDtypeStruct((8, LANES), F32),
        cost_estimate=pl.CostEstimate(flops=1, bytes_accessed=1, transcendentals=0),
        compiler_params=pltpu.CompilerParams(vmem_limit_bytes=40 * 2**20),
        name="squares",
    )(*flat)
    return jnp.sum(out)


RATES = (0.03, 0.1, 0.03, 0.02, 0.3, 0.3)


def adamw_kernel(factor, *refs):
    count = len(RATES)
    grads, states, outs = refs[:count], refs[count : 5 * count], refs[5 * count :]

    def update(at):
        scaled = grads[at][...] * factor[0]
        new = adamw(*[r[...] for r in states[4 * at : 4 * at + 4]], scaled, RATES[at])
        for out, value in zip(outs[4 * at : 4 * at + 4], new):
            out[...] = value

    for at in range(4):
        update(at)

    @pl.when(pl.program_id(0) == 0)
    def _():
        for at in range(4, count):
            update(at)


def adamw_all(factor, grads, states):
    steps = 6

    def block(at, shape):
        if at >= 4:
            return pl.BlockSpec(shape, lambda i: (0,) * len(shape))
        if at == 3:
            return pl.BlockSpec((shape[0] // steps, shape[1]), lambda i: (i, 0))
        return pl.BlockSpec((shape[0], shape[1] // steps), lambda i: (0, i))

    specs = [block(at, g.shape) for at, g in enumerate(grads)]
    wide = [s for s in specs for _ in range(4)]
    out = pl.pallas_call(
        adamw_kernel,
        grid=(steps,),
        in_specs=[pl.BlockSpec(memory_space=pltpu.SMEM)] + specs + wide,
        out_specs=wide,
        out_shape=[jax.ShapeDtypeStruct(g.shape, F32) for g in grads for _ in range(4)],
        compiler_params=pltpu.CompilerParams(vmem_limit_bytes=62 * 2**20),
        name="adamw_all",
    )(factor, *grads, *[v for state in states for v in state])
    return out


def first_kernel(offs, wanted, blocks, meta, tokens, *refs):
    count = 2 * (1 if offs is None else len(offs))
    sources, refs = refs[:count], refs[count:]
    outs, (first_in, gains, weight, mixed, sems) = refs[: len(wanted)], refs[len(wanted) :]
    side = weight.shape[1] // 2
    copies = []

    def copy(source, target):
        copies.append(pltpu.make_async_copy(source, target, sems.at[len(copies)]))

    for which in range(2):
        here = sources[which * (count // 2) : (which + 1) * (count // 2)]
        start = pl.multiple_of(jnp.bitwise_xor(meta[1], which) * side, side)
        if offs is None:
            copy(here[0].at[:, :side], weight.at[:, pl.ds(start, side)])
            if which == 0:
                copy(here[0].at[:, side:], mixed)
            continue
        own_rows = here[0].shape[1]
        for source, owners in zip(here, offs):
            for at, off in enumerate(owners):
                owner = jnp.bitwise_xor(meta[0], off)
                rows = pl.ds(pl.multiple_of(owner * own_rows, own_rows), own_rows)
                copy(source.at[at, :, :side], weight.at[rows, pl.ds(start, side)])
                if which == 0:
                    copy(source.at[at, :, side:], mixed.at[rows])
    for one in copies:
        one.start()
    for one in copies:
        one.wait()
    gain = mixed[...].astype(F32).T[:8]
    gains[...] = gain
    for block in range(blocks):
        value = tokens[meta[2 + block]].astype(F32)
        low = (value * inverse_rms(value) * gain[:1]).astype(BF)
        first_in[block * KEYS : (block + 1) * KEYS] = low
        if block not in wanted:
            continue
        out = outs[wanted.index(block)]
        wide = 2 * side // 3
        for col in range(0, 2 * side, wide):
            cols = slice(col, col + wide)
            out[:, cols] = dot(low, weight[:, cols]).astype(BF)


def first_product(meta, tokens, pieces, offs, wanted, blocks, with_weight):
    width = tokens.shape[2]
    rows = blocks * KEYS
    vmem = pl.BlockSpec(memory_space=pltpu.VMEM)
    out_shape = [
        *[jax.ShapeDtypeStruct((KEYS, 3 * width), BF) for _ in wanted],
        jax.ShapeDtypeStruct((rows, width), BF),
        jax.ShapeDtypeStruct((8, width), F32),
    ]
    scratch = [
        pltpu.VMEM((width, LANES), BF),
        pltpu.SemaphoreType.DMA((3 if offs is None else 3 * sum(len(o) for o in offs),)),
    ]
    if with_weight:
        out_shape.append(jax.ShapeDtypeStruct((width, 3 * width), BF))
    else:
        scratch = [pltpu.VMEM((width, 3 * width), BF)] + scratch
    return pl.pallas_call(
        partial(first_kernel, offs, wanted, blocks),
        in_specs=[pl.BlockSpec(memory_space=pltpu.SMEM), vmem] + [ANY] * len(pieces),
        out_specs=[vmem] * len(out_shape),
        out_shape=out_shape,
        scratch_shapes=scratch,
        compiler_params=pltpu.CompilerParams(vmem_limit_bytes=40 * 2**20),
        cost_estimate=pl.CostEstimate(
            flops=1, bytes_accessed=1, transcendentals=0
        ),
        name="first_product",
    )(meta, tokens, *pieces)


def first_grads_kernel(meta, first_in, *refs):
    cols, (out,) = refs[:-1], refs[-1:]
    side = out.shape[1]
    take = pl.ds(pl.multiple_of(meta[0] * side, side), side)
    total = None
    for block, grads in enumerate(cols):
        rows = first_in[block * KEYS : (block + 1) * KEYS].T
        term = dot(rows, grads[take], NT)
        total = term if block == 0 else total + term
        if block + 1 < len(cols):
            continue
        out[...] = total.astype(out.dtype)


def first_grads(which, first_in, cols, kind):
    width = first_in.shape[1]
    side = cols[0].shape[0] // 2
    vmem = pl.BlockSpec(memory_space=pltpu.VMEM)
    return pl.pallas_call(
        first_grads_kernel,
        in_specs=[pl.BlockSpec(memory_space=pltpu.SMEM)] + [vmem] * (1 + len(cols)),
        out_specs=vmem,
        out_shape=jax.ShapeDtypeStruct((width, side), kind),
        compiler_params=pltpu.CompilerParams(vmem_limit_bytes=50 * 2**20),
        cost_estimate=pl.CostEstimate(
            flops=1, bytes_accessed=1, transcendentals=0
        ),
        name="first_grads",
    )(which, first_in, *cols)


def token_grads_kernel(meta, gains, near, far, weight, tokens, grad_resid, *refs):
    out, gain_out = refs[-2:]
    step = pl.program_id(0)

    @pl.when(step == 0)
    def _():
        gain_out[...] = jnp.zeros_like(gain_out)

    for which, grads in enumerate((near, far)):

        @pl.when(step == which)
        def _():
            back = dot(weight[...], grads[...]).T
            value = tokens[...].astype(F32)
            scale = inverse_rms(value)
            normed = value * scale
            gain_out[...] += jnp.sum((back * normed).reshape(KEYS // 8, 8, -1), axis=0)
            out[...] = grad_resid[...] + rms_backward(scale, normed, back * gains[:1])


def token_grads(slot, seqs, gains, near, far, weight, tokens, grad_resid, before):
    _, rows, width = tokens.shape

    def whole(shape):
        return pl.BlockSpec(shape, lambda i, m: (0,) * len(shape), pipeline_mode=pl.Buffered(1))

    place = pl.BlockSpec((None, rows, width), lambda i, m: (m[i], 0, 0))
    extra = [] if before is None else [before]
    return pl.pallas_call(
        token_grads_kernel,
        grid_spec=pltpu.PrefetchScalarGridSpec(
            num_scalar_prefetch=1,
            grid=(2,),
            in_specs=[
                whole(gains.shape),
                whole(near.shape),
                whole(far.shape),
                whole(weight.shape),
                place,
                pl.BlockSpec((None, rows, width), lambda i, m: (2 * slot + i, 0, 0)),
            ]
            + [ANY] * len(extra),
            out_specs=[place, whole((8, width))],
        ),
        out_shape=[
            jax.ShapeDtypeStruct(tokens.shape, F32),
            jax.ShapeDtypeStruct((8, width), F32),
        ],
        input_output_aliases={7: 0} if extra else {},
        compiler_params=pltpu.CompilerParams(vmem_limit_bytes=50 * 2**20),
        cost_estimate=pl.CostEstimate(
            flops=1, bytes_accessed=1, transcendentals=0
        ),
        name="token_grads",
    )(seqs, gains, near, far, weight, tokens, grad_resid, *extra)


def prepare_kernel(owners, meta, inner, outer, proj, out):
    rows, hidden = inner.shape
    width = proj.shape[1]
    half = width // 2
    piece = hidden // owners // 2
    for core in range(2):

        @pl.when(meta[1] == core)
        def _():
            for owner in range(owners):
                at = (2 * owner + core) * piece
                out[:, owner * piece : (owner + 1) * piece] = inner[:, at : at + piece].astype(BF)
            cut = hidden // 2
            out[:, cut : cut + half] = proj[:, core * half : (core + 1) * half].astype(BF)
            for fold in range(piece // rows):
                at = core * piece + fold * rows
                start = cut + half + fold * width
                out[:, start : start + width] = outer[at : at + rows].astype(BF)


def prepare(meta, owners, inner, outer, proj):
    rows, hidden = inner.shape
    width = proj.shape[1]
    vmem = pl.BlockSpec(memory_space=pltpu.VMEM)
    return pl.pallas_call(
        partial(prepare_kernel, owners),
        in_specs=[pl.BlockSpec(memory_space=pltpu.SMEM)] + [vmem] * 3,
        out_specs=vmem,
        out_shape=jax.ShapeDtypeStruct((rows, hidden + width // 2), BF),
        cost_estimate=pl.CostEstimate(flops=1, bytes_accessed=1, transcendentals=0),
        compiler_params=pltpu.CompilerParams(vmem_limit_bytes=40 * 2**20),
        name="prepare",
    )(meta, inner, outer, proj)


def on_device(
    tokens,
    cotangent,
    lengths,
    qkv_weight,
    qkv_first,
    qkv_second,
    qkv_average,
    proj_weight,
    proj_first,
    proj_second,
    proj_average,
    inner_weight,
    inner_first,
    inner_second,
    inner_average,
    outer_weight,
    outer_first,
    outer_second,
    outer_average,
    gains,
    gain_first,
    gain_second,
    gain_average,
    mixes,
    mix_first,
    mix_second,
    mix_average,
):
    group_seqs, shard_len, width = tokens.shape
    owners = lax.axis_size("dp")
    heads = mixes.shape[1]
    own_rows = qkv_weight.shape[0]
    hidden = inner_weight.shape[1]
    half = width // 2
    slice_ff = hidden // owners // 2
    me = lax.axis_index("seq")
    pair = me // 2
    core = jnp.bitwise_and(me, 1)

    def by_core(mine, other, axis):
        return jnp.where(
            core == 0,
            jnp.concatenate([mine, other], axis),
            jnp.concatenate([other, mine], axis),
        )

    ahead = (lengths[None, :] > lengths[:, None]) | (
        (lengths[None, :] == lengths[:, None])
        & (jnp.arange(group_seqs)[None, :] < jnp.arange(group_seqs)[:, None])
    )
    rank = jnp.sum(ahead.astype(jnp.int32), axis=1)
    order = jnp.sum(
        jnp.where(
            rank[None, :] == jnp.arange(group_seqs)[:, None], jnp.arange(group_seqs)[None, :], 0
        ),
        axis=1,
    ).astype(jnp.int32)

    def sequence_of(slot, which):
        return order[which if slot == 0 else group_seqs - 1 - which]

    def arrange(value):
        return jnp.stack(
            [
                jnp.stack(
                    [
                        lax.dynamic_index_in_dim(
                            value, sequence_of(slot, jnp.bitwise_xor(pair, d)), 0, False
                        )
                        for d in range(2)
                    ]
                )
                for slot in range(2)
            ]
        )

    lengths_here = arrange(lengths)
    seqs = [jnp.stack([sequence_of(s, pair), sequence_of(s, 1 - pair)]) for s in range(2)]
    feed_meta = jnp.stack(
        [lax.axis_index("dp"), core]
        + [sequence_of(s, jnp.bitwise_xor(pair, d)) for s in range(2) for d in range(2)]
    ).astype(jnp.int32)
    metas = [jnp.stack([lengths_here[slot, 0], me, core]).astype(jnp.int32) for slot in range(2)]

    mixers = spread(mixes)
    positions = me * shard_len + jnp.arange(shard_len, dtype=jnp.int32)
    live = positions[None, None, :] < lengths_here[:, :, None]
    cot = arrange(cotangent)
    grad_out = jnp.where(live[..., None], cot, jnp.zeros_like(cot))
    folds = slice_ff // own_rows
    if own_rows % 16 == 0:
        rest = prepare(feed_meta, owners, inner_weight, outer_weight, proj_weight)[None]
    else:
        inner_mine = inner_weight.astype(BF).reshape(own_rows, owners, 2, slice_ff)
        inner_mine = lax.dynamic_index_in_dim(inner_mine, core, 2, False)
        outer_mine = outer_weight.astype(BF).reshape(2, folds, own_rows, width)
        outer_mine = lax.dynamic_index_in_dim(outer_mine, core, 0, False)
        rest = jnp.concatenate(
            [
                inner_mine.reshape(own_rows, owners * slice_ff),
                lax.dynamic_slice_in_dim(proj_weight.astype(BF), core * half, half, 1),
            ]
            + [outer_mine[f] for f in range(folds)],
            axis=1,
        )[None]
    side = qkv_weight.shape[1] // 2
    mine = lax.dynamic_slice_in_dim(qkv_weight.astype(BF), core * side, side, 1)
    mine = jnp.concatenate([mine, jnp.pad(gains.astype(BF).T, ((0, 0), (0, LANES - 2)))], 1)
    offs = None
    if owners == 8:
        shard = mine[None]
        got = swap(shard, "dp", 4)
        got = after(got, feed_meta, rest)
        pieces = [jnp.concatenate([shard, got])]
        far_z, far_x = swap(pieces[0], "dp", 2), swap(pieces[0], "dp", 1)
        beside = [swap(pieces[0], "seq", 1)]
        pieces += [far_z, far_x]
        pieces.append(swap(far_z, "dp", 1))
        beside += [swap(p, "seq", 1) for p in pieces[1:]]
        offs = ((0, 4), (2, 6), (1, 5), (3, 7))
        pieces += beside
        late = far_z
    else:
        mine = lax.all_gather(mine, "dp", axis=0, tiled=True)
        pieces = [mine, swap(mine, "seq", 1)]

    if offs is not None:
        got = swap(after(rest, late), "dp", 4)
    place = feed_meta
    near, far, *_ = first_product(
        place, tokens, pieces, offs, (0, 1), 2, False
    )
    near, far = [near], [far]
    here = swap(far[0], "seq", 2)
    beside = swap(near[0], "seq", 1)
    place, beside, mixers, metas, grad_out = lax.optimization_barrier(
        (place, beside, mixers, metas, grad_out)
    )
    pre_mix, post_mix, pre_back, post_back = mixers
    *out, first_in, gain_vals, weight_qkv = first_product(
        place, tokens, pieces, offs, (2, 3), 4, True
    )
    near.append(out[0])
    far.append(out[1])
    here = after(here, far[1], near[1])
    if offs is not None:
        here, got = lax.optimization_barrier((here, got))
        rest_pieces = [jnp.concatenate([rest, got])]
        far_z, far_x = swap(rest_pieces[0], "dp", 2), swap(rest_pieces[0], "dp", 1)
    sources = [[near[0], beside, here, swap(here, "seq", 1)]]
    next_far = swap(after(far[1], here), "seq", 2)
    beside = swap(after(near[1], here), "seq", 1)
    def by_half(rows):
        return jnp.where(core == 0, rows, rows[:, ::-1])

    rows, probs, weights = [None, None], [None, None], [None, None]
    meta = after(metas[0], sources[0])
    if offs is not None:
        meta = after(meta, rest_pieces)
        beside_rest = [swap(rest_pieces[0], "seq", 1)]
    rows[0], probs[0], weights[0] = attend(meta, sources[0], pre_mix, post_mix, heads, FLOPS[0])
    next_far, beside = lax.optimization_barrier((next_far, beside, rows[0]))[:2]
    if offs is not None:
        far_z, far_x, next_far, beside, beside_rest = lax.optimization_barrier(
            (far_z, far_x, next_far, beside, beside_rest)
        )
        rest_pieces += [far_z, far_x]
        beside_rest = list(beside_rest) + [swap(p, "seq", 1) for p in (far_z, far_x)]
        last = swap(far_z, "dp", 1)
    sources.append([near[1], beside, next_far, swap(next_far, "seq", 1)])
    far_rows = swap(rows[0][2:], "seq", 2)
    rows[1], probs[1], weights[1] = attend(
        metas[1], sources[1], pre_mix, post_mix, heads, FLOPS[1]
    )
    far_rows = after(far_rows, rows[1])
    cut = owners * slice_ff + half
    if offs is not None:
        last, *beside_rest = after([last] + beside_rest, rows[1])
        rest_pieces.append(last)
        feed_weights = rest_pieces + beside_rest + [swap(last, "seq", 1)]
    else:
        rest = lax.all_gather(rest[0], "dp")
        feed_weights = []
        for part in (rest, swap(rest, "seq", 1)):
            flat = part.reshape(owners * own_rows, -1)
            down = jnp.moveaxis(part[:, :, cut:].reshape(owners, own_rows, folds, width), 2, 1)
            feed_weights += [
                flat[:, : cut - half],
                flat[:, cut - half : cut],
                down.reshape(owners * slice_ff, width),
            ]
    far_rows = jnp.stack([far_rows, swap(rows[1][2:], "seq", 2)])
    near_rows = jnp.stack([rows[0][1], rows[1][1]])
    got = swap(jnp.stack([near_rows, far_rows[:, 1]]), "seq", 1)
    attention_output = jnp.stack(
        [
            by_half(
                jnp.stack(
                    [
                        jnp.stack([rows[slot][0], got[0, slot]]),
                        jnp.stack([far_rows[slot, 0], got[1, slot]]),
                    ]
                )
            ).reshape(2, 2 * ROWS, width)
            for slot in range(2)
        ]
    )

    flat = (-1, width)
    attention_output = attention_output.reshape(flat)
    flat_out = grad_out.reshape(flat)
    output, grad_resid, resid_low, grad_attended, gain_two, second_in, *wide = feed_forward(
        feed_meta,
        gain_vals[:2],
        tokens.reshape(flat),
        attention_output,
        flat_out,
        feed_weights,
        offs,
        hidden,
    )
    grad_attended = grad_attended.reshape(grad_out.shape)
    grad_resid = grad_resid.reshape(4, shard_len, width)

    def sums_of(side, which, kind):
        return weight_sums(
            which[None],
            second_in,
            attention_output,
            resid_low,
            flat_out,
            wide[side],
            wide[2 + side],
            kind,
        )

    output = output.reshape(tokens.shape)
    gain_two = jnp.sum(gain_two, axis=0)

    sent = sums_of(1, 1 - core, BF)
    arrived = swap(sent[0], "seq", 1), swap(sent[1], "seq", 1)
    meta = after(core, sent)
    mine = sums_of(0, meta, F32)
    arrived = after(arrived, mine, output)
    twos = [(2**k, 2) for k in range(owners.bit_length() - 1)]
    orders = [twos, twos[1:2] + twos[:1] + twos[2:]]
    chains = []
    for at in range(2):
        total = (mine[at] + arrived[at].astype(F32)).astype(BF)
        total = total.reshape((2,) * len(twos) + (-1, total.shape[1]))
        chains.append(split_blocks(total, "dp", twos[::-1], orders[at][0]))

    def send_step(at, turn, parts):
        stride, radix = orders[at][turn]
        return tuple(swap(parts[0][k], "dp", k * stride) for k in range(1, radix))

    def join_step(at, turn, parts, got):
        total = parts[0][0].astype(F32)
        for part in got:
            total = total + part.astype(F32)
        if turn + 1 == len(twos):
            return total
        return split_blocks(total.astype(BF), "dp", parts[1], orders[at][turn + 1])

    def step_on(at, turn, parts, *first):
        got = send_step(at, turn, parts)
        return join_step(at, turn, parts, after(got, *first) if first else got)

    def to_far(slot):
        found = by_half(grad_attended[slot].reshape(2, 2, ROWS, width)).reshape(4, ROWS, width)
        return found, swap(found[2:], "seq", 2)

    def from_near(found, far):
        got = swap(jnp.stack([found[1], far[1]]), "seq", 1)
        return jnp.stack([found[0], got[0], far[0], got[1]])

    def attend_slot(slot, meta, rows):
        return attend_back(
            meta, sources[slot], rows, pre_back, post_back, probs[slot], weights[slot], FLOPS[slot]
        )

    found, far = to_far(0)
    far = after(far, mine)
    next_found, next_far = to_far(1)
    meta = after(metas[0], chains)
    stay, away, back_pre, back_post = attend_slot(0, meta, from_near(found, far))
    grad_mixes = jnp.stack([back_pre[:, :heads], back_post[:, :heads]])
    chains = [step_on(at, 0, chains[at], stay) for at in range(2)]
    away, next_far = lax.optimization_barrier((away, next_far, chains))[:2]
    next_rows = from_near(next_found, next_far)
    summed = (stay + swap(away, "seq", 1).astype(F32)).astype(BF)
    far = swap(summed[1], "seq", 2)
    meta = after(metas[1], summed, chains)
    stay, away, back_pre, back_post = attend_slot(1, meta, next_rows)
    grad_mixes = grad_mixes + jnp.stack([back_pre[:, :heads], back_post[:, :heads]])
    got = [send_step(at, 1, chains[at]) for at in range(2)]
    away, far, got = lax.optimization_barrier((away, far, got, stay))[:3]
    grad_cols = [(summed[0], far)]
    summed = (stay + swap(away, "seq", 1).astype(F32)).astype(BF)
    got = after(got, summed)
    chains = [join_step(at, 1, chains[at], got[at]) for at in range(2)]
    far = swap(summed[1], "seq", 2)

    def to_tokens(slot, before, first):
        return token_grads(
            slot,
            after(seqs[slot], first),
            gain_vals,
            *grad_cols[slot],
            weight_qkv,
            tokens,
            grad_resid,
            before,
        )

    begun = to_tokens(0, None, summed)
    for turn in range(2, len(twos)):
        chains = [step_on(at, turn, chains[at], begun) for at in range(2)]
    first_part, second_part = chains
    others = first_part.astype(BF), second_part.astype(BF)
    far, begun, others = lax.optimization_barrier((far, begun, others))
    grad_cols.append((summed[0], far))
    cols = grad_cols[0] + grad_cols[1]
    sent = first_grads((1 - core)[None], first_in, cols, BF)
    qkv_mine = first_grads(after(core, sent)[None], first_in, cols, F32)

    def over_pairs(total, *first):
        total = lax.optimization_barrier(jax.tree.map(lambda v: v.astype(BF), total))
        got = jax.tree.map(lambda v: swap(v, "seq", 2), total)
        if first:
            got = after(got, *first)
        return jax.tree.map(lambda v, w: v.astype(F32) + w.astype(F32), total, got)

    arrived = after(swap(sent, "seq", 1), qkv_mine)
    qkv_total = (qkv_mine + arrived.astype(F32)).astype(BF)
    qkv_total = qkv_total.reshape((2,) * len(twos) + (own_rows, side))
    third = side // LANES // 3 * LANES
    chains = [qkv_total[..., third:], qkv_total[..., :third]]
    chains = [split_blocks(chains[at], "dp", twos[::-1], orders[at][0]) for at in range(2)]
    others = over_pairs(after(others, [p for p, _ in chains]))
    chains = [step_on(at, 0, chains[at]) for at in range(2)]
    got = [send_step(at, 1, chains[at]) for at in range(2)]
    grad_rows_tokens, gain_more = to_tokens(1, begun[0], got[1])
    gain_one = jnp.sum(begun[1] + gain_more, axis=0)
    small = jnp.concatenate([gain_one, gain_two, grad_mixes.reshape(-1)])
    count = small.shape[0]
    small = jnp.pad(small, (0, -(count + 1) % (8 * LANES) + 1)).reshape(-1, LANES)
    chains = [join_step(at, 1, chains[at], got[at]) for at in range(2)]

    first_halves = (others[0], swap(others[0], "seq", 1))
    last_halves = (others[1], swap(others[1], "seq", 1))
    if own_rows % 8 == 0:
        red_inner, red_proj, red_outer, squares = assemble(
            core, slice_ff, first_halves, last_halves
        )
    else:
        red_proj = by_core(*[g[:, cut - half :] for g in first_halves], 1)
        red_inner = by_core(
            *[g[:, : cut - half].reshape(own_rows, owners, 1, slice_ff) for g in first_halves], 2
        ).reshape(own_rows, hidden)
        red_outer = by_core(*last_halves, 0)
        squares = squares_of([first_halves, last_halves])
    small = small + swap(small, "seq", 1)
    small = small + swap(small, "seq", 2)
    pins = (red_inner, red_proj, red_outer, squares)
    for turn in range(2, len(twos)):
        chains = [step_on(at, turn, chains[at], *pins) for at in range(2)]
        pins = ()
    qkv_total = over_pairs(jnp.concatenate(chains[::-1], axis=-1), small)
    qkv_other = swap(qkv_total, "seq", 1)
    red_qkv = by_core(qkv_total, qkv_other, 1)

    squares = squares + squares_of([(qkv_total, qkv_other)])
    place = lax.broadcasted_iota(jnp.int32, small.shape, 0) * LANES
    place = place + lax.broadcasted_iota(jnp.int32, small.shape, 1)
    small = sum_everywhere(jnp.where(place == count, squares, small), "dp").reshape(-1)
    gain_all = small[: 2 * width].reshape(2, width)
    red_gains = lax.dynamic_slice_in_dim(gain_all, lax.axis_index("dp") * own_rows, own_rows, 1)
    red_mixes = small[2 * width : count].reshape(mixes.shape)
    grad_norm = jnp.sqrt(
        small[count] + jnp.sum(gain_all * gain_all) + jnp.sum(red_mixes * red_mixes)
    )
    factor = CLIP / jnp.maximum(grad_norm, CLIP)
    clipped_gains = red_gains * factor
    new = adamw_all(
        factor[None],
        (red_qkv, red_proj, red_inner, red_outer, red_gains, red_mixes),
        (
            (qkv_weight, qkv_first, qkv_second, qkv_average),
            (proj_weight, proj_first, proj_second, proj_average),
            (inner_weight, inner_first, inner_second, inner_average),
            (outer_weight, outer_first, outer_second, outer_average),
            (gains, gain_first, gain_second, gain_average),
            (mixes, mix_first, mix_second, mix_average),
        ),
    )
    return (
        output,
        grad_rows_tokens,
        grad_norm,
        *new,
        clipped_gains,
    )


def solution(mesh):
    rows = P("dp", "seq", None)
    matrix = P("dp", None)
    vector = P(None, "dp")
    in_specs = (rows, rows, P("dp")) + (matrix,) * 16 + (vector,) * 4 + (P(),) * 4
    out_specs = (rows, rows, P()) + (matrix,) * 16 + (vector,) * 4 + (P(),) * 4 + (vector,)
    return jax.shard_map(
        on_device, mesh=mesh, in_specs=in_specs, out_specs=out_specs, check_vma=False
    )
```

```python
from functools import partial
import math

import jax
import jax.numpy as jnp
from jax import lax
from jax.experimental import pallas as pl
from jax.experimental.pallas import tpu as pltpu
from jax.sharding import PartitionSpec as P

STEP = 10

NORM_EPS = 1e-06
BETA = 0.5
ADAM_EPS = 1e-08
DECAY = 0.01
EMA_KEEP = 0.8
CLIP = 1.0

BF = jnp.bfloat16
F32 = jnp.float32
ROWS = 128
KEYS = 256
GROUP = 16
LANES = 128
FLOPS = (60 * 10**9, 1)
SIDE = {1: 8, 2: 8, 3: 8, 4: 8}
SIDE_BACK = {1: 4, 2: 4, 3: 2, 4: 2}
NT = (((1,), (1,)), ((), ()))
NN = (((1,), (0,)), ((), ()))
TN = (((0,), (0,)), ((), ()))


def dot(left, right, dims=NN):
    return lax.dot_general(left, right, dims, preferred_element_type=F32)


def inverse_rms(values):
    return lax.rsqrt(jnp.mean(values * values, axis=-1, keepdims=True) + NORM_EPS)


def rms_backward(scale_inv, normed, grad_normed):
    return scale_inv * (
        grad_normed - normed * jnp.mean(normed * grad_normed, axis=-1, keepdims=True)
    )


def adamw(weight, first, second, average, grad, rate):
    first_new = BETA * first + (1.0 - BETA) * grad
    second_new = BETA * second + (1.0 - BETA) * grad * grad
    fix = 1.0 - BETA**STEP
    weight_new = weight - rate * (
        first_new / fix / (jnp.sqrt(second_new / fix) + ADAM_EPS) + DECAY * weight
    )
    average_new = EMA_KEEP * average + (1.0 - EMA_KEEP) * weight_new
    return (first_new, second_new, weight_new, average_new)


def swap(value, axis, mask):
    size = lax.axis_size(axis)
    return lax.ppermute(value, axis, [(i, i ^ mask) for i in range(size)])


def digits_of(size):
    found = []
    stride = 1
    while stride < size:
        radix = 2 if stride == 1 or size // stride < 4 else 4
        found.append((stride, radix))
        stride *= radix
    return found


def gather_steps(size):
    steps = []
    while size > 1:
        size //= 2
        steps.append(size)
    return steps


def own_order(shards, axis):
    size = shards.shape[0]
    order = jnp.bitwise_xor(jnp.arange(size, dtype=jnp.int32), lax.axis_index(axis))
    return shards.at[order].get(mode="promise_in_bounds")


def join_pieces(pieces, axis):
    place = {}
    for _, offs in pieces:
        for off in offs:
            place[off] = len(place)
    spots = jnp.array([place[off] for off in range(len(place))], jnp.int32)
    order = jnp.bitwise_xor(jnp.arange(len(place), dtype=jnp.int32), lax.axis_index(axis))
    whole = jnp.concatenate([piece for piece, _ in pieces])
    return whole.at[spots.at[order].get(mode="promise_in_bounds")].get(mode="promise_in_bounds")


def split_blocks(blocks, axis, digits, digit):
    stride, radix = digit
    place = digits.index(digit)
    mine = (lax.axis_index(axis) // stride) % radix
    parts = [
        lax.dynamic_index_in_dim(blocks, jnp.bitwise_xor(mine, k), place, False)
        for k in range(radix)
    ]
    return parts, [d for d in digits if d != digit]


def join_blocks(parts, axis, digit, *first):
    stride, radix = digit
    got = tuple(swap(parts[k], axis, k * stride) for k in range(1, radix))
    if first:
        got = after(got, *first)
    total = parts[0].astype(F32)
    for part in got:
        total = total + part.astype(F32)
    return total


def sum_everywhere(value, axis):
    size = lax.axis_size(axis)
    stride = 1
    while stride < size:
        radix = min(8, size // stride)
        parts = [value] + [swap(value, axis, k * stride) for k in range(1, radix)]
        while len(parts) > 1:
            parts = [parts[i] + parts[i + 1] for i in range(0, len(parts), 2)]
        value = parts[0]
        stride *= radix
    return value


def after(value, *first):
    return lax.optimization_barrier((value,) + first)[0]


def spread_kernel(mixes, pre, post, pre_back, post_back):
    heads = mixes.shape[1]
    tall = heads * GROUP
    wide = (lax.broadcasted_iota(jnp.int32, (tall, heads), 0) // GROUP) == (
        lax.broadcasted_iota(jnp.int32, (tall, heads), 1)
    )
    wide = wide.astype(F32)
    row = lax.broadcasted_iota(jnp.int32, (tall, tall), 0)
    col = lax.broadcasted_iota(jnp.int32, (tall, tall), 1)
    same = row % GROUP == col % GROUP

    def exact(left, right, dims):
        return lax.dot_general(
            left, right, dims, precision=lax.Precision.HIGHEST, preferred_element_type=F32
        )

    for which, (turned, straight) in enumerate(((pre, pre_back), (post, post_back))):
        matrix = mixes[which]
        for out, dims in ((straight, NN), (turned, NT)):
            tallest = exact(wide, matrix, dims)
            full = jnp.where(same, exact(tallest, wide, NT), 0.0)
            high = full.astype(BF)
            out[:tall, :] = high
            out[tall:, :] = (full - high.astype(F32)).astype(BF)


def spread(mixes):
    tall = mixes.shape[1] * GROUP
    return pl.pallas_call(
        spread_kernel,
        out_shape=[jax.ShapeDtypeStruct((2 * tall, tall), BF)] * 4,
        name="spread",
    )(mixes)


def two_heads(rows, first, second):
    return jnp.concatenate([rows * first, rows * second], 0)


def mix(matrix, values):
    out = dot(matrix, values)
    half = matrix.shape[0] // 2
    return out[:half] + out[half:]


def head_masks(scaling):
    lane = lax.broadcasted_iota(jnp.int32, (1, LANES), 1)
    low = lane < LANES // 2
    return low, jnp.where(low, scaling, 0.0).astype(BF), jnp.where(low, 0.0, scaling).astype(BF)


def fill_sequence(meta, sources, qkv, sems):
    copies = []
    for d, source in enumerate(sources):
        start = pl.multiple_of(jnp.bitwise_xor(meta[1], d) * KEYS, KEYS)
        copies.append(pltpu.make_async_copy(source, qkv.at[pl.ds(start, KEYS)], sems.at[d]))
    for copy in copies:
        copy.start()
    for copy in copies:
        copy.wait()


def forward_kernel(meta, *refs):
    sources, (pre, post, attended, probs, weights, qkv, held, sems) = refs[:4], refs[4:]
    heads = probs.shape[0]
    width = attended.shape[1]
    pairs = heads // 2
    tall = heads * GROUP
    step = pl.program_id(0)
    pl.when(step == 0)(partial(fill_sequence, meta, sources, qkv, sems))
    length = meta[0]
    row0 = pl.multiple_of(step * KEYS + meta[2] * ROWS, ROWS)
    chunks = (jnp.minimum(row0 + ROWS, length) + KEYS - 1) // KEYS
    low, first_s, second_s = head_masks(1.0 / math.sqrt(width // heads))

    def score(kc, carry):
        k0 = pl.multiple_of(kc * KEYS, KEYS)
        for p in range(pairs):
            at = p * LANES
            queries = two_heads(qkv[pl.ds(row0, ROWS), at : at + LANES], first_s, second_s)
            keys = qkv[pl.ds(k0, KEYS), width + at : width + at + LANES]
            scores = dot(queries, keys, NT).astype(BF)
            weights[2 * p : 2 * p + 2, :, pl.ds(k0, KEYS)] = scores.reshape(2, ROWS, KEYS)
        return carry

    lax.fori_loop(0, chunks, score, 0)

    def group(n, batch, carry):
        side = SIDE[n]
        rows = [
            pl.ds(pl.multiple_of((batch * side + u) * GROUP, GROUP), GROUP) for u in range(side)
        ]
        col_at = lax.broadcasted_iota(jnp.int32, (GROUP, KEYS), 1)
        row_at = lax.broadcasted_iota(jnp.int32, (GROUP, KEYS), 0)
        peak = [None] * side
        total = [None] * side
        for kc in range(n):
            cols = slice(kc * KEYS, (kc + 1) * KEYS)
            for u in range(side):
                mixed = mix(pre[...], weights[:, rows[u], cols].reshape(tall, KEYS))
                key_pos = col_at + kc * KEYS
                query_pos = row0 + (batch * side + u) * GROUP + row_at
                allowed = (key_pos <= query_pos) & (key_pos < length)
                mixed = jnp.where(allowed[None], mixed.reshape(heads, GROUP, KEYS), -1e30)
                mixed = mixed.reshape(tall, KEYS)
                held[u, :, cols] = mixed
                part = jnp.maximum(mixed[:, :LANES], mixed[:, LANES:])
                peak[u] = part if kc == 0 else jnp.maximum(peak[u], part)
        top = [jnp.max(peak[u], axis=1, keepdims=True) for u in range(side)]
        for kc in range(n):
            cols = slice(kc * KEYS, (kc + 1) * KEYS)
            for u in range(side):
                shifted = jnp.exp(held[u, :, cols] - top[u])
                held[u, :, cols] = shifted
                part = shifted[:, :LANES] + shifted[:, LANES:]
                total[u] = part if kc == 0 else total[u] + part
        inverse = [1.0 / jnp.sum(total[u], axis=1, keepdims=True) for u in range(side)]
        for kc in range(n):
            cols = slice(kc * KEYS, (kc + 1) * KEYS)
            for u in range(side):
                low_probs = (held[u, :, cols] * inverse[u]).astype(BF)
                probs[:, rows[u], cols] = low_probs.reshape(heads, GROUP, KEYS)
                mixed = mix(post[...], low_probs).astype(BF)
                weights[:, rows[u], cols] = mixed.reshape(heads, GROUP, KEYS)
        return carry

    def rest(n):
        lax.fori_loop(0, ROWS // GROUP // SIDE[n], partial(group, n), 0)
        for p in range(pairs):
            at = p * LANES
            pair = weights[2 * p : 2 * p + 2, :, : n * KEYS].reshape(2 * ROWS, n * KEYS)
            out = dot(pair, qkv[: n * KEYS, 2 * width + at : 2 * width + at + LANES])
            attended[:, at : at + LANES] = jnp.where(low, out[:ROWS], out[ROWS:]).astype(BF)

    for n in range(1, probs.shape[2] // KEYS + 1):
        pl.when(chunks == n)(partial(rest, n))


def backward_kernel(meta, *refs):
    sources, refs = refs[:4], refs[4:]
    grad_rows, pre, post, probs, weights, stay, away, grad_pre, grad_post = refs[:9]
    qkv, scores, grads, held, grad_qkv, sum_pre, sum_post, sems = refs[9:]
    heads = probs.shape[0]
    width = grad_rows.shape[1]
    pairs = heads // 2
    tall = heads * GROUP
    step = pl.program_id(0)
    me = meta[1]

    @pl.when(step == 0)
    def _():
        grad_qkv[...] = jnp.zeros_like(grad_qkv)
        sum_pre[...] = jnp.zeros_like(sum_pre)
        sum_post[...] = jnp.zeros_like(sum_post)
        fill_sequence(meta, sources, qkv, sems)

    length = meta[0]
    row0 = pl.multiple_of(step * KEYS + meta[2] * ROWS, ROWS)
    chunks = (jnp.minimum(row0 + ROWS, length) + KEYS - 1) // KEYS
    chunks = jnp.where(row0 < length, chunks, 0)
    scaling = 1.0 / math.sqrt(width // heads)
    low, first_s, second_s = head_masks(scaling)
    low, first_one, second_one = head_masks(1.0)
    lanes = pl.ds(pl.multiple_of(meta[2] * ROWS, ROWS), ROWS)

    def slot_of(home):
        d = jnp.bitwise_xor(me, home)
        return 2 * jnp.bitwise_and(d, 1) + d // 2


    def score(kc, carry):
        k0 = pl.multiple_of(kc * KEYS, KEYS)
        for p in range(pairs):
            at = p * LANES
            queries = two_heads(qkv[pl.ds(row0, ROWS), at : at + LANES], first_s, second_s)
            grad = two_heads(grad_rows[:, at : at + LANES], first_one, second_one)
            keys = qkv[pl.ds(k0, KEYS), width + at : width + at + LANES]
            values = qkv[pl.ds(k0, KEYS), 2 * width + at : 2 * width + at + LANES]
            both = slice(2 * p, 2 * p + 2)
            cols = pl.ds(k0, KEYS)
            scores[both, :, cols] = dot(queries, keys, NT).astype(BF).reshape(2, ROWS, KEYS)
            grads[both, :, cols] = dot(grad, values, NT).astype(BF).reshape(2, ROWS, KEYS)
        return carry

    lax.fori_loop(0, chunks, score, 0)

    def group(n, batch, carry):
        side = SIDE_BACK[n]
        rows = [
            pl.ds(pl.multiple_of((batch * side + u) * GROUP, GROUP), GROUP) for u in range(side)
        ]
        span = slice(0, n * KEYS)
        total = [None] * side
        for kc in range(n):
            cols = slice(kc * KEYS, (kc + 1) * KEYS)
            for u in range(side):
                grad_probs = mix(post[...], grads[:, rows[u], cols].reshape(tall, KEYS))
                held[u, :, cols] = grad_probs
                term = probs[:, rows[u], cols].reshape(tall, KEYS).astype(F32) * grad_probs
                part = term[:, :LANES] + term[:, LANES:]
                total[u] = part if kc == 0 else total[u] + part
        added = None
        for u in range(side):
            left = probs[:, rows[u], span].reshape(tall, n * KEYS)
            term = dot(left, grads[:, rows[u], span].reshape(tall, n * KEYS), NT)
            added = term if u == 0 else added + term
        sum_post[...] += added
        delta = [jnp.sum(total[u], axis=1, keepdims=True) for u in range(side)]
        mixed = [[] for _ in range(side)]
        for kc in range(n):
            cols = slice(kc * KEYS, (kc + 1) * KEYS)
            for u in range(side):
                prob = probs[:, rows[u], cols].reshape(tall, KEYS).astype(F32)
                grad_mixed = (prob * (held[u, :, cols] - delta[u])).astype(BF)
                mixed[u].append(grad_mixed)
                back = mix(pre[...], grad_mixed).astype(BF)
                grads[:, rows[u], cols] = back.reshape(heads, GROUP, KEYS)
        added = None
        for u in range(side):
            left = scores[:, rows[u], span].reshape(tall, n * KEYS)
            term = dot(left, jnp.concatenate(mixed[u], 1), NT)
            added = term if u == 0 else added + term
        sum_pre[...] += added
        return carry

    def rest(n):
        lax.fori_loop(0, ROWS // GROUP // SIDE_BACK[n], partial(group, n), 0)
        for p in range(pairs):
            at = p * LANES
            mine = slice(at, at + LANES)
            both = slice(2 * p, 2 * p + 2)
            queries = two_heads(qkv[pl.ds(row0, ROWS), mine], first_s, second_s).T
            grad = two_heads(grad_rows[:, mine], first_one, second_one).T
            back = grads[both, :, : n * KEYS].reshape(2 * ROWS, n * KEYS)
            out = dot(back, qkv[: n * KEYS, width + at : width + at + LANES])
            out = jnp.where(low, out[:ROWS], out[ROWS:]) * scaling
            grad_qkv[slot_of(step), mine, lanes] = out.T
            for kc in range(n):
                cols = slice(kc * KEYS, (kc + 1) * KEYS)
                to = slot_of(kc)
                grad_qkv[to, width + at : width + at + LANES, :] += dot(
                    queries, grads[both, :, cols].reshape(2 * ROWS, KEYS)
                )
                grad_qkv[to, 2 * width + at : 2 * width + at + LANES, :] += dot(
                    grad, weights[both, :, cols].reshape(2 * ROWS, KEYS)
                )

    for n in range(1, probs.shape[2] // KEYS + 1):
        pl.when(chunks == n)(partial(rest, n))

    @pl.when(step == pl.num_programs(0) - 1)
    def _():
        stay[...] = grad_qkv[:2]
        away[...] = grad_qkv[2:].astype(BF)
        row = lax.broadcasted_iota(jnp.int32, (tall, tall), 0)
        col = lax.broadcasted_iota(jnp.int32, (tall, tall), 1)
        same = row % GROUP == col % GROUP
        pick = (
            lax.broadcasted_iota(jnp.int32, (tall, LANES), 0) // GROUP
            == lax.broadcasted_iota(jnp.int32, (tall, LANES), 1)
        ).astype(F32)
        for source, out in ((sum_pre, grad_pre), (sum_post, grad_post)):
            kept = jnp.where(same, source[...], 0.0)
            wide = lax.dot_general(
                kept, pick, NN, precision=lax.Precision.HIGHEST, preferred_element_type=F32
            )
            for head in range(heads):
                out[head : head + 1, :] = jnp.sum(
                    wide[head * GROUP : (head + 1) * GROUP], axis=0, keepdims=True
                )


ANY = pl.BlockSpec(memory_space=pl.ANY)


def is_live(step, meta):
    return step * KEYS + meta[2] * ROWS < meta[0]


def attend(meta, sources, pre, post, heads, flops):
    width = sources[0].shape[1] // 3
    tall = heads * GROUP
    steps = 4
    full_len = steps * KEYS
    matrix = pl.BlockSpec((2 * tall, tall), lambda i, m: (0, 0), pipeline_mode=pl.Buffered(1))
    wide = pl.BlockSpec(
        (None, heads, ROWS, full_len), lambda i, m: (jnp.where(is_live(i, m), i, steps), 0, 0, 0)
    )
    kept = jax.ShapeDtypeStruct((steps + 1, heads, ROWS, full_len), BF)
    return pl.pallas_call(
        forward_kernel,
        grid_spec=pltpu.PrefetchScalarGridSpec(
            num_scalar_prefetch=1,
            grid=(steps,),
            in_specs=[ANY] * 4 + [matrix, matrix],
            out_specs=[
                pl.BlockSpec((None, ROWS, width), lambda i, m: (jnp.bitwise_xor(i, m[1]), 0, 0)),
                wide,
                wide,
            ],
            scratch_shapes=[
                pltpu.VMEM((full_len, 3 * width), BF),
                pltpu.VMEM((8, tall, full_len), F32),
                pltpu.SemaphoreType.DMA((4,)),
            ],
        ),
        out_shape=[jax.ShapeDtypeStruct((steps, ROWS, width), BF), kept, kept],
        compiler_params=pltpu.CompilerParams(vmem_limit_bytes=56 * 2**20),
        cost_estimate=pl.CostEstimate(
            flops=flops, bytes_accessed=1, transcendentals=0
        ),
        name="attend",
    )(meta, *sources, pre, post)


def attend_back(meta, sources, grad_rows, pre, post, probs, weights, flops):
    width = sources[0].shape[1] // 3
    steps = 4
    heads = probs.shape[1]
    tall = heads * GROUP
    full_len = steps * KEYS

    def newest(step, meta):
        last = 0
        for other in range(1, steps):
            last = jnp.where(is_live(other, meta), other, last)
        return jnp.minimum(step, last)

    matrix = pl.BlockSpec((2 * tall, tall), lambda i, m: (0, 0), pipeline_mode=pl.Buffered(1))
    wide = pl.BlockSpec((None, heads, ROWS, full_len), lambda i, m: (newest(i, m), 0, 0, 0))
    rows = pl.BlockSpec((None, ROWS, width), lambda i, m: (jnp.bitwise_xor(i, m[1]), 0, 0))
    small = pl.BlockSpec((heads, LANES), lambda i, m: (0, 0))
    pairs = pl.BlockSpec(
        (2, 3 * width, KEYS), lambda i, m: (0, 0, 0), pipeline_mode=pl.Buffered(1)
    )
    return pl.pallas_call(
        backward_kernel,
        grid_spec=pltpu.PrefetchScalarGridSpec(
            num_scalar_prefetch=1,
            grid=(steps,),
            in_specs=[ANY] * 4 + [rows, matrix, matrix, wide, wide],
            out_specs=[
                pairs,
                pairs,
                small,
                small,
            ],
            scratch_shapes=[
                pltpu.VMEM((full_len, 3 * width), BF),
                pltpu.VMEM((heads, ROWS, full_len), BF),
                pltpu.VMEM((heads, ROWS, full_len), BF),
                pltpu.VMEM((4, tall, full_len), F32),
                pltpu.VMEM((4, 3 * width, KEYS), F32),
                pltpu.VMEM((tall, tall), F32),
                pltpu.VMEM((tall, tall), F32),
                pltpu.SemaphoreType.DMA((4,)),
            ],
        ),
        out_shape=[
            jax.ShapeDtypeStruct((2, 3 * width, KEYS), F32),
            jax.ShapeDtypeStruct((2, 3 * width, KEYS), BF),
            jax.ShapeDtypeStruct((heads, LANES), F32),
            jax.ShapeDtypeStruct((heads, LANES), F32),
        ],
        compiler_params=pltpu.CompilerParams(vmem_limit_bytes=60 * 2**20),
        cost_estimate=pl.CostEstimate(
            flops=flops, bytes_accessed=1, transcendentals=0
        ),
        name="attend_back",
    )(meta, *sources, grad_rows, pre, post, probs, weights)


def gelu_both(value):
    scale = math.sqrt(2.0 / math.pi)
    square = value * value
    bent = jnp.tanh(scale * (value + 0.044715 * (square * value)))
    share = 0.5 * (1.0 + bent)
    slope = share + 0.5 * value * (1.0 - bent * bent) * (
        scale * (1.0 + 3.0 * 0.044715 * square)
    )
    return value * share, slope


def fill_weights(meta, sources, offs, inner, outer, proj, sems):
    hidden = inner.shape[1] // 2
    width = proj.shape[0]
    half = width // 2
    late, early = [], []

    def copy(source, target, kind=None):
        sem = sems.at[len(late) + len(early)]
        (late if kind is None else early).append(pltpu.make_async_copy(source, target, sem))

    count = len(sources) // 2
    for side in range(2):
        lanes = jnp.bitwise_xor(meta[1], side) * half
        to_proj = pl.ds(pl.multiple_of(lanes, LANES), half)
        to_inner = slice(side * hidden, (side + 1) * hidden)
        here = sources[count * side : count * side + count]
        if offs is None:
            copy(here[0], inner.at[:, to_inner])
            copy(here[1], proj.at[:, to_proj], 1)
            copy(here[2], outer.at[to_inner])
            continue
        own_rows = here[0].shape[1]
        folds = hidden * own_rows // width // own_rows
        for source, owners in zip(here, offs):
            for at_source, off in enumerate(owners):
                block = source.at[at_source]
                owner = jnp.bitwise_xor(meta[0], off)
                rows = pl.ds(pl.multiple_of(owner * own_rows, own_rows), own_rows)
                copy(block.at[:, :hidden], inner.at[rows, to_inner])
                copy(block.at[:, hidden : hidden + half], proj.at[rows, to_proj], 1)
                for fold in range(folds):
                    start = side * hidden + (owner * folds + fold) * own_rows
                    at = hidden + half + fold * width
                    copy(
                        block.at[:, at : at + width],
                        outer.at[pl.ds(pl.multiple_of(start, own_rows), own_rows)],
                    )
    for one in early + late:
        one.start()
    return early, late


TILE = 256
CHUNK = 512


def feed_kernel(offs, meta, gains, tokens, attended, grad_out, *refs):
    count = len(refs) - 17
    sources, refs = refs[:count], refs[count:]
    output, grad_resid, resid_low, grad_attended, gain_two, second_in = refs[:6]
    active, grad_hidden = refs[6:8], refs[8:10]
    inner, outer, proj, resid, out_sum, grad_sum, sems = refs[10:]
    rows = tokens.shape[0]
    step = pl.program_id(0)
    tiles = [slice(at, at + TILE) for at in range(0, rows, TILE)]

    @pl.when(step == 0)
    def _():
        early, late = fill_weights(meta, sources, offs, inner, outer, proj, sems)
        for one in early:
            one.wait()
        for tile in tiles:
            seq = meta[2 + tile.start // TILE]
            value = tokens[pl.ds(pl.multiple_of(seq * TILE, TILE), TILE)].astype(F32)
            value = value + dot(attended[tile], proj[...])
            resid[tile] = value
            out_sum[tile] = value
            grad_sum[tile] = jnp.zeros_like(value)
            second_in[tile] = (value * inverse_rms(value) * gains[1:2]).astype(BF)
        for one in late:
            one.wait()

    cols = pl.ds(pl.multiple_of(step * CHUNK, CHUNK), CHUNK)
    for tile in tiles:
        up = inner[:, cols]
        down = outer[cols]
        value, slope = gelu_both(dot(second_in[tile], up))
        value = value.astype(BF)
        back = (dot(grad_out[tile], down, NT) * slope).astype(BF)
        for side in range(2):

            @pl.when((step * 2 >= pl.num_programs(0)) == (side == 1))
            def _():
                active[side][tile] = value
                grad_hidden[side][tile] = back

        out_sum[tile] += dot(value, down)
        grad_sum[tile] += dot(back, up, NT)

    @pl.when(step == pl.num_programs(0) - 1)
    def _():
        gain_sum = jnp.zeros((8, proj.shape[0]), F32)
        for tile in tiles:
            seq = meta[2 + tile.start // TILE]
            output[pl.ds(pl.multiple_of(seq * TILE, TILE), TILE)] = out_sum[tile].astype(BF)
            value = resid[tile]
            scale = inverse_rms(value)
            normed = value * scale
            grad = grad_sum[tile]
            gain_sum += jnp.sum((grad * normed).reshape(TILE // 8, 8, -1), axis=0)
            back = grad_out[tile].astype(F32) + rms_backward(scale, normed, grad * gains[1:2])
            grad_resid[tile] = back
            back = back.astype(BF)
            resid_low[tile] = back
            grad_attended[tile] = dot(back, proj[...], NT).astype(BF)
        gain_two[...] = gain_sum


def feed_forward(meta, gains, tokens, attended, grad_out, sources, offs, hidden):
    rows, width = tokens.shape
    copies = 6
    if offs is not None:
        owners = sum(len(o) for o in offs)
        copies = 2 * owners * (2 + hidden // 2 // width)
    chunks = hidden // CHUNK

    def whole(shape):
        return pl.BlockSpec(shape, lambda c, m: (0,) * len(shape), pipeline_mode=pl.Buffered(1))

    flat = whole((rows, width))
    first = pl.BlockSpec((rows, CHUNK), lambda c, m: (0, jnp.minimum(c, chunks // 2 - 1)))
    second = pl.BlockSpec((rows, CHUNK), lambda c, m: (0, jnp.maximum(c - chunks // 2, 0)))
    wide = jax.ShapeDtypeStruct((rows, hidden // 2), BF)
    return pl.pallas_call(
        partial(feed_kernel, offs),
        grid_spec=pltpu.PrefetchScalarGridSpec(
            num_scalar_prefetch=1,
            grid=(chunks,),
            in_specs=[whole((2, width)), flat, flat, flat] + [ANY] * len(sources),
            out_specs=[flat, flat, flat, flat, whole((8, width)), flat, first, second, first, second],
            scratch_shapes=[
                pltpu.VMEM((width, hidden), BF),
                pltpu.VMEM((hidden, width), BF),
                pltpu.VMEM((width, width), BF),
                pltpu.VMEM((rows, width), F32),
                pltpu.VMEM((rows, width), F32),
                pltpu.VMEM((rows, width), F32),
                pltpu.SemaphoreType.DMA((copies,)),
            ],
        ),
        out_shape=[
            jax.ShapeDtypeStruct((rows, width), BF),
            jax.ShapeDtypeStruct((rows, width), F32),
            jax.ShapeDtypeStruct((rows, width), BF),
            jax.ShapeDtypeStruct((rows, width), BF),
            jax.ShapeDtypeStruct((8, width), F32),
            jax.ShapeDtypeStruct((rows, width), BF),
            wide,
            wide,
            wide,
            wide,
        ],
        compiler_params=pltpu.CompilerParams(vmem_limit_bytes=56 * 2**20),
        cost_estimate=pl.CostEstimate(
            flops=22 * 10**9, bytes_accessed=40 * 10**6, transcendentals=0
        ),
        name="feed_forward",
    )(meta, gains, tokens, attended, grad_out, *sources)


def weight_kernel(meta, second_in, attended, resid_low, grad_out, active, back, first, last, turned):
    width = second_in.shape[1]
    half = width // 2
    step = pl.program_id(0)

    @pl.when(step == 0)
    def _():
        turned[...] = second_in[...].T
        lanes = pl.ds(pl.multiple_of(meta[0] * half, LANES), half)
        hidden = first.shape[1] - half
        first[:, hidden:] = dot(attended[...], resid_low[:, lanes], TN).astype(first.dtype)

    cols = pl.ds(pl.multiple_of(step * CHUNK, CHUNK), CHUNK)
    first[:, cols] = dot(turned[...], back[...]).astype(first.dtype)
    last[...] = dot(active[...], grad_out[...], TN).astype(last.dtype)


def weight_sums(which, second_in, attended, resid_low, grad_out, active, back, kind):
    rows, width = second_in.shape
    hidden = active.shape[1]

    def whole(shape):
        return pl.BlockSpec(shape, lambda c, m: (0, 0), pipeline_mode=pl.Buffered(1))

    flat = whole((rows, width))
    chunk = pl.BlockSpec((rows, CHUNK), lambda c, m: (0, c))
    return pl.pallas_call(
        weight_kernel,
        grid_spec=pltpu.PrefetchScalarGridSpec(
            num_scalar_prefetch=1,
            grid=(hidden // CHUNK,),
            in_specs=[flat] * 4 + [chunk, chunk],
            out_specs=[
                whole((width, hidden + width // 2)),
                pl.BlockSpec((CHUNK, width), lambda c, m: (c, 0)),
            ],
            scratch_shapes=[pltpu.VMEM((width, rows), BF)],
        ),
        out_shape=[
            jax.ShapeDtypeStruct((width, hidden + width // 2), kind),
            jax.ShapeDtypeStruct((hidden, width), kind),
        ],
        compiler_params=pltpu.CompilerParams(vmem_limit_bytes=56 * 2**20),
        cost_estimate=pl.CostEstimate(flops=1, bytes_accessed=1, transcendentals=0),
        name="weight_sums",
    )(which, second_in, attended, resid_low, grad_out, active, back)


def squares_kernel(*refs):
    pairs, out = refs[:-1], refs[-1]
    total = jnp.zeros((8, LANES), F32)
    for at in range(0, len(pairs), 2):
        both = []
        for ref in pairs[at : at + 2]:
            rows, cols = ref.shape
            part = jnp.zeros((8, LANES), F32)
            value = ref[...]
            value = value * value
            value = jnp.sum(value.reshape(rows // 8, 8, cols), axis=0)
            for lane in range(0, cols, LANES):
                part = part + value[:, lane : lane + LANES]
            both.append(part)
        total = total + (both[0] + both[1])
    out[...] = total


def assemble_kernel(piece, meta, mine, other, last_mine, last_other, inner, proj, outer, out):
    squares_kernel(mine, other, last_mine, last_other, out)
    first = meta[0] == 0
    width = proj.shape[1]
    cut = inner.shape[1] // 2
    for which, (left, right) in enumerate(((mine, other), (other, mine))):

        @pl.when(first == (which == 0))
        def _():
            proj[:, : width // 2] = left[:, cut:]
            proj[:, width // 2 :] = right[:, cut:]
            for at in range(0, cut, piece):
                cols = slice(at, at + piece)
                inner[:, 2 * at : 2 * at + 2 * piece] = jnp.concatenate(
                    [left[:, cols], right[:, cols]], axis=1
                )

    for which, (left, right) in enumerate(((last_mine, last_other), (last_other, last_mine))):

        @pl.when(first == (which == 0))
        def _():
            rows = left.shape[0]
            outer[:rows] = left[...]
            outer[rows:] = right[...]


def assemble(core, piece, halves, last_halves):
    rows, wide = halves[0].shape
    last_rows, width = last_halves[0].shape
    vmem = pl.BlockSpec(memory_space=pltpu.VMEM)
    *found, squares = pl.pallas_call(
        partial(assemble_kernel, piece),
        in_specs=[pl.BlockSpec(memory_space=pltpu.SMEM)] + [vmem] * 4,
        out_specs=[vmem] * 4,
        out_shape=[
            jax.ShapeDtypeStruct((rows, 2 * wide - width), F32),
            jax.ShapeDtypeStruct((rows, width), F32),
            jax.ShapeDtypeStruct((2 * last_rows, width), F32),
            jax.ShapeDtypeStruct((8, LANES), F32),
        ],
        cost_estimate=pl.CostEstimate(flops=1, bytes_accessed=1, transcendentals=0),
        compiler_params=pltpu.CompilerParams(vmem_limit_bytes=40 * 2**20),
        name="assemble",
    )(core[None], *halves, *last_halves)
    return *found, jnp.sum(squares)


def squares_of(pairs):
    if any(v.shape[0] % 8 for pair in pairs for v in pair):
        found = [jnp.sum(a * a) + jnp.sum(b * b) for a, b in pairs]
        return sum(found[1:], found[0])
    vmem = pl.BlockSpec(memory_space=pltpu.VMEM)
    flat = [v for pair in pairs for v in pair]
    out = pl.pallas_call(
        squares_kernel,
        in_specs=[vmem] * len(flat),
        out_specs=vmem,
        out_shape=jax.ShapeDtypeStruct((8, LANES), F32),
        cost_estimate=pl.CostEstimate(flops=1, bytes_accessed=1, transcendentals=0),
        compiler_params=pltpu.CompilerParams(vmem_limit_bytes=40 * 2**20),
        name="squares",
    )(*flat)
    return jnp.sum(out)


RATES = (0.03, 0.1, 0.03, 0.02, 0.3)


def adamw_kernel(factor, *refs):
    count = len(RATES)
    grads, states, outs = refs[:count], refs[count : 5 * count], refs[5 * count :]

    def update(at):
        scaled = grads[at][...] * factor[0]
        new = adamw(*[r[...] for r in states[4 * at : 4 * at + 4]], scaled, RATES[at])
        for out, value in zip(outs[4 * at : 4 * at + 4], new):
            out[...] = value

    for at in range(4):
        update(at)

    @pl.when(pl.program_id(0) == 0)
    def _():
        for at in range(4, count):
            update(at)


def adamw_all(factor, grads, states):
    steps = 6

    def block(at, shape):
        if at >= 4:
            return pl.BlockSpec(shape, lambda i: (0,) * len(shape))
        if at == 3:
            return pl.BlockSpec((shape[0] // steps, shape[1]), lambda i: (i, 0))
        return pl.BlockSpec((shape[0], shape[1] // steps), lambda i: (0, i))

    specs = [block(at, g.shape) for at, g in enumerate(grads)]
    wide = [s for s in specs for _ in range(4)]
    out = pl.pallas_call(
        adamw_kernel,
        grid=(steps,),
        in_specs=[pl.BlockSpec(memory_space=pltpu.SMEM)] + specs + wide,
        out_specs=wide,
        out_shape=[jax.ShapeDtypeStruct(g.shape, F32) for g in grads for _ in range(4)],
        compiler_params=pltpu.CompilerParams(vmem_limit_bytes=62 * 2**20),
        name="adamw_all",
    )(factor, *grads, *[v for state in states for v in state])
    return out


def first_kernel(offs, wanted, blocks, meta, tokens, *refs):
    count = 2 * (1 if offs is None else len(offs))
    sources, refs = refs[:count], refs[count:]
    outs, (first_in, gains, weight, mixed, sems) = refs[: len(wanted)], refs[len(wanted) :]
    side = weight.shape[1] // 2
    copies = []

    def copy(source, target):
        copies.append(pltpu.make_async_copy(source, target, sems.at[len(copies)]))

    for which in range(2):
        here = sources[which * (count // 2) : (which + 1) * (count // 2)]
        start = pl.multiple_of(jnp.bitwise_xor(meta[1], which) * side, side)
        if offs is None:
            copy(here[0].at[:, :side], weight.at[:, pl.ds(start, side)])
            if which == 0:
                copy(here[0].at[:, side:], mixed)
            continue
        own_rows = here[0].shape[1]
        for source, owners in zip(here, offs):
            for at, off in enumerate(owners):
                owner = jnp.bitwise_xor(meta[0], off)
                rows = pl.ds(pl.multiple_of(owner * own_rows, own_rows), own_rows)
                copy(source.at[at, :, :side], weight.at[rows, pl.ds(start, side)])
                if which == 0:
                    copy(source.at[at, :, side:], mixed.at[rows])
    for one in copies:
        one.start()
    for one in copies:
        one.wait()
    gain = mixed[...].astype(F32).T[:8]
    gains[...] = gain
    for block in range(blocks):
        value = tokens[meta[2 + block]].astype(F32)
        low = (value * inverse_rms(value) * gain[:1]).astype(BF)
        first_in[block * KEYS : (block + 1) * KEYS] = low
        if block not in wanted:
            continue
        out = outs[wanted.index(block)]
        wide = 2 * side // 3
        for col in range(0, 2 * side, wide):
            cols = slice(col, col + wide)
            out[:, cols] = dot(low, weight[:, cols]).astype(BF)


def first_product(meta, tokens, pieces, offs, wanted, blocks, with_weight):
    width = tokens.shape[2]
    rows = blocks * KEYS
    vmem = pl.BlockSpec(memory_space=pltpu.VMEM)
    out_shape = [
        *[jax.ShapeDtypeStruct((KEYS, 3 * width), BF) for _ in wanted],
        jax.ShapeDtypeStruct((rows, width), BF),
        jax.ShapeDtypeStruct((8, width), F32),
    ]
    scratch = [
        pltpu.VMEM((width, LANES), BF),
        pltpu.SemaphoreType.DMA((3 if offs is None else 3 * sum(len(o) for o in offs),)),
    ]
    if with_weight:
        out_shape.append(jax.ShapeDtypeStruct((width, 3 * width), BF))
    else:
        scratch = [pltpu.VMEM((width, 3 * width), BF)] + scratch
    return pl.pallas_call(
        partial(first_kernel, offs, wanted, blocks),
        in_specs=[pl.BlockSpec(memory_space=pltpu.SMEM), vmem] + [ANY] * len(pieces),
        out_specs=[vmem] * len(out_shape),
        out_shape=out_shape,
        scratch_shapes=scratch,
        compiler_params=pltpu.CompilerParams(vmem_limit_bytes=40 * 2**20),
        cost_estimate=pl.CostEstimate(
            flops=1, bytes_accessed=1, transcendentals=0
        ),
        name="first_product",
    )(meta, tokens, *pieces)


def first_grads_kernel(meta, first_in, *refs):
    cols, (out,) = refs[:-1], refs[-1:]
    side = out.shape[1]
    take = pl.ds(pl.multiple_of(meta[0] * side, side), side)
    total = None
    for block, grads in enumerate(cols):
        rows = first_in[block * KEYS : (block + 1) * KEYS].T
        term = dot(rows, grads[take], NT)
        total = term if block == 0 else total + term
        if block + 1 < len(cols):
            continue
        out[...] = total.astype(out.dtype)


def first_grads(which, first_in, cols, kind):
    width = first_in.shape[1]
    side = cols[0].shape[0] // 2
    vmem = pl.BlockSpec(memory_space=pltpu.VMEM)
    return pl.pallas_call(
        first_grads_kernel,
        in_specs=[pl.BlockSpec(memory_space=pltpu.SMEM)] + [vmem] * (1 + len(cols)),
        out_specs=vmem,
        out_shape=jax.ShapeDtypeStruct((width, side), kind),
        compiler_params=pltpu.CompilerParams(vmem_limit_bytes=50 * 2**20),
        cost_estimate=pl.CostEstimate(
            flops=1, bytes_accessed=1, transcendentals=0
        ),
        name="first_grads",
    )(which, first_in, *cols)


def token_grads_kernel(meta, gains, near, far, weight, tokens, grad_resid, *refs):
    out, gain_out = refs[-2:]
    step = pl.program_id(0)

    @pl.when(step == 0)
    def _():
        gain_out[...] = jnp.zeros_like(gain_out)

    for which, grads in enumerate((near, far)):

        @pl.when(step == which)
        def _():
            back = dot(weight[...], grads[...]).T
            value = tokens[...].astype(F32)
            scale = inverse_rms(value)
            normed = value * scale
            gain_out[...] += jnp.sum((back * normed).reshape(KEYS // 8, 8, -1), axis=0)
            out[...] = grad_resid[...] + rms_backward(scale, normed, back * gains[:1])


def token_grads(slot, seqs, gains, near, far, weight, tokens, grad_resid, before):
    _, rows, width = tokens.shape

    def whole(shape):
        return pl.BlockSpec(shape, lambda i, m: (0,) * len(shape), pipeline_mode=pl.Buffered(1))

    place = pl.BlockSpec((None, rows, width), lambda i, m: (m[i], 0, 0))
    extra = [] if before is None else [before]
    return pl.pallas_call(
        token_grads_kernel,
        grid_spec=pltpu.PrefetchScalarGridSpec(
            num_scalar_prefetch=1,
            grid=(2,),
            in_specs=[
                whole(gains.shape),
                whole(near.shape),
                whole(far.shape),
                whole(weight.shape),
                place,
                pl.BlockSpec((None, rows, width), lambda i, m: (2 * slot + i, 0, 0)),
            ]
            + [ANY] * len(extra),
            out_specs=[place, whole((8, width))],
        ),
        out_shape=[
            jax.ShapeDtypeStruct(tokens.shape, F32),
            jax.ShapeDtypeStruct((8, width), F32),
        ],
        input_output_aliases={7: 0} if extra else {},
        compiler_params=pltpu.CompilerParams(vmem_limit_bytes=50 * 2**20),
        cost_estimate=pl.CostEstimate(
            flops=1, bytes_accessed=1, transcendentals=0
        ),
        name="token_grads",
    )(seqs, gains, near, far, weight, tokens, grad_resid, *extra)


def prepare_kernel(owners, meta, inner, outer, proj, out):
    rows, hidden = inner.shape
    width = proj.shape[1]
    half = width // 2
    piece = hidden // owners // 2
    for core in range(2):

        @pl.when(meta[1] == core)
        def _():
            for owner in range(owners):
                at = (2 * owner + core) * piece
                out[:, owner * piece : (owner + 1) * piece] = inner[:, at : at + piece].astype(BF)
            cut = hidden // 2
            out[:, cut : cut + half] = proj[:, core * half : (core + 1) * half].astype(BF)
            for fold in range(piece // rows):
                at = core * piece + fold * rows
                start = cut + half + fold * width
                out[:, start : start + width] = outer[at : at + rows].astype(BF)


def prepare(meta, owners, inner, outer, proj):
    rows, hidden = inner.shape
    width = proj.shape[1]
    vmem = pl.BlockSpec(memory_space=pltpu.VMEM)
    return pl.pallas_call(
        partial(prepare_kernel, owners),
        in_specs=[pl.BlockSpec(memory_space=pltpu.SMEM)] + [vmem] * 3,
        out_specs=vmem,
        out_shape=jax.ShapeDtypeStruct((rows, hidden + width // 2), BF),
        cost_estimate=pl.CostEstimate(flops=1, bytes_accessed=1, transcendentals=0),
        compiler_params=pltpu.CompilerParams(vmem_limit_bytes=40 * 2**20),
        name="prepare",
    )(meta, inner, outer, proj)


def on_device(
    tokens,
    cotangent,
    lengths,
    qkv_weight,
    qkv_first,
    qkv_second,
    qkv_average,
    proj_weight,
    proj_first,
    proj_second,
    proj_average,
    inner_weight,
    inner_first,
    inner_second,
    inner_average,
    outer_weight,
    outer_first,
    outer_second,
    outer_average,
    gains,
    gain_first,
    gain_second,
    gain_average,
    mixes,
    mix_first,
    mix_second,
    mix_average,
):
    group_seqs, shard_len, width = tokens.shape
    owners = lax.axis_size("dp")
    heads = mixes.shape[1]
    own_rows = qkv_weight.shape[0]
    hidden = inner_weight.shape[1]
    half = width // 2
    slice_ff = hidden // owners // 2
    me = lax.axis_index("seq")
    pair = me // 2
    core = jnp.bitwise_and(me, 1)

    def by_core(mine, other, axis):
        return jnp.where(
            core == 0,
            jnp.concatenate([mine, other], axis),
            jnp.concatenate([other, mine], axis),
        )

    ahead = (lengths[None, :] > lengths[:, None]) | (
        (lengths[None, :] == lengths[:, None])
        & (jnp.arange(group_seqs)[None, :] < jnp.arange(group_seqs)[:, None])
    )
    rank = jnp.sum(ahead.astype(jnp.int32), axis=1)
    def by_rank(place, values):
        return jnp.sum(jnp.where(rank == place, values, 0)).astype(jnp.int32)

    def of_slot(slot, which, values):
        first, second = (0, 1) if slot == 0 else (group_seqs - 1, group_seqs - 2)
        return jnp.where(which == 0, by_rank(first, values), by_rank(second, values))

    def sequence_of(slot, which):
        return of_slot(slot, which, jnp.arange(group_seqs, dtype=jnp.int32))

    def pack(values):
        spot = jnp.arange(len(values), dtype=jnp.int32)
        total = jnp.zeros((len(values),), jnp.int32)
        for at, value in enumerate(values):
            total = jnp.where(spot == at, value, total)
        return total

    def arrange(value):
        return jnp.stack(
            [
                jnp.stack(
                    [
                        lax.dynamic_index_in_dim(
                            value, sequence_of(slot, jnp.bitwise_xor(pair, d)), 0, False
                        )
                        for d in range(2)
                    ]
                )
                for slot in range(2)
            ]
        )

    lengths_here = [[of_slot(s, jnp.bitwise_xor(pair, d), lengths) for d in range(2)] for s in range(2)]
    seqs = [pack([sequence_of(s, pair), sequence_of(s, 1 - pair)]) for s in range(2)]
    feed_meta = pack(
        [lax.axis_index("dp"), core]
        + [sequence_of(s, jnp.bitwise_xor(pair, d)) for s in range(2) for d in range(2)]
    )
    metas = [pack([lengths_here[slot][0], me, core]) for slot in range(2)]

    mixers = spread(mixes)
    positions = me * shard_len + jnp.arange(shard_len, dtype=jnp.int32)
    used = jnp.stack([jnp.stack(found) for found in lengths_here])
    live = positions[None, None, :] < used[:, :, None]
    cot = arrange(cotangent)
    grad_out = jnp.where(live[..., None], cot, jnp.zeros_like(cot))
    folds = slice_ff // own_rows
    if own_rows % 16 == 0:
        rest = prepare(feed_meta, owners, inner_weight, outer_weight, proj_weight)[None]
    else:
        inner_mine = inner_weight.astype(BF).reshape(own_rows, owners, 2, slice_ff)
        inner_mine = lax.dynamic_index_in_dim(inner_mine, core, 2, False)
        outer_mine = outer_weight.astype(BF).reshape(2, folds, own_rows, width)
        outer_mine = lax.dynamic_index_in_dim(outer_mine, core, 0, False)
        rest = jnp.concatenate(
            [
                inner_mine.reshape(own_rows, owners * slice_ff),
                lax.dynamic_slice_in_dim(proj_weight.astype(BF), core * half, half, 1),
            ]
            + [outer_mine[f] for f in range(folds)],
            axis=1,
        )[None]
    side = qkv_weight.shape[1] // 2
    mine = lax.dynamic_slice_in_dim(qkv_weight.astype(BF), core * side, side, 1)
    mine = jnp.concatenate([mine, jnp.pad(gains.astype(BF).T, ((0, 0), (0, LANES - 2)))], 1)
    offs = None
    if owners == 8:
        shard = mine[None]
        got = swap(shard, "dp", 4)
        got = after(got, feed_meta, rest)
        pieces = [jnp.concatenate([shard, got])]
        far_z, far_x = swap(pieces[0], "dp", 2), swap(pieces[0], "dp", 1)
        beside = [swap(pieces[0], "seq", 1)]
        pieces += [far_z, far_x]
        pieces.append(swap(far_z, "dp", 1))
        beside += [swap(p, "seq", 1) for p in pieces[1:]]
        offs = ((0, 4), (2, 6), (1, 5), (3, 7))
        pieces += beside
        late = far_z
    else:
        mine = lax.all_gather(mine, "dp", axis=0, tiled=True)
        pieces = [mine, swap(mine, "seq", 1)]

    if offs is not None:
        got = swap(after(rest, late), "dp", 4)
    place = feed_meta
    near, far, *_ = first_product(
        place, tokens, pieces, offs, (0, 1), 2, False
    )
    near, far = [near], [far]
    here = swap(far[0], "seq", 2)
    beside = swap(near[0], "seq", 1)
    place, beside, mixers, metas, grad_out = lax.optimization_barrier(
        (place, beside, mixers, metas, grad_out)
    )
    pre_mix, post_mix, pre_back, post_back = mixers
    *out, first_in, gain_vals, weight_qkv = first_product(
        place, tokens, pieces, offs, (2, 3), 4, True
    )
    near.append(out[0])
    far.append(out[1])
    here = after(here, far[1], near[1])
    if offs is not None:
        here, got = lax.optimization_barrier((here, got))
        rest_pieces = [jnp.concatenate([rest, got])]
        far_z, far_x = swap(rest_pieces[0], "dp", 2), swap(rest_pieces[0], "dp", 1)
    sources = [[near[0], beside, here, swap(here, "seq", 1)]]
    next_far = swap(after(far[1], here), "seq", 2)
    beside = swap(after(near[1], here), "seq", 1)
    def by_half(rows):
        return jnp.where(core == 0, rows, rows[:, ::-1])

    rows, probs, weights = [None, None], [None, None], [None, None]
    meta = after(metas[0], sources[0])
    if offs is not None:
        meta = after(meta, rest_pieces)
        beside_rest = [swap(rest_pieces[0], "seq", 1)]
    rows[0], probs[0], weights[0] = attend(meta, sources[0], pre_mix, post_mix, heads, FLOPS[0])
    next_far, beside = lax.optimization_barrier((next_far, beside, rows[0]))[:2]
    if offs is not None:
        far_z, far_x, next_far, beside, beside_rest = lax.optimization_barrier(
            (far_z, far_x, next_far, beside, beside_rest)
        )
        rest_pieces += [far_z, far_x]
        beside_rest = list(beside_rest) + [swap(p, "seq", 1) for p in (far_z, far_x)]
        last = swap(far_z, "dp", 1)
    sources.append([near[1], beside, next_far, swap(next_far, "seq", 1)])
    far_rows = swap(rows[0][2:], "seq", 2)
    rows[1], probs[1], weights[1] = attend(
        metas[1], sources[1], pre_mix, post_mix, heads, FLOPS[1]
    )
    far_rows = after(far_rows, rows[1])
    cut = owners * slice_ff + half
    if offs is not None:
        last, *beside_rest = after([last] + beside_rest, rows[1])
        rest_pieces.append(last)
        feed_weights = rest_pieces + beside_rest + [swap(last, "seq", 1)]
    else:
        rest = lax.all_gather(rest[0], "dp")
        feed_weights = []
        for part in (rest, swap(rest, "seq", 1)):
            flat = part.reshape(owners * own_rows, -1)
            down = jnp.moveaxis(part[:, :, cut:].reshape(owners, own_rows, folds, width), 2, 1)
            feed_weights += [
                flat[:, : cut - half],
                flat[:, cut - half : cut],
                down.reshape(owners * slice_ff, width),
            ]
    far_rows = jnp.stack([far_rows, swap(rows[1][2:], "seq", 2)])
    near_rows = jnp.stack([rows[0][1], rows[1][1]])
    got = swap(jnp.stack([near_rows, far_rows[:, 1]]), "seq", 1)
    attention_output = jnp.stack(
        [
            by_half(
                jnp.stack(
                    [
                        jnp.stack([rows[slot][0], got[0, slot]]),
                        jnp.stack([far_rows[slot, 0], got[1, slot]]),
                    ]
                )
            ).reshape(2, 2 * ROWS, width)
            for slot in range(2)
        ]
    )

    flat = (-1, width)
    attention_output = attention_output.reshape(flat)
    flat_out = grad_out.reshape(flat)
    output, grad_resid, resid_low, grad_attended, gain_two, second_in, *wide = feed_forward(
        feed_meta,
        gain_vals[:2],
        tokens.reshape(flat),
        attention_output,
        flat_out,
        feed_weights,
        offs,
        hidden,
    )
    grad_attended = grad_attended.reshape(grad_out.shape)
    grad_resid = grad_resid.reshape(4, shard_len, width)

    def sums_of(side, which, kind):
        return weight_sums(
            which[None],
            second_in,
            attention_output,
            resid_low,
            flat_out,
            wide[side],
            wide[2 + side],
            kind,
        )

    output = output.reshape(tokens.shape)
    gain_two = jnp.sum(gain_two, axis=0)

    sent = sums_of(1, 1 - core, BF)
    arrived = swap(sent[0], "seq", 1), swap(sent[1], "seq", 1)
    meta = after(core, sent)
    mine = sums_of(0, meta, F32)
    arrived = after(arrived, mine, output)
    twos = [(2**k, 2) for k in range(owners.bit_length() - 1)]
    orders = [twos, twos[1:2] + twos[:1] + twos[2:]]
    chains = []
    for at in range(2):
        total = (mine[at] + arrived[at].astype(F32)).astype(BF)
        total = total.reshape((2,) * len(twos) + (-1, total.shape[1]))
        chains.append(split_blocks(total, "dp", twos[::-1], orders[at][0]))

    def send_step(at, turn, parts):
        stride, radix = orders[at][turn]
        return tuple(swap(parts[0][k], "dp", k * stride) for k in range(1, radix))

    def join_step(at, turn, parts, got):
        total = parts[0][0].astype(F32)
        for part in got:
            total = total + part.astype(F32)
        if turn + 1 == len(twos):
            return total
        return split_blocks(total.astype(BF), "dp", parts[1], orders[at][turn + 1])

    def step_on(at, turn, parts, *first):
        got = send_step(at, turn, parts)
        return join_step(at, turn, parts, after(got, *first) if first else got)

    def to_far(slot):
        found = by_half(grad_attended[slot].reshape(2, 2, ROWS, width)).reshape(4, ROWS, width)
        return found, swap(found[2:], "seq", 2)

    def from_near(found, far):
        got = swap(jnp.stack([found[1], far[1]]), "seq", 1)
        return jnp.stack([found[0], got[0], far[0], got[1]])

    def attend_slot(slot, meta, rows):
        return attend_back(
            meta, sources[slot], rows, pre_back, post_back, probs[slot], weights[slot], FLOPS[slot]
        )

    found, far = to_far(0)
    far = after(far, mine)
    next_found, next_far = to_far(1)
    meta = after(metas[0], chains)
    stay, away, back_pre, back_post = attend_slot(0, meta, from_near(found, far))
    grad_mixes = jnp.stack([back_pre[:, :heads], back_post[:, :heads]])
    chains = [step_on(at, 0, chains[at], stay) for at in range(2)]
    away, next_far = lax.optimization_barrier((away, next_far, chains))[:2]
    next_rows = from_near(next_found, next_far)
    summed = (stay + swap(away, "seq", 1).astype(F32)).astype(BF)
    far = swap(summed[1], "seq", 2)
    meta = after(metas[1], summed, chains)
    stay, away, back_pre, back_post = attend_slot(1, meta, next_rows)
    grad_mixes = grad_mixes + jnp.stack([back_pre[:, :heads], back_post[:, :heads]])
    got = [send_step(at, 1, chains[at]) for at in range(2)]
    away, far, got = lax.optimization_barrier((away, far, got, stay))[:3]
    grad_cols = [(summed[0], far)]
    summed = (stay + swap(away, "seq", 1).astype(F32)).astype(BF)
    got = after(got, summed)
    chains = [join_step(at, 1, chains[at], got[at]) for at in range(2)]
    far = swap(summed[1], "seq", 2)

    def to_tokens(slot, before, first):
        return token_grads(
            slot,
            after(seqs[slot], first),
            gain_vals,
            *grad_cols[slot],
            weight_qkv,
            tokens,
            grad_resid,
            before,
        )

    begun = to_tokens(0, None, summed)
    for turn in range(2, len(twos)):
        chains = [step_on(at, turn, chains[at], begun) for at in range(2)]
    first_part, second_part = chains
    others = first_part.astype(BF), second_part.astype(BF)
    far, begun, others = lax.optimization_barrier((far, begun, others))
    grad_cols.append((summed[0], far))
    cols = grad_cols[0] + grad_cols[1]
    sent = first_grads((1 - core)[None], first_in, cols, BF)
    qkv_mine = first_grads(after(core, sent)[None], first_in, cols, F32)

    def over_pairs(total, *first):
        total = lax.optimization_barrier(jax.tree.map(lambda v: v.astype(BF), total))
        got = jax.tree.map(lambda v: swap(v, "seq", 2), total)
        if first:
            got = after(got, *first)
        return jax.tree.map(lambda v, w: v.astype(F32) + w.astype(F32), total, got)

    arrived = after(swap(sent, "seq", 1), qkv_mine)
    qkv_total = (qkv_mine + arrived.astype(F32)).astype(BF)
    qkv_total = qkv_total.reshape((2,) * len(twos) + (own_rows, side))
    third = side // LANES // 3 * LANES
    chains = [qkv_total[..., third:], qkv_total[..., :third]]
    chains = [split_blocks(chains[at], "dp", twos[::-1], orders[at][0]) for at in range(2)]
    others = over_pairs(after(others, [p for p, _ in chains]))
    got = [send_step(at, 0, chains[at]) for at in range(2)]
    grad_rows_tokens, gain_more = to_tokens(1, begun[0], got[1])
    got[0] = after(got[0], grad_rows_tokens)
    chains = [join_step(at, 0, chains[at], got[at]) for at in range(2)]
    got = [send_step(at, 1, chains[at]) for at in range(2)]
    gain_one = jnp.sum(begun[1] + gain_more, axis=0)
    small = jnp.concatenate([gain_one, gain_two, grad_mixes.reshape(-1)])
    count = small.shape[0]
    small = jnp.pad(small, (0, -(count + 1) % (8 * LANES) + 1)).reshape(-1, LANES)
    chains = [join_step(at, 1, chains[at], got[at]) for at in range(2)]

    first_halves = (others[0], swap(others[0], "seq", 1))
    last_halves = (others[1], swap(others[1], "seq", 1))
    if own_rows % 8 == 0:
        red_inner, red_proj, red_outer, squares = assemble(
            core, slice_ff, first_halves, last_halves
        )
    else:
        red_proj = by_core(*[g[:, cut - half :] for g in first_halves], 1)
        red_inner = by_core(
            *[g[:, : cut - half].reshape(own_rows, owners, 1, slice_ff) for g in first_halves], 2
        ).reshape(own_rows, hidden)
        red_outer = by_core(*last_halves, 0)
        squares = squares_of([first_halves, last_halves])
    small = small + swap(small, "seq", 1)
    small = small + swap(small, "seq", 2)
    pins = (red_inner, red_proj, red_outer, squares)
    for turn in range(2, len(twos)):
        chains = [step_on(at, turn, chains[at], *pins) for at in range(2)]
        pins = ()
    qkv_total = over_pairs(jnp.concatenate(chains[::-1], axis=-1), small)
    qkv_other = swap(qkv_total, "seq", 1)
    red_qkv = by_core(qkv_total, qkv_other, 1)

    squares = squares + squares_of([(qkv_total, qkv_other)])
    place = lax.broadcasted_iota(jnp.int32, small.shape, 0) * LANES
    place = place + lax.broadcasted_iota(jnp.int32, small.shape, 1)
    small = sum_everywhere(jnp.where(place == count, squares, small), "dp").reshape(-1)
    gain_all = small[: 2 * width].reshape(2, width)
    red_gains = lax.dynamic_slice_in_dim(gain_all, lax.axis_index("dp") * own_rows, own_rows, 1)
    red_mixes = small[2 * width : count].reshape(mixes.shape)
    grad_norm = jnp.sqrt(
        small[count] + jnp.sum(gain_all * gain_all) + jnp.sum(red_mixes * red_mixes)
    )
    factor = CLIP / jnp.maximum(grad_norm, CLIP)
    clipped_gains = red_gains * factor
    new = adamw_all(
        factor[None],
        (red_qkv, red_proj, red_inner, red_outer, red_gains),
        (
            (qkv_weight, qkv_first, qkv_second, qkv_average),
            (proj_weight, proj_first, proj_second, proj_average),
            (inner_weight, inner_first, inner_second, inner_average),
            (outer_weight, outer_first, outer_second, outer_average),
            (gains, gain_first, gain_second, gain_average),
        ),
    )
    mix_new = adamw(mixes, mix_first, mix_second, mix_average, red_mixes * factor, 0.3)
    return (
        output,
        grad_rows_tokens,
        grad_norm,
        *new,
        *mix_new,
        clipped_gains,
    )


def solution(mesh):
    rows = P("dp", "seq", None)
    matrix = P("dp", None)
    vector = P(None, "dp")
    in_specs = (rows, rows, P("dp")) + (matrix,) * 16 + (vector,) * 4 + (P(),) * 4
    out_specs = (rows, rows, P()) + (matrix,) * 16 + (vector,) * 4 + (P(),) * 4 + (vector,)
    return jax.shard_map(
        on_device, mesh=mesh, in_specs=in_specs, out_specs=out_specs, check_vma=False
    )
```

```python
from functools import partial
import math

import jax
import jax.numpy as jnp
from jax import lax
from jax.experimental import pallas as pl
from jax.experimental.pallas import tpu as pltpu
from jax.sharding import PartitionSpec as P

STEP = 10

NORM_EPS = 1e-06
BETA = 0.5
ADAM_EPS = 1e-08
DECAY = 0.01
EMA_KEEP = 0.8
CLIP = 1.0

BF = jnp.bfloat16
F32 = jnp.float32
ROWS = 128
KEYS = 256
GROUP = 16
LANES = 128
FLOPS = (60 * 10**9, 1)
SIDE = {1: 8, 2: 8, 3: 8, 4: 8}
SIDE_BACK = {1: 4, 2: 4, 3: 2, 4: 2}
NT = (((1,), (1,)), ((), ()))
NN = (((1,), (0,)), ((), ()))
TN = (((0,), (0,)), ((), ()))


def dot(left, right, dims=NN):
    return lax.dot_general(left, right, dims, preferred_element_type=F32)


def inverse_rms(values):
    return lax.rsqrt(jnp.mean(values * values, axis=-1, keepdims=True) + NORM_EPS)


def rms_backward(scale_inv, normed, grad_normed):
    return scale_inv * (
        grad_normed - normed * jnp.mean(normed * grad_normed, axis=-1, keepdims=True)
    )


def adamw(weight, first, second, average, grad, rate):
    first_new = BETA * first + (1.0 - BETA) * grad
    second_new = BETA * second + (1.0 - BETA) * grad * grad
    fix = 1.0 - BETA**STEP
    weight_new = weight - rate * (
        first_new / fix / (jnp.sqrt(second_new / fix) + ADAM_EPS) + DECAY * weight
    )
    average_new = EMA_KEEP * average + (1.0 - EMA_KEEP) * weight_new
    return (first_new, second_new, weight_new, average_new)


def swap(value, axis, mask):
    size = lax.axis_size(axis)
    return lax.ppermute(value, axis, [(i, i ^ mask) for i in range(size)])


def digits_of(size):
    found = []
    stride = 1
    while stride < size:
        radix = 2 if stride == 1 or size // stride < 4 else 4
        found.append((stride, radix))
        stride *= radix
    return found


def gather_steps(size):
    steps = []
    while size > 1:
        size //= 2
        steps.append(size)
    return steps


def own_order(shards, axis):
    size = shards.shape[0]
    order = jnp.bitwise_xor(jnp.arange(size, dtype=jnp.int32), lax.axis_index(axis))
    return shards.at[order].get(mode="promise_in_bounds")


def join_pieces(pieces, axis):
    place = {}
    for _, offs in pieces:
        for off in offs:
            place[off] = len(place)
    spots = jnp.array([place[off] for off in range(len(place))], jnp.int32)
    order = jnp.bitwise_xor(jnp.arange(len(place), dtype=jnp.int32), lax.axis_index(axis))
    whole = jnp.concatenate([piece for piece, _ in pieces])
    return whole.at[spots.at[order].get(mode="promise_in_bounds")].get(mode="promise_in_bounds")


def split_blocks(blocks, axis, digits, digit):
    stride, radix = digit
    place = digits.index(digit)
    mine = (lax.axis_index(axis) // stride) % radix
    parts = [
        lax.dynamic_index_in_dim(blocks, jnp.bitwise_xor(mine, k), place, False)
        for k in range(radix)
    ]
    return parts, [d for d in digits if d != digit]


def join_blocks(parts, axis, digit, *first):
    stride, radix = digit
    got = tuple(swap(parts[k], axis, k * stride) for k in range(1, radix))
    if first:
        got = after(got, *first)
    total = parts[0].astype(F32)
    for part in got:
        total = total + part.astype(F32)
    return total


def sum_everywhere(value, axis):
    size = lax.axis_size(axis)
    stride = 1
    while stride < size:
        radix = min(8, size // stride)
        parts = [value] + [swap(value, axis, k * stride) for k in range(1, radix)]
        while len(parts) > 1:
            parts = [parts[i] + parts[i + 1] for i in range(0, len(parts), 2)]
        value = parts[0]
        stride *= radix
    return value


def after(value, *first):
    return lax.optimization_barrier((value,) + first)[0]


def spread_kernel(mixes, pre, post, pre_back, post_back):
    heads = mixes.shape[1]
    tall = heads * GROUP
    wide = (lax.broadcasted_iota(jnp.int32, (tall, heads), 0) // GROUP) == (
        lax.broadcasted_iota(jnp.int32, (tall, heads), 1)
    )
    wide = wide.astype(F32)
    row = lax.broadcasted_iota(jnp.int32, (tall, tall), 0)
    col = lax.broadcasted_iota(jnp.int32, (tall, tall), 1)
    same = row % GROUP == col % GROUP

    def exact(left, right, dims):
        return lax.dot_general(
            left, right, dims, precision=lax.Precision.HIGHEST, preferred_element_type=F32
        )

    for which, (turned, straight) in enumerate(((pre, pre_back), (post, post_back))):
        matrix = mixes[which]
        for out, dims in ((straight, NN), (turned, NT)):
            tallest = exact(wide, matrix, dims)
            full = jnp.where(same, exact(tallest, wide, NT), 0.0)
            high = full.astype(BF)
            out[:tall, :] = high
            out[tall:, :] = (full - high.astype(F32)).astype(BF)


def spread(mixes):
    tall = mixes.shape[1] * GROUP
    return pl.pallas_call(
        spread_kernel,
        out_shape=[jax.ShapeDtypeStruct((2 * tall, tall), BF)] * 4,
        name="spread",
    )(mixes)


def two_heads(rows, first, second):
    return jnp.concatenate([rows * first, rows * second], 0)


def mix(matrix, values):
    out = dot(matrix, values)
    half = matrix.shape[0] // 2
    return out[:half] + out[half:]


def head_masks(scaling):
    lane = lax.broadcasted_iota(jnp.int32, (1, LANES), 1)
    low = lane < LANES // 2
    return low, jnp.where(low, scaling, 0.0).astype(BF), jnp.where(low, 0.0, scaling).astype(BF)


def fill_sequence(meta, sources, qkv, sems):
    copies = []
    for d, source in enumerate(sources):
        start = pl.multiple_of(jnp.bitwise_xor(meta[1], d) * KEYS, KEYS)
        copies.append(pltpu.make_async_copy(source, qkv.at[pl.ds(start, KEYS)], sems.at[d]))
    for copy in copies:
        copy.start()
    for copy in copies:
        copy.wait()


def forward_kernel(meta, *refs):
    sources, (pre, post, attended, probs, weights, qkv, held, sems) = refs[:4], refs[4:]
    heads = probs.shape[0]
    width = attended.shape[1]
    pairs = heads // 2
    tall = heads * GROUP
    step = pl.program_id(0)
    pl.when(step == 0)(partial(fill_sequence, meta, sources, qkv, sems))
    length = meta[0]
    row0 = pl.multiple_of(step * KEYS + meta[2] * ROWS, ROWS)
    chunks = (jnp.minimum(row0 + ROWS, length) + KEYS - 1) // KEYS
    low, first_s, second_s = head_masks(1.0 / math.sqrt(width // heads))

    def score(kc, carry):
        k0 = pl.multiple_of(kc * KEYS, KEYS)
        for p in range(pairs):
            at = p * LANES
            queries = two_heads(qkv[pl.ds(row0, ROWS), at : at + LANES], first_s, second_s)
            keys = qkv[pl.ds(k0, KEYS), width + at : width + at + LANES]
            scores = dot(queries, keys, NT).astype(BF)
            weights[2 * p : 2 * p + 2, :, pl.ds(k0, KEYS)] = scores.reshape(2, ROWS, KEYS)
        return carry

    lax.fori_loop(0, chunks, score, 0)

    def group(n, batch, carry):
        side = SIDE[n]
        rows = [
            pl.ds(pl.multiple_of((batch * side + u) * GROUP, GROUP), GROUP) for u in range(side)
        ]
        col_at = lax.broadcasted_iota(jnp.int32, (GROUP, KEYS), 1)
        row_at = lax.broadcasted_iota(jnp.int32, (GROUP, KEYS), 0)
        peak = [None] * side
        total = [None] * side
        for kc in range(n):
            cols = slice(kc * KEYS, (kc + 1) * KEYS)
            for u in range(side):
                mixed = mix(pre[...], weights[:, rows[u], cols].reshape(tall, KEYS))
                key_pos = col_at + kc * KEYS
                query_pos = row0 + (batch * side + u) * GROUP + row_at
                allowed = (key_pos <= query_pos) & (key_pos < length)
                mixed = jnp.where(allowed[None], mixed.reshape(heads, GROUP, KEYS), -1e30)
                mixed = mixed.reshape(tall, KEYS)
                held[u, :, cols] = mixed
                part = jnp.maximum(mixed[:, :LANES], mixed[:, LANES:])
                peak[u] = part if kc == 0 else jnp.maximum(peak[u], part)
        top = [jnp.max(peak[u], axis=1, keepdims=True) for u in range(side)]
        for kc in range(n):
            cols = slice(kc * KEYS, (kc + 1) * KEYS)
            for u in range(side):
                shifted = jnp.exp(held[u, :, cols] - top[u])
                held[u, :, cols] = shifted
                part = shifted[:, :LANES] + shifted[:, LANES:]
                total[u] = part if kc == 0 else total[u] + part
        inverse = [1.0 / jnp.sum(total[u], axis=1, keepdims=True) for u in range(side)]
        for kc in range(n):
            cols = slice(kc * KEYS, (kc + 1) * KEYS)
            for u in range(side):
                low_probs = (held[u, :, cols] * inverse[u]).astype(BF)
                probs[:, rows[u], cols] = low_probs.reshape(heads, GROUP, KEYS)
                mixed = mix(post[...], low_probs).astype(BF)
                weights[:, rows[u], cols] = mixed.reshape(heads, GROUP, KEYS)
        return carry

    def rest(n):
        lax.fori_loop(0, ROWS // GROUP // SIDE[n], partial(group, n), 0)
        for p in range(pairs):
            at = p * LANES
            pair = weights[2 * p : 2 * p + 2, :, : n * KEYS].reshape(2 * ROWS, n * KEYS)
            out = dot(pair, qkv[: n * KEYS, 2 * width + at : 2 * width + at + LANES])
            attended[:, at : at + LANES] = jnp.where(low, out[:ROWS], out[ROWS:]).astype(BF)

    for n in range(1, probs.shape[2] // KEYS + 1):
        pl.when(chunks == n)(partial(rest, n))


def backward_kernel(meta, *refs):
    sources, refs = refs[:4], refs[4:]
    grad_rows, pre, post, probs, weights, stay, away, grad_pre, grad_post = refs[:9]
    qkv, scores, grads, held, grad_qkv, sum_pre, sum_post, sems = refs[9:]
    heads = probs.shape[0]
    width = grad_rows.shape[1]
    pairs = heads // 2
    tall = heads * GROUP
    step = pl.program_id(0)
    me = meta[1]

    @pl.when(step == 0)
    def _():
        grad_qkv[...] = jnp.zeros_like(grad_qkv)
        sum_pre[...] = jnp.zeros_like(sum_pre)
        sum_post[...] = jnp.zeros_like(sum_post)
        fill_sequence(meta, sources, qkv, sems)

    length = meta[0]
    row0 = pl.multiple_of(step * KEYS + meta[2] * ROWS, ROWS)
    chunks = (jnp.minimum(row0 + ROWS, length) + KEYS - 1) // KEYS
    chunks = jnp.where(row0 < length, chunks, 0)
    scaling = 1.0 / math.sqrt(width // heads)
    low, first_s, second_s = head_masks(scaling)
    low, first_one, second_one = head_masks(1.0)
    lanes = pl.ds(pl.multiple_of(meta[2] * ROWS, ROWS), ROWS)

    def slot_of(home):
        d = jnp.bitwise_xor(me, home)
        return 2 * jnp.bitwise_and(d, 1) + d // 2


    def score(kc, carry):
        k0 = pl.multiple_of(kc * KEYS, KEYS)
        for p in range(pairs):
            at = p * LANES
            queries = two_heads(qkv[pl.ds(row0, ROWS), at : at + LANES], first_s, second_s)
            grad = two_heads(grad_rows[:, at : at + LANES], first_one, second_one)
            keys = qkv[pl.ds(k0, KEYS), width + at : width + at + LANES]
            values = qkv[pl.ds(k0, KEYS), 2 * width + at : 2 * width + at + LANES]
            both = slice(2 * p, 2 * p + 2)
            cols = pl.ds(k0, KEYS)
            scores[both, :, cols] = dot(queries, keys, NT).astype(BF).reshape(2, ROWS, KEYS)
            grads[both, :, cols] = dot(grad, values, NT).astype(BF).reshape(2, ROWS, KEYS)
        return carry

    lax.fori_loop(0, chunks, score, 0)

    def group(n, batch, carry):
        side = SIDE_BACK[n]
        rows = [
            pl.ds(pl.multiple_of((batch * side + u) * GROUP, GROUP), GROUP) for u in range(side)
        ]
        span = slice(0, n * KEYS)
        total = [None] * side
        for kc in range(n):
            cols = slice(kc * KEYS, (kc + 1) * KEYS)
            for u in range(side):
                grad_probs = mix(post[...], grads[:, rows[u], cols].reshape(tall, KEYS))
                held[u, :, cols] = grad_probs
                term = probs[:, rows[u], cols].reshape(tall, KEYS).astype(F32) * grad_probs
                part = term[:, :LANES] + term[:, LANES:]
                total[u] = part if kc == 0 else total[u] + part
        added = None
        for u in range(side):
            left = probs[:, rows[u], span].reshape(tall, n * KEYS)
            term = dot(left, grads[:, rows[u], span].reshape(tall, n * KEYS), NT)
            added = term if u == 0 else added + term
        sum_post[...] += added
        delta = [jnp.sum(total[u], axis=1, keepdims=True) for u in range(side)]
        mixed = [[] for _ in range(side)]
        for kc in range(n):
            cols = slice(kc * KEYS, (kc + 1) * KEYS)
            for u in range(side):
                prob = probs[:, rows[u], cols].reshape(tall, KEYS).astype(F32)
                grad_mixed = (prob * (held[u, :, cols] - delta[u])).astype(BF)
                mixed[u].append(grad_mixed)
                back = mix(pre[...], grad_mixed).astype(BF)
                grads[:, rows[u], cols] = back.reshape(heads, GROUP, KEYS)
        added = None
        for u in range(side):
            left = scores[:, rows[u], span].reshape(tall, n * KEYS)
            term = dot(left, jnp.concatenate(mixed[u], 1), NT)
            added = term if u == 0 else added + term
        sum_pre[...] += added
        return carry

    def rest(n):
        lax.fori_loop(0, ROWS // GROUP // SIDE_BACK[n], partial(group, n), 0)
        for p in range(pairs):
            at = p * LANES
            mine = slice(at, at + LANES)
            both = slice(2 * p, 2 * p + 2)
            queries = two_heads(qkv[pl.ds(row0, ROWS), mine], first_s, second_s).T
            grad = two_heads(grad_rows[:, mine], first_one, second_one).T
            back = grads[both, :, : n * KEYS].reshape(2 * ROWS, n * KEYS)
            out = dot(back, qkv[: n * KEYS, width + at : width + at + LANES])
            out = jnp.where(low, out[:ROWS], out[ROWS:]) * scaling
            grad_qkv[slot_of(step), mine, lanes] = out.T
            for kc in range(n):
                cols = slice(kc * KEYS, (kc + 1) * KEYS)
                to = slot_of(kc)
                grad_qkv[to, width + at : width + at + LANES, :] += dot(
                    queries, grads[both, :, cols].reshape(2 * ROWS, KEYS)
                )
                grad_qkv[to, 2 * width + at : 2 * width + at + LANES, :] += dot(
                    grad, weights[both, :, cols].reshape(2 * ROWS, KEYS)
                )

    for n in range(1, probs.shape[2] // KEYS + 1):
        pl.when(chunks == n)(partial(rest, n))

    @pl.when(step == pl.num_programs(0) - 1)
    def _():
        stay[...] = grad_qkv[:2]
        away[...] = grad_qkv[2:].astype(BF)
        row = lax.broadcasted_iota(jnp.int32, (tall, tall), 0)
        col = lax.broadcasted_iota(jnp.int32, (tall, tall), 1)
        same = row % GROUP == col % GROUP
        pick = (
            lax.broadcasted_iota(jnp.int32, (tall, LANES), 0) // GROUP
            == lax.broadcasted_iota(jnp.int32, (tall, LANES), 1)
        ).astype(F32)
        for source, out in ((sum_pre, grad_pre), (sum_post, grad_post)):
            kept = jnp.where(same, source[...], 0.0)
            wide = lax.dot_general(
                kept, pick, NN, precision=lax.Precision.HIGHEST, preferred_element_type=F32
            )
            for head in range(heads):
                out[head : head + 1, :] = jnp.sum(
                    wide[head * GROUP : (head + 1) * GROUP], axis=0, keepdims=True
                )


ANY = pl.BlockSpec(memory_space=pl.ANY)


def is_live(step, meta):
    return step * KEYS + meta[2] * ROWS < meta[0]


def attend(meta, sources, pre, post, heads, flops):
    width = sources[0].shape[1] // 3
    tall = heads * GROUP
    steps = 4
    full_len = steps * KEYS
    matrix = pl.BlockSpec((2 * tall, tall), lambda i, m: (0, 0), pipeline_mode=pl.Buffered(1))
    wide = pl.BlockSpec(
        (None, heads, ROWS, full_len), lambda i, m: (jnp.where(is_live(i, m), i, steps), 0, 0, 0)
    )
    kept = jax.ShapeDtypeStruct((steps + 1, heads, ROWS, full_len), BF)
    return pl.pallas_call(
        forward_kernel,
        grid_spec=pltpu.PrefetchScalarGridSpec(
            num_scalar_prefetch=1,
            grid=(steps,),
            in_specs=[ANY] * 4 + [matrix, matrix],
            out_specs=[
                pl.BlockSpec((None, ROWS, width), lambda i, m: (jnp.bitwise_xor(i, m[1]), 0, 0)),
                wide,
                wide,
            ],
            scratch_shapes=[
                pltpu.VMEM((full_len, 3 * width), BF),
                pltpu.VMEM((8, tall, full_len), F32),
                pltpu.SemaphoreType.DMA((4,)),
            ],
        ),
        out_shape=[jax.ShapeDtypeStruct((steps, ROWS, width), BF), kept, kept],
        compiler_params=pltpu.CompilerParams(vmem_limit_bytes=56 * 2**20),
        cost_estimate=pl.CostEstimate(
            flops=flops, bytes_accessed=1, transcendentals=0
        ),
        name="attend",
    )(meta, *sources, pre, post)


def attend_back(meta, sources, grad_rows, pre, post, probs, weights, flops):
    width = sources[0].shape[1] // 3
    steps = 4
    heads = probs.shape[1]
    tall = heads * GROUP
    full_len = steps * KEYS

    def newest(step, meta):
        last = 0
        for other in range(1, steps):
            last = jnp.where(is_live(other, meta), other, last)
        return jnp.minimum(step, last)

    matrix = pl.BlockSpec((2 * tall, tall), lambda i, m: (0, 0), pipeline_mode=pl.Buffered(1))
    wide = pl.BlockSpec((None, heads, ROWS, full_len), lambda i, m: (newest(i, m), 0, 0, 0))
    rows = pl.BlockSpec((None, ROWS, width), lambda i, m: (jnp.bitwise_xor(i, m[1]), 0, 0))
    small = pl.BlockSpec((heads, LANES), lambda i, m: (0, 0))
    pairs = pl.BlockSpec(
        (2, 3 * width, KEYS), lambda i, m: (0, 0, 0), pipeline_mode=pl.Buffered(1)
    )
    return pl.pallas_call(
        backward_kernel,
        grid_spec=pltpu.PrefetchScalarGridSpec(
            num_scalar_prefetch=1,
            grid=(steps,),
            in_specs=[ANY] * 4 + [rows, matrix, matrix, wide, wide],
            out_specs=[
                pairs,
                pairs,
                small,
                small,
            ],
            scratch_shapes=[
                pltpu.VMEM((full_len, 3 * width), BF),
                pltpu.VMEM((heads, ROWS, full_len), BF),
                pltpu.VMEM((heads, ROWS, full_len), BF),
                pltpu.VMEM((4, tall, full_len), F32),
                pltpu.VMEM((4, 3 * width, KEYS), F32),
                pltpu.VMEM((tall, tall), F32),
                pltpu.VMEM((tall, tall), F32),
                pltpu.SemaphoreType.DMA((4,)),
            ],
        ),
        out_shape=[
            jax.ShapeDtypeStruct((2, 3 * width, KEYS), F32),
            jax.ShapeDtypeStruct((2, 3 * width, KEYS), BF),
            jax.ShapeDtypeStruct((heads, LANES), F32),
            jax.ShapeDtypeStruct((heads, LANES), F32),
        ],
        compiler_params=pltpu.CompilerParams(vmem_limit_bytes=60 * 2**20),
        cost_estimate=pl.CostEstimate(
            flops=flops, bytes_accessed=1, transcendentals=0
        ),
        name="attend_back",
    )(meta, *sources, grad_rows, pre, post, probs, weights)


def gelu_both(value):
    scale = math.sqrt(2.0 / math.pi)
    square = value * value
    bent = jnp.tanh(scale * (value + 0.044715 * (square * value)))
    share = 0.5 * (1.0 + bent)
    slope = share + 0.5 * value * (1.0 - bent * bent) * (
        scale * (1.0 + 3.0 * 0.044715 * square)
    )
    return value * share, slope


def fill_weights(meta, sources, offs, inner, outer, proj, sems):
    hidden = inner.shape[1] // 2
    width = proj.shape[0]
    half = width // 2
    late, early = [], []

    def copy(source, target, kind=None):
        sem = sems.at[len(late) + len(early)]
        (late if kind is None else early).append(pltpu.make_async_copy(source, target, sem))

    count = len(sources) // 2
    for side in range(2):
        lanes = jnp.bitwise_xor(meta[1], side) * half
        to_proj = pl.ds(pl.multiple_of(lanes, LANES), half)
        to_inner = slice(side * hidden, (side + 1) * hidden)
        here = sources[count * side : count * side + count]
        if offs is None:
            copy(here[0], inner.at[:, to_inner])
            copy(here[1], proj.at[:, to_proj], 1)
            copy(here[2], outer.at[to_inner])
            continue
        own_rows = here[0].shape[1]
        folds = hidden * own_rows // width // own_rows
        for source, owners in zip(here, offs):
            for at_source, off in enumerate(owners):
                block = source.at[at_source]
                owner = jnp.bitwise_xor(meta[0], off)
                rows = pl.ds(pl.multiple_of(owner * own_rows, own_rows), own_rows)
                copy(block.at[:, :hidden], inner.at[rows, to_inner])
                copy(block.at[:, hidden : hidden + half], proj.at[rows, to_proj], 1)
                for fold in range(folds):
                    start = side * hidden + (owner * folds + fold) * own_rows
                    at = hidden + half + fold * width
                    copy(
                        block.at[:, at : at + width],
                        outer.at[pl.ds(pl.multiple_of(start, own_rows), own_rows)],
                    )
    for one in early + late:
        one.start()
    return early, late


TILE = 256
CHUNK = 512


def feed_kernel(offs, meta, gains, tokens, attended, grad_out, *refs):
    count = len(refs) - 17
    sources, refs = refs[:count], refs[count:]
    output, grad_resid, resid_low, grad_attended, gain_two, second_in = refs[:6]
    active, grad_hidden = refs[6:8], refs[8:10]
    inner, outer, proj, resid, out_sum, grad_sum, sems = refs[10:]
    rows = tokens.shape[0]
    step = pl.program_id(0)
    tiles = [slice(at, at + TILE) for at in range(0, rows, TILE)]

    @pl.when(step == 0)
    def _():
        early, late = fill_weights(meta, sources, offs, inner, outer, proj, sems)
        for one in early:
            one.wait()
        for tile in tiles:
            seq = meta[2 + tile.start // TILE]
            value = tokens[pl.ds(pl.multiple_of(seq * TILE, TILE), TILE)].astype(F32)
            value = value + dot(attended[tile], proj[...])
            resid[tile] = value
            out_sum[tile] = value
            grad_sum[tile] = jnp.zeros_like(value)
            second_in[tile] = (value * inverse_rms(value) * gains[1:2]).astype(BF)
        for one in late:
            one.wait()

    cols = pl.ds(pl.multiple_of(step * CHUNK, CHUNK), CHUNK)
    for tile in tiles:
        up = inner[:, cols]
        down = outer[cols]
        value, slope = gelu_both(dot(second_in[tile], up))
        value = value.astype(BF)
        back = (dot(grad_out[tile], down, NT) * slope).astype(BF)
        for side in range(2):

            @pl.when((step * 2 >= pl.num_programs(0)) == (side == 1))
            def _():
                active[side][tile] = value
                grad_hidden[side][tile] = back

        out_sum[tile] += dot(value, down)
        grad_sum[tile] += dot(back, up, NT)

    @pl.when(step == pl.num_programs(0) - 1)
    def _():
        gain_sum = jnp.zeros((8, proj.shape[0]), F32)
        for tile in tiles:
            seq = meta[2 + tile.start // TILE]
            output[pl.ds(pl.multiple_of(seq * TILE, TILE), TILE)] = out_sum[tile].astype(BF)
            value = resid[tile]
            scale = inverse_rms(value)
            normed = value * scale
            grad = grad_sum[tile]
            gain_sum += jnp.sum((grad * normed).reshape(TILE // 8, 8, -1), axis=0)
            back = grad_out[tile].astype(F32) + rms_backward(scale, normed, grad * gains[1:2])
            grad_resid[tile] = back
            back = back.astype(BF)
            resid_low[tile] = back
            grad_attended[tile] = dot(back, proj[...], NT).astype(BF)
        gain_two[...] = gain_sum


def feed_forward(meta, gains, tokens, attended, grad_out, sources, offs, hidden):
    rows, width = tokens.shape
    copies = 6
    if offs is not None:
        owners = sum(len(o) for o in offs)
        copies = 2 * owners * (2 + hidden // 2 // width)
    chunks = hidden // CHUNK

    def whole(shape):
        return pl.BlockSpec(shape, lambda c, m: (0,) * len(shape), pipeline_mode=pl.Buffered(1))

    flat = whole((rows, width))
    first = pl.BlockSpec((rows, CHUNK), lambda c, m: (0, jnp.minimum(c, chunks // 2 - 1)))
    second = pl.BlockSpec((rows, CHUNK), lambda c, m: (0, jnp.maximum(c - chunks // 2, 0)))
    wide = jax.ShapeDtypeStruct((rows, hidden // 2), BF)
    return pl.pallas_call(
        partial(feed_kernel, offs),
        grid_spec=pltpu.PrefetchScalarGridSpec(
            num_scalar_prefetch=1,
            grid=(chunks,),
            in_specs=[whole((2, width)), flat, flat, flat] + [ANY] * len(sources),
            out_specs=[flat, flat, flat, flat, whole((8, width)), flat, first, second, first, second],
            scratch_shapes=[
                pltpu.VMEM((width, hidden), BF),
                pltpu.VMEM((hidden, width), BF),
                pltpu.VMEM((width, width), BF),
                pltpu.VMEM((rows, width), F32),
                pltpu.VMEM((rows, width), F32),
                pltpu.VMEM((rows, width), F32),
                pltpu.SemaphoreType.DMA((copies,)),
            ],
        ),
        out_shape=[
            jax.ShapeDtypeStruct((rows, width), BF),
            jax.ShapeDtypeStruct((rows, width), F32),
            jax.ShapeDtypeStruct((rows, width), BF),
            jax.ShapeDtypeStruct((rows, width), BF),
            jax.ShapeDtypeStruct((8, width), F32),
            jax.ShapeDtypeStruct((rows, width), BF),
            wide,
            wide,
            wide,
            wide,
        ],
        compiler_params=pltpu.CompilerParams(vmem_limit_bytes=56 * 2**20),
        cost_estimate=pl.CostEstimate(
            flops=22 * 10**9, bytes_accessed=40 * 10**6, transcendentals=0
        ),
        name="feed_forward",
    )(meta, gains, tokens, attended, grad_out, *sources)


def weight_kernel(meta, second_in, attended, resid_low, grad_out, active, back, first, last, turned):
    width = second_in.shape[1]
    half = width // 2
    step = pl.program_id(0)

    @pl.when(step == 0)
    def _():
        turned[...] = second_in[...].T
        lanes = pl.ds(pl.multiple_of(meta[0] * half, LANES), half)
        hidden = first.shape[1] - half
        first[:, hidden:] = dot(attended[...], resid_low[:, lanes], TN).astype(first.dtype)

    cols = pl.ds(pl.multiple_of(step * CHUNK, CHUNK), CHUNK)
    first[:, cols] = dot(turned[...], back[...]).astype(first.dtype)
    last[...] = dot(active[...], grad_out[...], TN).astype(last.dtype)


def weight_sums(which, second_in, attended, resid_low, grad_out, active, back, kind):
    rows, width = second_in.shape
    hidden = active.shape[1]

    def whole(shape):
        return pl.BlockSpec(shape, lambda c, m: (0, 0), pipeline_mode=pl.Buffered(1))

    flat = whole((rows, width))
    chunk = pl.BlockSpec((rows, CHUNK), lambda c, m: (0, c))
    return pl.pallas_call(
        weight_kernel,
        grid_spec=pltpu.PrefetchScalarGridSpec(
            num_scalar_prefetch=1,
            grid=(hidden // CHUNK,),
            in_specs=[flat] * 4 + [chunk, chunk],
            out_specs=[
                whole((width, hidden + width // 2)),
                pl.BlockSpec((CHUNK, width), lambda c, m: (c, 0)),
            ],
            scratch_shapes=[pltpu.VMEM((width, rows), BF)],
        ),
        out_shape=[
            jax.ShapeDtypeStruct((width, hidden + width // 2), kind),
            jax.ShapeDtypeStruct((hidden, width), kind),
        ],
        compiler_params=pltpu.CompilerParams(vmem_limit_bytes=56 * 2**20),
        cost_estimate=pl.CostEstimate(flops=1, bytes_accessed=1, transcendentals=0),
        name="weight_sums",
    )(which, second_in, attended, resid_low, grad_out, active, back)


def squares_kernel(*refs):
    pairs, out = refs[:-1], refs[-1]
    total = jnp.zeros((8, LANES), F32)
    for at in range(0, len(pairs), 2):
        both = []
        for ref in pairs[at : at + 2]:
            rows, cols = ref.shape
            part = jnp.zeros((8, LANES), F32)
            value = ref[...]
            value = value * value
            value = jnp.sum(value.reshape(rows // 8, 8, cols), axis=0)
            for lane in range(0, cols, LANES):
                part = part + value[:, lane : lane + LANES]
            both.append(part)
        total = total + (both[0] + both[1])
    out[...] = total


def assemble_kernel(piece, meta, mine, other, last_mine, last_other, inner, proj, outer, out):
    squares_kernel(mine, other, last_mine, last_other, out)
    first = meta[0] == 0
    width = proj.shape[1]
    cut = inner.shape[1] // 2
    for which, (left, right) in enumerate(((mine, other), (other, mine))):

        @pl.when(first == (which == 0))
        def _():
            proj[:, : width // 2] = left[:, cut:]
            proj[:, width // 2 :] = right[:, cut:]
            for at in range(0, cut, piece):
                cols = slice(at, at + piece)
                inner[:, 2 * at : 2 * at + 2 * piece] = jnp.concatenate(
                    [left[:, cols], right[:, cols]], axis=1
                )

    for which, (left, right) in enumerate(((last_mine, last_other), (last_other, last_mine))):

        @pl.when(first == (which == 0))
        def _():
            rows = left.shape[0]
            outer[:rows] = left[...]
            outer[rows:] = right[...]


def assemble(core, piece, halves, last_halves):
    rows, wide = halves[0].shape
    last_rows, width = last_halves[0].shape
    vmem = pl.BlockSpec(memory_space=pltpu.VMEM)
    *found, squares = pl.pallas_call(
        partial(assemble_kernel, piece),
        in_specs=[pl.BlockSpec(memory_space=pltpu.SMEM)] + [vmem] * 4,
        out_specs=[vmem] * 4,
        out_shape=[
            jax.ShapeDtypeStruct((rows, 2 * wide - width), F32),
            jax.ShapeDtypeStruct((rows, width), F32),
            jax.ShapeDtypeStruct((2 * last_rows, width), F32),
            jax.ShapeDtypeStruct((8, LANES), F32),
        ],
        cost_estimate=pl.CostEstimate(flops=1, bytes_accessed=1, transcendentals=0),
        compiler_params=pltpu.CompilerParams(vmem_limit_bytes=40 * 2**20),
        name="assemble",
    )(core[None], *halves, *last_halves)
    return *found, jnp.sum(squares)


def squares_of(pairs):
    if any(v.shape[0] % 8 for pair in pairs for v in pair):
        found = [jnp.sum(a * a) + jnp.sum(b * b) for a, b in pairs]
        return sum(found[1:], found[0])
    vmem = pl.BlockSpec(memory_space=pltpu.VMEM)
    flat = [v for pair in pairs for v in pair]
    out = pl.pallas_call(
        squares_kernel,
        in_specs=[vmem] * len(flat),
        out_specs=vmem,
        out_shape=jax.ShapeDtypeStruct((8, LANES), F32),
        cost_estimate=pl.CostEstimate(flops=1, bytes_accessed=1, transcendentals=0),
        compiler_params=pltpu.CompilerParams(vmem_limit_bytes=40 * 2**20),
        name="squares",
    )(*flat)
    return jnp.sum(out)


RATES = (0.03, 0.1, 0.03, 0.02, 0.3)


def adamw_kernel(factor, *refs):
    count = len(RATES)
    grads, states, outs = refs[:count], refs[count : 5 * count], refs[5 * count :]

    def update(at):
        scaled = grads[at][...] * factor[0]
        new = adamw(*[r[...] for r in states[4 * at : 4 * at + 4]], scaled, RATES[at])
        for out, value in zip(outs[4 * at : 4 * at + 4], new):
            out[...] = value

    for at in range(4):
        update(at)

    @pl.when(pl.program_id(0) == 0)
    def _():
        for at in range(4, count):
            update(at)


def adamw_all(factor, grads, states):
    steps = 6

    def block(at, shape):
        if at >= 4:
            return pl.BlockSpec(shape, lambda i: (0,) * len(shape))
        if at == 3:
            return pl.BlockSpec((shape[0] // steps, shape[1]), lambda i: (i, 0))
        return pl.BlockSpec((shape[0], shape[1] // steps), lambda i: (0, i))

    specs = [block(at, g.shape) for at, g in enumerate(grads)]
    wide = [s for s in specs for _ in range(4)]
    out = pl.pallas_call(
        adamw_kernel,
        grid=(steps,),
        in_specs=[pl.BlockSpec(memory_space=pltpu.SMEM)] + specs + wide,
        out_specs=wide,
        out_shape=[jax.ShapeDtypeStruct(g.shape, F32) for g in grads for _ in range(4)],
        compiler_params=pltpu.CompilerParams(vmem_limit_bytes=62 * 2**20),
        name="adamw_all",
    )(factor, *grads, *[v for state in states for v in state])
    return out


def first_kernel(offs, wanted, blocks, meta, tokens, *refs):
    count = 2 * (1 if offs is None else len(offs))
    sources, refs = refs[:count], refs[count:]
    outs, (first_in, gains, weight, mixed, sems) = refs[: len(wanted)], refs[len(wanted) :]
    side = weight.shape[1] // 2
    copies = []

    def copy(source, target):
        copies.append(pltpu.make_async_copy(source, target, sems.at[len(copies)]))

    for which in range(2):
        here = sources[which * (count // 2) : (which + 1) * (count // 2)]
        start = pl.multiple_of(jnp.bitwise_xor(meta[1], which) * side, side)
        if offs is None:
            copy(here[0].at[:, :side], weight.at[:, pl.ds(start, side)])
            if which == 0:
                copy(here[0].at[:, side:], mixed)
            continue
        own_rows = here[0].shape[1]
        for source, owners in zip(here, offs):
            for at, off in enumerate(owners):
                owner = jnp.bitwise_xor(meta[0], off)
                rows = pl.ds(pl.multiple_of(owner * own_rows, own_rows), own_rows)
                copy(source.at[at, :, :side], weight.at[rows, pl.ds(start, side)])
                if which == 0:
                    copy(source.at[at, :, side:], mixed.at[rows])
    for one in copies:
        one.start()
    for one in copies:
        one.wait()
    gain = mixed[...].astype(F32).T[:8]
    gains[...] = gain
    for block in range(blocks):
        value = tokens[meta[2 + block]].astype(F32)
        low = (value * inverse_rms(value) * gain[:1]).astype(BF)
        first_in[block * KEYS : (block + 1) * KEYS] = low
        if block not in wanted:
            continue
        out = outs[wanted.index(block)]
        wide = 2 * side // 3
        for col in range(0, 2 * side, wide):
            cols = slice(col, col + wide)
            out[:, cols] = dot(low, weight[:, cols]).astype(BF)


def first_product(meta, tokens, pieces, offs, wanted, blocks, with_weight):
    width = tokens.shape[2]
    rows = blocks * KEYS
    vmem = pl.BlockSpec(memory_space=pltpu.VMEM)
    out_shape = [
        *[jax.ShapeDtypeStruct((KEYS, 3 * width), BF) for _ in wanted],
        jax.ShapeDtypeStruct((rows, width), BF),
        jax.ShapeDtypeStruct((8, width), F32),
    ]
    scratch = [
        pltpu.VMEM((width, LANES), BF),
        pltpu.SemaphoreType.DMA((3 if offs is None else 3 * sum(len(o) for o in offs),)),
    ]
    if with_weight:
        out_shape.append(jax.ShapeDtypeStruct((width, 3 * width), BF))
    else:
        scratch = [pltpu.VMEM((width, 3 * width), BF)] + scratch
    return pl.pallas_call(
        partial(first_kernel, offs, wanted, blocks),
        in_specs=[pl.BlockSpec(memory_space=pltpu.SMEM), vmem] + [ANY] * len(pieces),
        out_specs=[vmem] * len(out_shape),
        out_shape=out_shape,
        scratch_shapes=scratch,
        compiler_params=pltpu.CompilerParams(vmem_limit_bytes=40 * 2**20),
        cost_estimate=pl.CostEstimate(
            flops=1, bytes_accessed=1, transcendentals=0
        ),
        name="first_product",
    )(meta, tokens, *pieces)


def first_grads_kernel(meta, first_in, *refs):
    cols, (out,) = refs[:-1], refs[-1:]
    side = out.shape[1]
    take = pl.ds(pl.multiple_of(meta[0] * side, side), side)
    total = None
    for block, grads in enumerate(cols):
        rows = first_in[block * KEYS : (block + 1) * KEYS].T
        term = dot(rows, grads[take], NT)
        total = term if block == 0 else total + term
        if block + 1 < len(cols):
            continue
        out[...] = total.astype(out.dtype)


def first_grads(which, first_in, cols, kind):
    width = first_in.shape[1]
    side = cols[0].shape[0] // 2
    vmem = pl.BlockSpec(memory_space=pltpu.VMEM)
    return pl.pallas_call(
        first_grads_kernel,
        in_specs=[pl.BlockSpec(memory_space=pltpu.SMEM)] + [vmem] * (1 + len(cols)),
        out_specs=vmem,
        out_shape=jax.ShapeDtypeStruct((width, side), kind),
        compiler_params=pltpu.CompilerParams(vmem_limit_bytes=50 * 2**20),
        cost_estimate=pl.CostEstimate(
            flops=1, bytes_accessed=1, transcendentals=0
        ),
        name="first_grads",
    )(which, first_in, *cols)


def token_grads_kernel(meta, gains, near, far, weight, tokens, grad_resid, *refs):
    out, gain_out = refs[-2:]
    step = pl.program_id(0)

    @pl.when(step == 0)
    def _():
        gain_out[...] = jnp.zeros_like(gain_out)

    for which, grads in enumerate((near, far)):

        @pl.when(step == which)
        def _():
            back = dot(weight[...], grads[...]).T
            value = tokens[...].astype(F32)
            scale = inverse_rms(value)
            normed = value * scale
            gain_out[...] += jnp.sum((back * normed).reshape(KEYS // 8, 8, -1), axis=0)
            out[...] = grad_resid[...] + rms_backward(scale, normed, back * gains[:1])


def token_grads(slot, seqs, gains, near, far, weight, tokens, grad_resid, before):
    _, rows, width = tokens.shape

    def whole(shape):
        return pl.BlockSpec(shape, lambda i, m: (0,) * len(shape), pipeline_mode=pl.Buffered(1))

    place = pl.BlockSpec((None, rows, width), lambda i, m: (m[i], 0, 0))
    extra = [] if before is None else [before]
    return pl.pallas_call(
        token_grads_kernel,
        grid_spec=pltpu.PrefetchScalarGridSpec(
            num_scalar_prefetch=1,
            grid=(2,),
            in_specs=[
                whole(gains.shape),
                whole(near.shape),
                whole(far.shape),
                whole(weight.shape),
                place,
                pl.BlockSpec((None, rows, width), lambda i, m: (2 * slot + i, 0, 0)),
            ]
            + [ANY] * len(extra),
            out_specs=[place, whole((8, width))],
        ),
        out_shape=[
            jax.ShapeDtypeStruct(tokens.shape, F32),
            jax.ShapeDtypeStruct((8, width), F32),
        ],
        input_output_aliases={7: 0} if extra else {},
        compiler_params=pltpu.CompilerParams(vmem_limit_bytes=50 * 2**20),
        cost_estimate=pl.CostEstimate(
            flops=1, bytes_accessed=1, transcendentals=0
        ),
        name="token_grads",
    )(seqs, gains, near, far, weight, tokens, grad_resid, *extra)


def prepare_kernel(owners, meta, inner, outer, proj, out):
    rows, hidden = inner.shape
    width = proj.shape[1]
    half = width // 2
    piece = hidden // owners // 2
    for core in range(2):

        @pl.when(meta[1] == core)
        def _():
            for owner in range(owners):
                at = (2 * owner + core) * piece
                out[:, owner * piece : (owner + 1) * piece] = inner[:, at : at + piece].astype(BF)
            cut = hidden // 2
            out[:, cut : cut + half] = proj[:, core * half : (core + 1) * half].astype(BF)
            for fold in range(piece // rows):
                at = core * piece + fold * rows
                start = cut + half + fold * width
                out[:, start : start + width] = outer[at : at + rows].astype(BF)


def prepare(meta, owners, inner, outer, proj):
    rows, hidden = inner.shape
    width = proj.shape[1]
    vmem = pl.BlockSpec(memory_space=pltpu.VMEM)
    return pl.pallas_call(
        partial(prepare_kernel, owners),
        in_specs=[pl.BlockSpec(memory_space=pltpu.SMEM)] + [vmem] * 3,
        out_specs=vmem,
        out_shape=jax.ShapeDtypeStruct((rows, hidden + width // 2), BF),
        cost_estimate=pl.CostEstimate(flops=1, bytes_accessed=1, transcendentals=0),
        compiler_params=pltpu.CompilerParams(vmem_limit_bytes=40 * 2**20),
        name="prepare",
    )(meta, inner, outer, proj)


def on_device(
    tokens,
    cotangent,
    lengths,
    qkv_weight,
    qkv_first,
    qkv_second,
    qkv_average,
    proj_weight,
    proj_first,
    proj_second,
    proj_average,
    inner_weight,
    inner_first,
    inner_second,
    inner_average,
    outer_weight,
    outer_first,
    outer_second,
    outer_average,
    gains,
    gain_first,
    gain_second,
    gain_average,
    mixes,
    mix_first,
    mix_second,
    mix_average,
):
    group_seqs, shard_len, width = tokens.shape
    owners = lax.axis_size("dp")
    heads = mixes.shape[1]
    own_rows = qkv_weight.shape[0]
    hidden = inner_weight.shape[1]
    half = width // 2
    slice_ff = hidden // owners // 2
    me = lax.axis_index("seq")
    pair = me // 2
    core = jnp.bitwise_and(me, 1)

    def by_core(mine, other, axis):
        return jnp.where(
            core == 0,
            jnp.concatenate([mine, other], axis),
            jnp.concatenate([other, mine], axis),
        )

    ahead = (lengths[None, :] > lengths[:, None]) | (
        (lengths[None, :] == lengths[:, None])
        & (jnp.arange(group_seqs)[None, :] < jnp.arange(group_seqs)[:, None])
    )
    rank = jnp.sum(ahead.astype(jnp.int32), axis=1)
    def by_rank(place, values):
        return jnp.sum(jnp.where(rank == place, values, 0)).astype(jnp.int32)

    def of_slot(slot, which, values):
        first, second = (0, 1) if slot == 0 else (group_seqs - 1, group_seqs - 2)
        return jnp.where(which == 0, by_rank(first, values), by_rank(second, values))

    def sequence_of(slot, which):
        return of_slot(slot, which, jnp.arange(group_seqs, dtype=jnp.int32))

    def pack(values):
        spot = jnp.arange(len(values), dtype=jnp.int32)
        total = jnp.zeros((len(values),), jnp.int32)
        for at, value in enumerate(values):
            total = jnp.where(spot == at, value, total)
        return total

    def arrange(value):
        return jnp.stack(
            [
                jnp.stack(
                    [
                        lax.dynamic_index_in_dim(
                            value, sequence_of(slot, jnp.bitwise_xor(pair, d)), 0, False
                        )
                        for d in range(2)
                    ]
                )
                for slot in range(2)
            ]
        )

    lengths_here = [[of_slot(s, jnp.bitwise_xor(pair, d), lengths) for d in range(2)] for s in range(2)]
    seqs = [pack([sequence_of(s, pair), sequence_of(s, 1 - pair)]) for s in range(2)]
    feed_meta = pack(
        [lax.axis_index("dp"), core]
        + [sequence_of(s, jnp.bitwise_xor(pair, d)) for s in range(2) for d in range(2)]
    )
    metas = [pack([lengths_here[slot][0], me, core]) for slot in range(2)]

    mixers = spread(mixes)
    positions = me * shard_len + jnp.arange(shard_len, dtype=jnp.int32)
    used = jnp.stack([jnp.stack(found) for found in lengths_here])
    live = positions[None, None, :] < used[:, :, None]
    cot = arrange(cotangent)
    grad_out = jnp.where(live[..., None], cot, jnp.zeros_like(cot))
    folds = slice_ff // own_rows
    if own_rows % 16 == 0:
        rest = prepare(feed_meta, owners, inner_weight, outer_weight, proj_weight)[None]
    else:
        inner_mine = inner_weight.astype(BF).reshape(own_rows, owners, 2, slice_ff)
        inner_mine = lax.dynamic_index_in_dim(inner_mine, core, 2, False)
        outer_mine = outer_weight.astype(BF).reshape(2, folds, own_rows, width)
        outer_mine = lax.dynamic_index_in_dim(outer_mine, core, 0, False)
        rest = jnp.concatenate(
            [
                inner_mine.reshape(own_rows, owners * slice_ff),
                lax.dynamic_slice_in_dim(proj_weight.astype(BF), core * half, half, 1),
            ]
            + [outer_mine[f] for f in range(folds)],
            axis=1,
        )[None]
    side = qkv_weight.shape[1] // 2
    mine = lax.dynamic_slice_in_dim(qkv_weight.astype(BF), core * side, side, 1)
    mine = jnp.concatenate([mine, jnp.pad(gains.astype(BF).T, ((0, 0), (0, LANES - 2)))], 1)
    offs = None
    if owners == 8:
        shard = mine[None]
        got = swap(shard, "dp", 4)
        got = after(got, feed_meta, rest)
        pieces = [jnp.concatenate([shard, got])]
        far_z, far_x = swap(pieces[0], "dp", 2), swap(pieces[0], "dp", 1)
        beside = [swap(pieces[0], "seq", 1)]
        pieces += [far_z, far_x]
        pieces.append(swap(far_z, "dp", 1))
        beside += [swap(p, "seq", 1) for p in pieces[1:]]
        offs = ((0, 4), (2, 6), (1, 5), (3, 7))
        pieces += beside
        late = far_z
    else:
        mine = lax.all_gather(mine, "dp", axis=0, tiled=True)
        pieces = [mine, swap(mine, "seq", 1)]

    if offs is not None:
        got = swap(after(rest, late), "dp", 4)
    place = feed_meta
    near, far, *_ = first_product(
        place, tokens, pieces, offs, (0, 1), 2, False
    )
    near, far = [near], [far]
    here = swap(far[0], "seq", 2)
    beside = swap(near[0], "seq", 1)
    place, beside, mixers, metas, grad_out = lax.optimization_barrier(
        (place, beside, mixers, metas, grad_out)
    )
    if offs is not None:
        place, got = lax.optimization_barrier((place, got))
    pre_mix, post_mix, pre_back, post_back = mixers
    *out, first_in, gain_vals, weight_qkv = first_product(
        place, tokens, pieces, offs, (2, 3), 4, True
    )
    near.append(out[0])
    far.append(out[1])
    here = after(here, far[1], near[1])
    if offs is not None:
        rest_pieces = [jnp.concatenate([rest, got])]
        far_z, far_x = swap(rest_pieces[0], "dp", 2), swap(rest_pieces[0], "dp", 1)
    sources = [[near[0], beside, here, swap(here, "seq", 1)]]
    next_far = swap(after(far[1], here), "seq", 2)
    beside = swap(after(near[1], here), "seq", 1)
    def by_half(rows):
        return jnp.where(core == 0, rows, rows[:, ::-1])

    rows, probs, weights = [None, None], [None, None], [None, None]
    meta = after(metas[0], sources[0])
    if offs is not None:
        meta = after(meta, rest_pieces)
        beside_rest = [swap(rest_pieces[0], "seq", 1)]
    rows[0], probs[0], weights[0] = attend(meta, sources[0], pre_mix, post_mix, heads, FLOPS[0])
    next_far, beside = lax.optimization_barrier((next_far, beside, rows[0]))[:2]
    if offs is not None:
        far_z, far_x, next_far, beside, beside_rest = lax.optimization_barrier(
            (far_z, far_x, next_far, beside, beside_rest)
        )
        rest_pieces += [far_z, far_x]
        beside_rest = list(beside_rest) + [swap(p, "seq", 1) for p in (far_z, far_x)]
        last = swap(far_z, "dp", 1)
    sources.append([near[1], beside, next_far, swap(next_far, "seq", 1)])
    far_rows = swap(rows[0][2:], "seq", 2)
    rows[1], probs[1], weights[1] = attend(
        metas[1], sources[1], pre_mix, post_mix, heads, FLOPS[1]
    )
    far_rows = after(far_rows, rows[1])
    cut = owners * slice_ff + half
    if offs is not None:
        last, *beside_rest = after([last] + beside_rest, rows[1])
        rest_pieces.append(last)
        feed_weights = rest_pieces + beside_rest + [swap(last, "seq", 1)]
    else:
        rest = lax.all_gather(rest[0], "dp")
        feed_weights = []
        for part in (rest, swap(rest, "seq", 1)):
            flat = part.reshape(owners * own_rows, -1)
            down = jnp.moveaxis(part[:, :, cut:].reshape(owners, own_rows, folds, width), 2, 1)
            feed_weights += [
                flat[:, : cut - half],
                flat[:, cut - half : cut],
                down.reshape(owners * slice_ff, width),
            ]
    far_rows = jnp.stack([far_rows, swap(rows[1][2:], "seq", 2)])
    near_rows = jnp.stack([rows[0][1], rows[1][1]])
    got = swap(jnp.stack([near_rows, far_rows[:, 1]]), "seq", 1)
    attention_output = jnp.stack(
        [
            by_half(
                jnp.stack(
                    [
                        jnp.stack([rows[slot][0], got[0, slot]]),
                        jnp.stack([far_rows[slot, 0], got[1, slot]]),
                    ]
                )
            ).reshape(2, 2 * ROWS, width)
            for slot in range(2)
        ]
    )

    flat = (-1, width)
    attention_output = attention_output.reshape(flat)
    flat_out = grad_out.reshape(flat)
    output, grad_resid, resid_low, grad_attended, gain_two, second_in, *wide = feed_forward(
        feed_meta,
        gain_vals[:2],
        tokens.reshape(flat),
        attention_output,
        flat_out,
        feed_weights,
        offs,
        hidden,
    )
    grad_attended = grad_attended.reshape(grad_out.shape)
    grad_resid = grad_resid.reshape(4, shard_len, width)

    def sums_of(side, which, kind):
        return weight_sums(
            which[None],
            second_in,
            attention_output,
            resid_low,
            flat_out,
            wide[side],
            wide[2 + side],
            kind,
        )

    output = output.reshape(tokens.shape)
    gain_two = jnp.sum(gain_two, axis=0)

    sent = sums_of(1, 1 - core, BF)
    arrived = swap(sent[0], "seq", 1), swap(sent[1], "seq", 1)
    meta = after(core, sent)
    mine = sums_of(0, meta, F32)
    arrived = after(arrived, mine, output)
    twos = [(2**k, 2) for k in range(owners.bit_length() - 1)]
    orders = [twos, twos[1:2] + twos[:1] + twos[2:]]
    chains = []
    for at in range(2):
        total = (mine[at] + arrived[at].astype(F32)).astype(BF)
        total = total.reshape((2,) * len(twos) + (-1, total.shape[1]))
        chains.append(split_blocks(total, "dp", twos[::-1], orders[at][0]))

    def send_step(at, turn, parts):
        stride, radix = orders[at][turn]
        return tuple(swap(parts[0][k], "dp", k * stride) for k in range(1, radix))

    def join_step(at, turn, parts, got):
        total = parts[0][0].astype(F32)
        for part in got:
            total = total + part.astype(F32)
        if turn + 1 == len(twos):
            return total
        return split_blocks(total.astype(BF), "dp", parts[1], orders[at][turn + 1])

    def step_on(at, turn, parts, *first):
        got = send_step(at, turn, parts)
        return join_step(at, turn, parts, after(got, *first) if first else got)

    def to_far(slot):
        found = by_half(grad_attended[slot].reshape(2, 2, ROWS, width)).reshape(4, ROWS, width)
        return found, swap(found[2:], "seq", 2)

    def from_near(found, far):
        got = swap(jnp.stack([found[1], far[1]]), "seq", 1)
        return jnp.stack([found[0], got[0], far[0], got[1]])

    def attend_slot(slot, meta, rows):
        return attend_back(
            meta, sources[slot], rows, pre_back, post_back, probs[slot], weights[slot], FLOPS[slot]
        )

    found, far = to_far(0)
    far = after(far, mine)
    next_found, next_far = to_far(1)
    meta = after(metas[0], chains)
    stay, away, back_pre, back_post = attend_slot(0, meta, from_near(found, far))
    grad_mixes = jnp.stack([back_pre[:, :heads], back_post[:, :heads]])
    chains = [step_on(at, 0, chains[at], stay) for at in range(2)]
    away, next_far = lax.optimization_barrier((away, next_far, chains))[:2]
    next_rows = from_near(next_found, next_far)
    summed = (stay + swap(away, "seq", 1).astype(F32)).astype(BF)
    far = swap(summed[1], "seq", 2)
    meta = after(metas[1], summed, chains)
    stay, away, back_pre, back_post = attend_slot(1, meta, next_rows)
    grad_mixes = grad_mixes + jnp.stack([back_pre[:, :heads], back_post[:, :heads]])
    got = [send_step(at, 1, chains[at]) for at in range(2)]
    away, far, got = lax.optimization_barrier((away, far, got, stay))[:3]
    grad_cols = [(summed[0], far)]
    summed = (stay + swap(away, "seq", 1).astype(F32)).astype(BF)
    got = after(got, summed)
    chains = [join_step(at, 1, chains[at], got[at]) for at in range(2)]
    far = swap(summed[1], "seq", 2)

    def to_tokens(slot, before, first):
        return token_grads(
            slot,
            after(seqs[slot], first),
            gain_vals,
            *grad_cols[slot],
            weight_qkv,
            tokens,
            grad_resid,
            before,
        )

    begun = to_tokens(0, None, summed)
    for turn in range(2, len(twos)):
        chains = [step_on(at, turn, chains[at], begun) for at in range(2)]
    first_part, second_part = chains
    others = first_part.astype(BF), second_part.astype(BF)
    far, begun, others = lax.optimization_barrier((far, begun, others))
    grad_cols.append((summed[0], far))
    cols = grad_cols[0] + grad_cols[1]
    sent = first_grads((1 - core)[None], first_in, cols, BF)
    qkv_mine = first_grads(after(core, sent)[None], first_in, cols, F32)

    def over_pairs(total, *first):
        total = lax.optimization_barrier(jax.tree.map(lambda v: v.astype(BF), total))
        got = jax.tree.map(lambda v: swap(v, "seq", 2), total)
        if first:
            got = after(got, *first)
        return jax.tree.map(lambda v, w: v.astype(F32) + w.astype(F32), total, got)

    arrived = after(swap(sent, "seq", 1), qkv_mine)
    qkv_total = (qkv_mine + arrived.astype(F32)).astype(BF)
    qkv_total = qkv_total.reshape((2,) * len(twos) + (own_rows, side))
    third = side // LANES // 3 * LANES
    chains = [qkv_total[..., third:], qkv_total[..., :third]]
    chains = [split_blocks(chains[at], "dp", twos[::-1], orders[at][0]) for at in range(2)]
    others = over_pairs(after(others, [p for p, _ in chains]))
    got = [send_step(at, 0, chains[at]) for at in range(2)]
    grad_rows_tokens, gain_more = to_tokens(1, begun[0], got[1])
    got[0] = after(got[0], grad_rows_tokens)
    chains = [join_step(at, 0, chains[at], got[at]) for at in range(2)]
    got = [send_step(at, 1, chains[at]) for at in range(2)]
    gain_one = jnp.sum(begun[1] + gain_more, axis=0)
    small = jnp.concatenate([gain_one, gain_two, grad_mixes.reshape(-1)])
    count = small.shape[0]
    small = jnp.pad(small, (0, -(count + 1) % (8 * LANES) + 1)).reshape(-1, LANES)
    chains = [join_step(at, 1, chains[at], got[at]) for at in range(2)]

    first_halves = (others[0], swap(others[0], "seq", 1))
    last_halves = (others[1], swap(others[1], "seq", 1))
    if own_rows % 8 == 0:
        red_inner, red_proj, red_outer, squares = assemble(
            core, slice_ff, first_halves, last_halves
        )
    else:
        red_proj = by_core(*[g[:, cut - half :] for g in first_halves], 1)
        red_inner = by_core(
            *[g[:, : cut - half].reshape(own_rows, owners, 1, slice_ff) for g in first_halves], 2
        ).reshape(own_rows, hidden)
        red_outer = by_core(*last_halves, 0)
        squares = squares_of([first_halves, last_halves])
    small = small + swap(small, "seq", 1)
    small = small + swap(small, "seq", 2)
    pins = (red_inner, red_proj, red_outer, squares)
    for turn in range(2, len(twos)):
        chains = [step_on(at, turn, chains[at], *pins) for at in range(2)]
        pins = ()
    qkv_total = over_pairs(jnp.concatenate(chains[::-1], axis=-1), small)
    qkv_other = swap(qkv_total, "seq", 1)
    red_qkv = by_core(qkv_total, qkv_other, 1)

    squares = squares + squares_of([(qkv_total, qkv_other)])
    place = lax.broadcasted_iota(jnp.int32, small.shape, 0) * LANES
    place = place + lax.broadcasted_iota(jnp.int32, small.shape, 1)
    small = sum_everywhere(jnp.where(place == count, squares, small), "dp").reshape(-1)
    gain_all = small[: 2 * width].reshape(2, width)
    red_gains = lax.dynamic_slice_in_dim(gain_all, lax.axis_index("dp") * own_rows, own_rows, 1)
    red_mixes = small[2 * width : count].reshape(mixes.shape)
    grad_norm = jnp.sqrt(
        small[count] + jnp.sum(gain_all * gain_all) + jnp.sum(red_mixes * red_mixes)
    )
    factor = CLIP / jnp.maximum(grad_norm, CLIP)
    clipped_gains = red_gains * factor
    new = adamw_all(
        factor[None],
        (red_qkv, red_proj, red_inner, red_outer, red_gains),
        (
            (qkv_weight, qkv_first, qkv_second, qkv_average),
            (proj_weight, proj_first, proj_second, proj_average),
            (inner_weight, inner_first, inner_second, inner_average),
            (outer_weight, outer_first, outer_second, outer_average),
            (gains, gain_first, gain_second, gain_average),
        ),
    )
    mix_new = adamw(mixes, mix_first, mix_second, mix_average, red_mixes * factor, 0.3)
    return (
        output,
        grad_rows_tokens,
        grad_norm,
        *new,
        *mix_new,
        clipped_gains,
    )


def solution(mesh):
    rows = P("dp", "seq", None)
    matrix = P("dp", None)
    vector = P(None, "dp")
    in_specs = (rows, rows, P("dp")) + (matrix,) * 16 + (vector,) * 4 + (P(),) * 4
    out_specs = (rows, rows, P()) + (matrix,) * 16 + (vector,) * 4 + (P(),) * 4 + (vector,)
    return jax.shard_map(
        on_device, mesh=mesh, in_specs=in_specs, out_specs=out_specs, check_vma=False
    )
```
